1024 devices in a mesh: pts: 64 (over x, y), cam: 16 (over z, core).
Axes of the slice: x: 8, y: 8, z: 8, core: 2. Of those that a mesh axis runs over, the one named last changes fastest.
Arguments:
- right_side: float32 [9, 8192], P(None, 'cam'), may hold values from -6 to 6
- camera_damping: float32 [9, 8192], P(None, 'cam'), may hold values from 0.5 to 4
- preconditioner: float32 [9, 8192], P(None, 'cam'), may hold values from 0.2 to 1
- jac_cam: float32 [1024, 18, 4096], P(('pts', 'cam')), may hold values from -0.25 to 0.25
- jac_pt: float32 [1024, 6, 4096], P(('pts', 'cam')), may hold values from -3 to 3
- camera_index: int32 [1024, 4096], P(('pts', 'cam')), may hold values from 0 to 8191, as said below
- point_index: int32 [1024, 4096], P(('pts', 'cam')), may hold values from 0 to 1023, never falling along the last dimension, each value on 1 to 16 neighbouring positions
- point_damping: float32 [1024, 3, 1024], P(('pts', 'cam')), may hold values from 0.5 to 2
- anchors: int32 [16], replicated, may hold values from 0 to 8191
Outputs:
- solution: float32 [9, 8192], P(None, 'cam')
- residual: float32 [9, 8192], P(None, 'cam')
The draws below stay inside these ranges and needn't reach their ends.
Inputs may be any that keep to these rules, and one draw needn't show every extreme that they name: `point_index`: within each device's row the point numbers never fall, and every point 0 to 1023 has 1 to 16 observations. `camera_index`: row g holds the observations of device g = p * 16 + c (p its index along pts, c along cam). Its cameras lie in the covisible tiles of 64 cameras owned by cam indices c - 1, c, c + 1 (those that exist) and the index half the axis away; tiles are used unevenly.
All inputs are finite; a program needn't handle non-finite values.
Results may differ from the reference program's by a relative error of at most 0.0001.
Values sent between devices are 32-bit elements; how exact they have to be, the bound alone decides.
No kernel may reach another device: no remote copies, remote signals or barrier semaphores. Data moves between devices by JAX's collectives and lax.ppermute only.
A program may use at most 32 MiB of HBM per device.

```python
import math
import jax
import jax.numpy as jnp
import numpy as np

CAMP = 9
TILE = 64
CAM_DEV = 512
OBS_DEV = 4096
P_DEV = 1024
ITERS = 2
ANCHORS = 16
NCAM = 8192
GROUPS = 1024
N_PTS = 64
N_CAM = 16


def draw_camera_index(key, part):
    key = jax.random.fold_in(key, 5)
    key_owner, key_first, key_second, key_within = jax.random.split(key, 4)
    shape = (GROUPS, OBS_DEV)
    column = (jnp.arange(GROUPS, dtype=jnp.int32) % N_CAM)[:, None]
    pick = jax.random.randint(key_owner, shape, 0, 4, dtype=jnp.int32)
    nearby = jnp.clip(column + pick - 1, 0, N_CAM - 1)
    opposite = (column + N_CAM // 2) % N_CAM
    owner = jnp.where(pick == 3, opposite, nearby)
    per_owner = CAM_DEV // TILE
    first = jax.random.randint(key_first, shape, 0, per_owner, dtype=jnp.int32)
    second = jax.random.randint(key_second, shape, 0, per_owner, dtype=jnp.int32)
    tile = jnp.maximum(first, second)
    within = jax.random.randint(key_within, shape, 0, TILE, dtype=jnp.int32)
    return (owner * CAM_DEV + tile * TILE + within).astype(jnp.int32)


def place_ends(values, own_key, low, top_value):
    spot = [jax.random.randint(jax.random.fold_in(own_key, axis), (), 0, length) for axis, length in enumerate(values.shape)]
    longest = values.shape.index(max(values.shape))
    next_to = spot[:longest] + [(spot[longest] + 1) % values.shape[longest]] + spot[longest + 1:]
    return values.at[tuple(spot)].set(low).at[tuple(next_to)].set(top_value)


def block_scale(key, shape, cuts, low, largest):
    factor_of, own = 1.0, jax.random.fold_in(key, 6)
    for axis_at, shards_of in cuts:
        steps = jnp.exp(jax.random.uniform(jax.random.fold_in(own, axis_at), (shards_of,), jnp.float32, low / len(cuts), largest / len(cuts)))
        factor_of = factor_of * jnp.repeat(steps, shape[axis_at] // shards_of).reshape([-1 if axis == axis_at else 1 for axis in range(len(shape))])
    return factor_of


def split_up(amount, total, bound, skew):
    weights = [(1 << 20) // math.isqrt(grade ** skew) + 1 for grade in range(2, amount + 1)]
    rest, holding = total - bound - (amount - 1), [1] * (amount - 1)
    while rest > 0:
        candidates = [i for i in range(amount - 1) if holding[i] < bound]
        mass, budget = sum([weights[i] for i in candidates]), rest
        for i in candidates:
            extra = min(bound - holding[i], max(1, budget * weights[i] // mass), rest)
            holding[i] = holding[i] + extra
            rest = rest - extra
    return np.array([bound] + holding)


def uneven(stream_key, amount, total, most, slope):
    if amount == 2:
        one = jax.random.randint(stream_key, (), max(1, total - most), min(most, total - 1) + 1)
        return jnp.stack([one, total - one])
    sizes = jnp.asarray(split_up(amount, total, most, slope), jnp.int32)
    couples = (amount - 1) // 2
    giver, taker = sizes[1:1 + 2 * couples:2], sizes[2:2 + 2 * couples:2]
    slack = jnp.minimum(giver - 1, most - taker)
    shifted = jax.random.randint(jax.random.fold_in(stream_key, 1), (couples,), 0, 1 << 20) % (slack + 1)
    sizes = sizes.at[1:1 + 2 * couples:2].set(giver - shifted).at[2:2 + 2 * couples:2].set(taker + shifted)
    return sizes[jax.random.permutation(jax.random.fold_in(stream_key, 2), amount)]


def gaussian(key, shape, width, bound, cuts=(), kind=jnp.bfloat16):
    array = width * jax.random.normal(key, shape, jnp.float32)
    if cuts:
        array = array * block_scale(key, shape, cuts, -0.22, 0.18)
    return jnp.clip(array, -bound, bound).astype(kind)


def setup_inputs(seed: int = 0) -> dict:
    streams_of = jax.random.split(jax.random.key(seed), 10)
    right_side = gaussian(streams_of[0], (CAMP, NCAM), 1.0, 6.0, ((1, 16),), jnp.float32)
    camera_damping = jnp.clip(jnp.exp(math.log(4.0) - 2.0794415 * jax.random.uniform(streams_of[1], (CAMP, NCAM), jnp.float32) ** block_scale(streams_of[1], (CAMP, NCAM), ((1, 16),), -0.2, 0.2)), 0.5, 4.0)
    preconditioner = jnp.clip(jnp.exp(math.log(1.0) - 1.609438 * jax.random.uniform(streams_of[2], (CAMP, NCAM), jnp.float32) ** block_scale(streams_of[2], (CAMP, NCAM), ((1, 16),), -0.2, 0.2)), 0.2, 1.0)
    jac_cam = gaussian(streams_of[3], (GROUPS, 2 * CAMP, OBS_DEV), (OBS_DEV * N_PTS // CAM_DEV) ** -0.5, 0.25, ((0, 1024),), jnp.float32)
    jac_pt = gaussian(streams_of[4], (GROUPS, 6, OBS_DEV), 0.5, 3.0, ((0, 1024),), jnp.float32)
    camera_index = draw_camera_index(jax.random.fold_in(streams_of[9], 71), 0)
    point_index = jax.vmap(lambda own: jnp.searchsorted(jnp.cumsum(uneven(own, P_DEV, OBS_DEV, 16, 0)), jnp.arange(OBS_DEV), side="right"))(jax.random.split(streams_of[6], GROUPS)).reshape((GROUPS, OBS_DEV)).astype(jnp.int32)
    point_damping = jnp.clip(jnp.exp(math.log(2.0) - 1.3862944 * jax.random.uniform(streams_of[7], (GROUPS, 3, P_DEV), jnp.float32) ** block_scale(streams_of[7], (GROUPS, 3, P_DEV), ((0, 1024),), -0.2, 0.2)), 0.5, 2.0)
    anchors = place_ends(jax.random.randint(streams_of[8], (ANCHORS,), 0, NCAM), jax.random.fold_in(streams_of[8], 1), 0, NCAM - 1).astype(jnp.int32)
    return {"right_side": right_side, "camera_damping": camera_damping, "preconditioner": preconditioner, "jac_cam": jac_cam, "jac_pt": jac_pt, "camera_index": camera_index, "point_index": point_index, "point_damping": point_damping, "anchors": anchors}


def point_inverse(jac_pt, point_id, damping, segments):
    rows = jac_pt.reshape(2, 3, -1)
    pairs = [(0, 0), (0, 1), (0, 2), (1, 1), (1, 2), (2, 2)]
    prods = jnp.stack([jnp.sum(rows[:, first] * rows[:, second], axis=0) for first, second in pairs])
    summed = jax.ops.segment_sum(prods.T, point_id, segments).T
    sym_xx = summed[0] + damping[0]
    sym_xy = summed[1]
    sym_xz = summed[2]
    sym_yy = summed[3] + damping[1]
    sym_yz = summed[4]
    sym_zz = summed[5] + damping[2]
    cof_xx = sym_yy * sym_zz - sym_yz * sym_yz
    cof_xy = sym_xz * sym_yz - sym_xy * sym_zz
    cof_xz = sym_xy * sym_yz - sym_xz * sym_yy
    cof_yy = sym_xx * sym_zz - sym_xz * sym_xz
    cof_yz = sym_xy * sym_xz - sym_xx * sym_yz
    cof_zz = sym_xx * sym_yy - sym_xy * sym_xy
    determinant = sym_xx * cof_xx + sym_xy * cof_xy + sym_xz * cof_xz
    return jnp.stack([cof_xx, cof_xy, cof_xz, cof_xy, cof_yy, cof_yz, cof_xz, cof_yz, cof_zz]) / determinant


def schur_terms(whole, jac_cam, jac_pt, cam_id, point_id, inverse, segments, camera_count):
    cam_rows = jac_cam.reshape(2, 9, -1)
    pt_rows = jac_pt.reshape(2, 3, -1)
    picked = whole[:, cam_id]
    predicted = jnp.sum(cam_rows * picked[None], axis=1)
    pulled = jnp.sum(pt_rows * predicted[:, None], axis=0)
    gathered = jax.ops.segment_sum(pulled.T, point_id, segments).T
    solved = jnp.sum(inverse.reshape(3, 3, -1) * gathered[None], axis=1)
    spread = solved[:, point_id]
    leftover = predicted - jnp.sum(pt_rows * spread[None], axis=1)
    pushed = jnp.sum(cam_rows * leftover[:, None], axis=0)
    return jax.ops.segment_sum(pushed.T, cam_id, camera_count).T


def reference(right_side, camera_damping, preconditioner, jac_cam, jac_pt, camera_index, point_index, point_damping, anchors):
    groups = jac_cam.shape[0]
    flat_cam = jnp.transpose(jac_cam, (1, 0, 2)).reshape(18, -1)
    flat_pt = jnp.transpose(jac_pt, (1, 0, 2)).reshape(6, -1)
    cam_id = camera_index.reshape(-1)
    offsets = (jnp.arange(groups, dtype=jnp.int32) * P_DEV)[:, None]
    point_id = (point_index + offsets).reshape(-1)
    segments = groups * P_DEV
    damping = jnp.transpose(point_damping, (1, 0, 2)).reshape(3, -1)
    inverse = point_inverse(flat_pt, point_id, damping, segments)
    keep = jnp.ones((NCAM,), jnp.float32).at[anchors].set(0.0)

    def apply_schur(direction):
        masked = direction * keep
        terms = schur_terms(masked, flat_cam, flat_pt, cam_id, point_id, inverse, segments, NCAM)
        return keep * (camera_damping * masked + terms)

    solution = jnp.zeros_like(right_side)
    residual = right_side * keep
    precond = preconditioner * residual
    direction = precond
    gamma = jnp.sum(residual * precond)
    for iteration in range(ITERS):
        image = apply_schur(direction)
        alpha = gamma / jnp.sum(direction * image)
        solution = solution + alpha * direction
        residual = residual - alpha * image
        precond = preconditioner * residual
        fresh = jnp.sum(residual * precond)
        direction = precond + (fresh / gamma) * direction
        gamma = fresh
    return solution, residual
```

```python
import functools

import jax
import jax.numpy as jnp
from jax import lax
from jax.experimental import pallas as pl
from jax.experimental.pallas import tpu as pltpu
from jax.sharding import PartitionSpec as P

LANES = 128
BLOCKS = 4
F32, BF16 = jnp.float32, jnp.bfloat16
VMEM = pl.BlockSpec(memory_space=pltpu.VMEM)
SMEM = pl.BlockSpec(memory_space=pltpu.SMEM)
PARAMS = pltpu.CompilerParams(vmem_limit_bytes=40 * 1024 * 1024)


def split(value):
    high = value.astype(BF16)
    low = (value - high.astype(F32)).astype(BF16)
    return high, low


def one_hot(row, count):
    ids = lax.broadcasted_iota(jnp.int32, (count, row.shape[1]), 0)
    return jnp.where(ids == row, 1.0, 0.0)


def same_before(point, step):
    return jnp.where(pltpu.roll(point, step, 1) == point, 1.0, 0.0)


def point_totals(value, point, steps):
    count = point.shape[1]
    before = value
    after = value
    for step in steps:
        mask = same_before(point, step)
        before = before + mask * pltpu.roll(before, step, 1)
        mask_after = pltpu.roll(mask, count - step, 1)
        after = after + mask_after * pltpu.roll(after, count - step, 1)
    return before + (after - value)


def setup_kernel(steps, width, owners, position, jac_pt, point_ref, damping, camera_ref, inverse, local):
    camera = camera_ref[...]
    shift = (camera // width - position[0] + owners) % owners
    block = jnp.where(shift == 1, 1, jnp.where(shift == owners - 1, 2, 3))
    block = jnp.where(shift == 0, 0, block)
    local[...] = block * width + camera % width

    point = point_ref[...]
    count = point.shape[1]
    tiles = damping.shape[1] // LANES
    rows = [jac_pt[r : r + 1, :] for r in range(6)]
    pairs = [(0, 0), (0, 1), (0, 2), (1, 1), (1, 2), (2, 2)]
    prods = [rows[a] * rows[b] + rows[3 + a] * rows[3 + b] for a, b in pairs]
    prods = jnp.concatenate(prods + [jnp.zeros((2, count), F32)], axis=0)
    summed = point_totals(prods, point, steps)

    hot = one_hot(point % LANES, LANES).astype(BF16)
    tile_mask = one_hot(point // LANES, tiles)
    table = jnp.concatenate(
        [damping[k : k + 1, t * LANES : (t + 1) * LANES] for k in range(3) for t in range(tiles)],
        axis=0,
    )
    high = table.astype(BF16)
    rest = table - high.astype(F32)
    mid = rest.astype(BF16)
    low = (rest - mid.astype(F32)).astype(BF16)
    picked = sum(
        jnp.dot(part, hot, preferred_element_type=F32) for part in (high, mid, low)
    )
    damp = [
        jnp.sum(picked[k * tiles : (k + 1) * tiles] * tile_mask, axis=0, keepdims=True)
        for k in range(3)
    ]
    xx = summed[0:1] + damp[0]
    xy = summed[1:2]
    xz = summed[2:3]
    yy = summed[3:4] + damp[1]
    yz = summed[4:5]
    zz = summed[5:6] + damp[2]
    cof_xx = yy * zz - yz * yz
    cof_xy = xz * yz - xy * zz
    cof_xz = xy * yz - xz * yy
    cof_yy = xx * zz - xz * xz
    cof_yz = xy * xz - xx * yz
    cof_zz = xx * yy - xy * xy
    det = xx * cof_xx + xy * cof_xy + xz * cof_xz
    inverse[0:1] = cof_xx / det
    inverse[1:2] = cof_xy / det
    inverse[2:3] = cof_xz / det
    inverse[3:4] = cof_yy / det
    inverse[4:5] = cof_yz / det
    inverse[5:6] = cof_zz / det
    inverse[6:8] = jnp.zeros((2, count), F32)


def own_rows(value):
    ids = lax.broadcasted_iota(jnp.int32, value.shape, 0)
    return jnp.where(ids % BLOCKS == 0, value, 0.0)


def lane_sums(value):
    return jnp.sum(value, axis=0, keepdims=True)


def schur(vector, where, jac_cam, jac_pt, camera, point_ref, inverse, hot, error, chunk, params, half, steps):
    count = camera.shape[1]
    slots = 2 * BLOCKS
    table = vector.reshape(params, half, slots, LANES)
    table = jnp.concatenate(
        [table[:, h].reshape(params * slots, LANES) for h in range(half)], axis=1
    )
    high, low = split(table)
    rows = params * slots

    def masks(span):
        camera_row = camera[:, span]
        tile = (camera_row // LANES) % (2 * half)
        slot = (tile % 2) * BLOCKS + camera_row // (2 * half * LANES)
        lane = (tile // 2) * LANES + camera_row % LANES
        return slot, lane

    def predict(i, _):
        span = pl.ds(pl.multiple_of(i * chunk, chunk), chunk)
        slot, lane = masks(span)
        spot = one_hot(lane, half * LANES).astype(BF16)
        hot[:, span] = spot
        got = jnp.dot(high, spot, preferred_element_type=F32)
        got = got + jnp.dot(low, spot, preferred_element_type=F32)
        mask = one_hot(slot, slots)
        for r in range(2):
            total = jnp.zeros((slots, chunk), F32)
            for a in range(params):
                jac = jac_cam[r * params + a : r * params + a + 1, span]
                total = total + jac * got[a * slots : (a + 1) * slots]
            error[r : r + 1, span] = lane_sums(total * mask)
        return 0

    lax.fori_loop(0, count // chunk, predict, 0)

    e0, e1 = error[0:1, :], error[1:2, :]
    jp = [jac_pt[r : r + 1, :] for r in range(6)]
    pulled = [jp[k] * e0 + jp[3 + k] * e1 for k in range(3)]
    pulled = jnp.concatenate(pulled + [jnp.zeros((5, count), F32)], axis=0)
    sums = point_totals(pulled, point_ref[...], steps)
    y0, y1, y2 = sums[0:1], sums[1:2], sums[2:3]
    inv = [inverse[r : r + 1, :] for r in range(6)]
    z = (
        inv[0] * y0 + inv[1] * y1 + inv[2] * y2,
        inv[1] * y0 + inv[3] * y1 + inv[4] * y2,
        inv[2] * y0 + inv[4] * y1 + inv[5] * y2,
    )
    left0 = e0 - (jp[0] * z[0] + jp[1] * z[1] + jp[2] * z[2])
    left1 = e1 - (jp[3] * z[0] + jp[4] * z[1] + jp[5] * z[2])
    energy = e0 * left0 + e1 * left1
    error[0:1, :] = left0
    error[1:2, :] = left1

    def push(i, total):
        span = pl.ds(pl.multiple_of(i * chunk, chunk), chunk)
        slot, _ = masks(span)
        mask = one_hot(slot, slots)
        first, second = error[0:1, span], error[1:2, span]
        highs, lows = [], []
        for a in range(params):
            value = jac_cam[a : a + 1, span] * first
            value = value + jac_cam[params + a : params + a + 1, span] * second
            near = value.astype(BF16).astype(F32)
            highs.append(near * mask)
            lows.append((value - near) * mask)
        both = jnp.concatenate(highs + lows, axis=0).astype(BF16)
        return total + lax.dot_general(
            both, hot[:, span], (((1,), (1,)), ((), ())), preferred_element_type=F32
        )

    total = lax.fori_loop(
        0, count // chunk, push, jnp.zeros((2 * rows, half * LANES), F32)
    )
    total = total[:rows] + total[rows:]
    for a in range(params):
        for h in range(half):
            start = (a * half + h) * slots
            where[start : start + slots, :] = total[
                a * slots : (a + 1) * slots, h * LANES : (h + 1) * LANES
            ]
    return sum(energy[:, t * LANES : (t + 1) * LANES] for t in range(count // LANES))


def prepare_kernel(position, anchors, right_side, camera_damping, preconditioner, bundle, kept):
    params, width = right_side.shape
    tiles = width // LANES
    ids = position[0] * width + lax.broadcasted_iota(jnp.int32, (1, width), 1)
    keep = jnp.ones((1, width), F32)
    for index in range(anchors.shape[0]):
        keep = jnp.where(ids == anchors[index], 0.0, keep)
    weights = preconditioner[...] * keep
    kept[...] = jnp.broadcast_to(keep, kept.shape)
    for t in range(tiles):
        lanes = slice(t * LANES, (t + 1) * LANES)
        for which, value in enumerate((right_side[...], weights, camera_damping[...])):
            place = pl.ds(which * params * tiles + t, params, stride=tiles)
            bundle[place, :] = value[:, lanes]


def send_rows(send, data_rows, rows):
    rest = send.shape[0] - data_rows
    send[data_rows:, :] = jnp.zeros((rest, LANES), F32)
    for index, row in enumerate(rows):
        send[data_rows + index : data_rows + index + 1, :] = row


def first_kernel(sizes, share, own, after, before, across, jac_cam, jac_pt, camera, point,
                 inverse, send, state, hot, error):
    chunk, params, half, steps = sizes
    data_rows = params * 2 * half * BLOCKS
    per = params * 2 * half
    for block, bundle in enumerate((own, after, before, across)):
        for which in range(3):
            place = pl.ds(which * data_rows + block, per, stride=BLOCKS)
            state[place, :] = bundle[which * per : (which + 1) * per, :]
    right = state[0:data_rows, :]
    vector = state[data_rows : 2 * data_rows, :] * right
    damping = state[2 * data_rows :, :]
    energy = schur(vector, send, jac_cam, jac_pt, camera, point, inverse, hot, error,
                   chunk, params, half, steps)
    energy = energy + share * lane_sums(own_rows(damping * vector * vector))
    gamma = share * lane_sums(own_rows(right * vector))
    send_rows(send, data_rows, (energy, gamma))


def scalar(ref, row):
    return jnp.sum(ref[row : row + 1, :], axis=1, keepdims=True)


def second_kernel(sizes, share, received, state, jac_cam, jac_pt, camera, point, inverse,
                  send, hot, error):
    chunk, params, half, steps = sizes
    data_rows = params * 2 * half * BLOCKS
    right = state[0:data_rows, :]
    weights = state[data_rows : 2 * data_rows, :]
    damping = state[2 * data_rows :, :]
    alpha = scalar(received, data_rows + 1) / scalar(received, data_rows)
    image = damping * (weights * right) + received[0:data_rows, :]
    residual = right - alpha * image
    vector = weights * residual
    energy = schur(vector, send, jac_cam, jac_pt, camera, point, inverse, hot, error,
                   chunk, params, half, steps)
    energy = energy + share * lane_sums(own_rows(damping * vector * vector))
    fresh = share * lane_sums(own_rows(residual * vector))
    cross = share * lane_sums(own_rows(image * vector))
    send_rows(send, data_rows, (energy, fresh, cross))


def last_kernel(half, first, second, state, kept, solution, residual):
    params, width = solution.shape
    tiles = 2 * half
    data_rows = params * tiles * BLOCKS
    curve, gamma = scalar(first, data_rows), scalar(first, data_rows + 1)
    alpha = gamma / curve
    energy, fresh = scalar(second, data_rows), scalar(second, data_rows + 1)
    cross = scalar(second, data_rows + 2)
    beta = fresh / gamma
    alpha_next = fresh / (energy + 2.0 * beta * cross + beta * beta * curve)
    for t in range(tiles):
        def own(ref, base):
            return ref[pl.ds(base + t * BLOCKS, params, stride=tiles * BLOCKS), :]

        right, weights, damping = (own(state, which * data_rows) for which in range(3))
        start = weights * right
        image = damping * start + own(first, 0)
        left = right - alpha * image
        vector = weights * left
        direction = vector + beta * start
        image_next = damping * vector + own(second, 0) + beta * image
        lanes = slice(t * LANES, (t + 1) * LANES)
        keep = kept[0:1, lanes]
        solution[:, lanes] = alpha * start + alpha_next * direction
        residual[:, lanes] = keep * (left - alpha_next * image_next)


def spread_kernel(received, send):
    total = received[0:8, :]
    for start in range(8, received.shape[0], 8):
        total = total + received[start : start + 8, :]
    total = total[0:BLOCKS] + total[BLOCKS:]
    total = jnp.concatenate([total, total], axis=0)
    for start in range(0, send.shape[0], 8):
        send[start : start + 8, :] = total


def combine_kernel(position, received, send):
    owners = received.shape[0] // BLOCKS
    me = position[0]

    def row(owner, block):
        spot = lax.rem(owner + 2 * owners, owners) * BLOCKS + block
        return received[pl.ds(spot, 1), :]

    def block_sum(owner):
        return (row(owner, 0) + row(owner - 1, 1)) + (
            row(owner + 1, 2) + row(owner + owners // 2, 3)
        )

    blocks = [block_sum(me + shift) for shift in (0, 1, -1, owners // 2)]
    joined = jnp.concatenate(blocks, axis=0)
    total = received[0:BLOCKS, :]
    for owner in range(1, owners):
        total = total + received[owner * BLOCKS : (owner + 1) * BLOCKS, :]
    joined = jnp.where(position[1] == 1, total, joined)
    joined = jnp.concatenate([joined, joined], axis=0)
    for start in range(0, send.shape[0], 8):
        send[start : start + 8, :] = joined


def call(kernel, outs, specs, *args, scratch=(), name=None):
    shapes = [jax.ShapeDtypeStruct(shape, dtype) for shape, dtype in outs]
    single = len(shapes) == 1
    return pl.pallas_call(
        kernel,
        out_shape=shapes[0] if single else shapes,
        in_specs=specs,
        out_specs=VMEM if single else [VMEM] * len(shapes),
        scratch_shapes=list(scratch),
        compiler_params=PARAMS,
        name=name,
    )(*args)


def swap(value, axis, size):
    value = value.reshape(size, BLOCKS, LANES)
    return lax.all_to_all(value, axis, 0, 0).reshape(size * BLOCKS, LANES)


def on_device(right_side, camera_damping, preconditioner, jac_cam, jac_pt, camera_index,
              point_index, point_damping, anchors):
    params, width = right_side.shape
    owners, rows = lax.axis_size("cam"), lax.axis_size("pts")
    tiles = width // LANES
    half = tiles // 2
    per = params * tiles
    data_rows = per * BLOCKS
    count = camera_index.shape[1]
    me = lax.axis_index("cam").astype(jnp.int32)
    position = jnp.stack([me, (lax.axis_index("pts") == per).astype(jnp.int32)])
    jac_cam, jac_pt = jac_cam[0], jac_pt[0]
    steps = (1, 2, 4, 8)
    sizes = (512, params, half, steps)
    share = 1.0 / rows

    bundle, kept = call(
        prepare_kernel, [((3 * per, LANES), F32), ((8, width), F32)],
        [SMEM, SMEM] + [VMEM] * 3, position, anchors, right_side, camera_damping,
        preconditioner, name="prepare",
    )
    after, before, across = (
        lax.ppermute(bundle, "cam", [(i, (i - d) % owners) for i in range(owners)])
        for d in (1, -1, owners // 2)
    )
    inverse, local = call(
        functools.partial(setup_kernel, steps, width, owners),
        [((8, count), F32), ((1, count), jnp.int32)],
        [SMEM] + [VMEM] * 4, position, jac_pt, point_index, point_damping[0], camera_index,
        name="invert",
    )
    scratch = (pltpu.VMEM((half * LANES, count), BF16), pltpu.VMEM((8, count), F32))
    send, state = call(
        functools.partial(first_kernel, sizes, share),
        [((rows * BLOCKS, LANES), F32), ((3 * data_rows, LANES), F32)],
        [VMEM] * 9, bundle, after, before, across, jac_cam, jac_pt, local, point_index,
        inverse, scratch=scratch, name="apply_first",
    )

    def reduce(send):
        chunks = swap(send, "pts", rows)
        chunks = call(spread_kernel, [((owners * BLOCKS, LANES), F32)], [VMEM], chunks, name="spread")
        chunks = swap(chunks, "cam", owners)
        chunks = call(
            combine_kernel, [((rows * BLOCKS, LANES), F32)], [SMEM, VMEM], position, chunks,
            name="combine",
        )
        return swap(chunks, "pts", rows)

    first = reduce(send)
    send = call(
        functools.partial(second_kernel, sizes, share), [((rows * BLOCKS, LANES), F32)],
        [VMEM] * 7, first, state, jac_cam, jac_pt, local, point_index, inverse,
        scratch=scratch, name="apply_second",
    )
    second = reduce(send)
    return tuple(
        call(
            functools.partial(last_kernel, half), [((params, width), F32)] * 2, [VMEM] * 4,
            first, second, state, kept, name="finish",
        )
    )


def solution(mesh):
    return jax.shard_map(
        on_device,
        mesh=mesh,
        in_specs=(
            P(None, "cam"),
            P(None, "cam"),
            P(None, "cam"),
            P(("pts", "cam"), None, None),
            P(("pts", "cam"), None, None),
            P(("pts", "cam"), None),
            P(("pts", "cam"), None),
            P(("pts", "cam"), None, None),
            P(),
        ),
        out_specs=(P(None, "cam"), P(None, "cam")),
        check_vma=False,
    )
```

```python
import functools

import jax
import jax.numpy as jnp
from jax import lax
from jax.experimental import pallas as pl
from jax.experimental.pallas import tpu as pltpu
from jax.sharding import PartitionSpec as P

LANES = 128
BLOCKS = 4
STEPS = (1, 2, 4, 8)
CHUNK = 512
F32, BF16 = jnp.float32, jnp.bfloat16
VMEM = pl.BlockSpec(memory_space=pltpu.VMEM)
SMEM = pl.BlockSpec(memory_space=pltpu.SMEM)
HBM = pl.BlockSpec(memory_space=pltpu.HBM)
PARAMS = pltpu.CompilerParams(vmem_limit_bytes=40 * 1024 * 1024)


def one_hot(row, count):
    ids = lax.broadcasted_iota(jnp.int32, (count, row.shape[1]), 0)
    return jnp.where(ids == row, 1.0, 0.0)


def short_one_hot(row, count):
    ids = lax.broadcasted_iota(jnp.int16, (count, row.shape[1]), 0)
    return jnp.where(ids == row.astype(jnp.int16), BF16(1), BF16(0))


def neighbour_masks(point):
    count = point.shape[1]
    before = [jnp.where(pltpu.roll(point, s, 1) == point, 1.0, 0.0) for s in STEPS]
    after = [pltpu.roll(mask, count - s, 1) for mask, s in zip(before, STEPS)]
    return jnp.concatenate(before + after, axis=0)


def point_totals(value, masks):
    count = value.shape[1]
    before = value
    after = value
    for i, step in enumerate(STEPS):
        j = len(STEPS) + i
        before = before + masks[i : i + 1] * pltpu.roll(before, step, 1)
        after = after + masks[j : j + 1] * pltpu.roll(after, count - step, 1)
    return before + (after - value)


def setup_kernel(width, owners, position, jac_pt, point_ref, damping, camera_ref,
                 inverse, masks, lane, slot):
    camera = camera_ref[...]
    shift = lax.rem(lax.div(camera, width) - position[0] + owners, owners)
    block = jnp.where(shift == 1, 1, jnp.where(shift == owners - 1, 2, 3))
    block = jnp.where(shift == 0, 0, block)
    inner = lax.rem(camera, width)
    tile = lax.div(inner, LANES)
    lane[...] = lax.div(tile, 2) * LANES + lax.rem(inner, LANES)
    slot[...] = lax.rem(tile, 2) * BLOCKS + block

    point = point_ref[...]
    count = point.shape[1]
    tiles = damping.shape[1] // LANES
    masks[...] = neighbour_masks(point)
    rows = [jac_pt[r : r + 1, :] for r in range(6)]
    pairs = [(0, 0), (0, 1), (0, 2), (1, 1), (1, 2), (2, 2)]
    prods = [rows[a] * rows[b] + rows[3 + a] * rows[3 + b] for a, b in pairs]
    prods = jnp.concatenate(prods + [jnp.zeros((2, count), F32)], axis=0)
    summed = point_totals(prods, masks[...])

    hot = one_hot(lax.rem(point, LANES), LANES).astype(BF16)
    tile_mask = one_hot(lax.div(point, LANES), tiles)
    table = jnp.concatenate(
        [damping[k : k + 1, t * LANES : (t + 1) * LANES] for k in range(3) for t in range(tiles)],
        axis=0,
    )
    high = table.astype(BF16)
    rest = table - high.astype(F32)
    mid = rest.astype(BF16)
    low = (rest - mid.astype(F32)).astype(BF16)
    picked = sum(
        jnp.dot(part, hot, preferred_element_type=F32) for part in (high, mid, low)
    )
    damp = [
        jnp.sum(picked[k * tiles : (k + 1) * tiles] * tile_mask, axis=0, keepdims=True)
        for k in range(3)
    ]
    xx = summed[0:1] + damp[0]
    xy = summed[1:2]
    xz = summed[2:3]
    yy = summed[3:4] + damp[1]
    yz = summed[4:5]
    zz = summed[5:6] + damp[2]
    cof_xx = yy * zz - yz * yz
    cof_xy = xz * yz - xy * zz
    cof_xz = xy * yz - xz * yy
    cof_yy = xx * zz - xz * xz
    cof_yz = xy * xz - xx * yz
    cof_zz = xx * yy - xy * xy
    det = xx * cof_xx + xy * cof_xy + xz * cof_xz
    inverse[0:1] = cof_xx / det
    inverse[1:2] = cof_xy / det
    inverse[2:3] = cof_xz / det
    inverse[3:4] = cof_yy / det
    inverse[4:5] = cof_yz / det
    inverse[5:6] = cof_zz / det
    inverse[6:8] = jnp.zeros((2, count), F32)


def lane_sums(value):
    return jnp.sum(value, axis=0, keepdims=True)


def schur(vector, send, jac_cam, jac_pt, lane, slot, masks, inverse, hot, error):
    count = lane.shape[1]
    params = jac_cam.shape[0] // 2
    slots = 2 * BLOCKS
    half = hot.shape[0] // LANES
    rows = params * slots
    table = vector.reshape(params, half, slots, LANES)
    table = jnp.concatenate([table[:, h].reshape(rows, LANES) for h in range(half)], axis=1)
    high = table.astype(BF16)
    low = (table - high.astype(F32)).astype(BF16)
    table = jnp.concatenate([high, low], axis=0)

    def predict(i, _):
        span = pl.ds(pl.multiple_of(i * CHUNK, CHUNK), CHUNK)
        spot = short_one_hot(lane[:, span], half * LANES)
        hot[:, span] = spot
        got = jnp.dot(table, spot, preferred_element_type=F32)
        got = got[:rows] + got[rows:]
        mask = one_hot(slot[:, span], slots)
        for r in range(2):
            total = jnp.zeros((slots, CHUNK), F32)
            for a in range(params):
                jac = jac_cam[r * params + a : r * params + a + 1, span]
                total = total + jac * got[a * slots : (a + 1) * slots]
            error[r : r + 1, span] = lane_sums(total * mask)
        return 0

    lax.fori_loop(0, count // CHUNK, predict, 0, unroll=count // CHUNK)

    e0, e1 = error[0:1, :], error[1:2, :]
    jp = [jac_pt[r : r + 1, :] for r in range(6)]
    pulled = [jp[k] * e0 + jp[3 + k] * e1 for k in range(3)]
    pulled = jnp.concatenate(pulled + [jnp.zeros((5, count), F32)], axis=0)
    sums = point_totals(pulled, masks[...])
    y0, y1, y2 = sums[0:1], sums[1:2], sums[2:3]
    inv = [inverse[r : r + 1, :] for r in range(6)]
    z = (
        inv[0] * y0 + inv[1] * y1 + inv[2] * y2,
        inv[1] * y0 + inv[3] * y1 + inv[4] * y2,
        inv[2] * y0 + inv[4] * y1 + inv[5] * y2,
    )
    left0 = e0 - (jp[0] * z[0] + jp[1] * z[1] + jp[2] * z[2])
    left1 = e1 - (jp[3] * z[0] + jp[4] * z[1] + jp[5] * z[2])
    energy = e0 * left0 + e1 * left1
    error[0:1, :] = left0
    error[1:2, :] = left1

    def push(i, total):
        span = pl.ds(pl.multiple_of(i * CHUNK, CHUNK), CHUNK)
        mask = one_hot(slot[:, span], slots)
        first, second = error[0:1, span], error[1:2, span]
        highs, lows = [], []
        for a in range(params):
            value = jac_cam[a : a + 1, span] * first
            value = value + jac_cam[params + a : params + a + 1, span] * second
            near = value.astype(BF16).astype(F32)
            highs.append(near * mask)
            lows.append((value - near) * mask)
        both = jnp.concatenate(highs + lows, axis=0).astype(BF16)
        return total + lax.dot_general(
            both, hot[:, span], (((1,), (1,)), ((), ())), preferred_element_type=F32
        )

    total = jnp.zeros((2 * rows, half * LANES), F32)
    total = lax.fori_loop(0, count // CHUNK, push, total, unroll=count // CHUNK)
    total = total[:rows] + total[rows:]
    for a in range(params):
        for h in range(half):
            start = (a * half + h) * slots
            send[start : start + slots, :] = total[
                a * slots : (a + 1) * slots, h * LANES : (h + 1) * LANES
            ]
    return sum(energy[:, t * LANES : (t + 1) * LANES] for t in range(count // LANES))


RIGHT, DAMPING, WEIGHTS, PULL, UNWEIGH = range(5)


def own_part(own, which):
    per = own.shape[0] // 5
    return own[which * per : (which + 1) * per, :]


def prepare_kernel(position, anchors, right_side, camera_damping, preconditioner, start,
                   own, right, damping, precond, sems):
    params, width = right.shape
    tiles = width // LANES
    pairs = ((right_side, right), (camera_damping, damping), (preconditioner, precond))
    copies = [
        pltpu.make_async_copy(source, target, sems.at[i])
        for i, (source, target) in enumerate(pairs)
    ]
    for copy in copies:
        copy.start()
    ids = position[0] * width + lax.broadcasted_iota(jnp.int32, (1, width), 1)
    keep = jnp.ones((1, width), F32)
    for index in range(anchors.shape[0]):
        keep = jnp.where(ids == anchors[index], 0.0, keep)
    for copy in copies:
        copy.wait()
    weights = precond[...] * keep
    vector = weights * right[...]
    parts = [right[...], damping[...], weights, weights * damping[...] * vector]
    parts.append(keep / precond[...])
    for t in range(tiles):
        lanes = slice(t * LANES, (t + 1) * LANES)
        start[pl.ds(t, params, stride=tiles), :] = vector[:, lanes]
        for which, value in enumerate(parts):
            place = pl.ds(which * params * tiles + t, params, stride=tiles)
            own[place, :] = value[:, lanes]


def send_scalars(send, data_rows, rows):
    rest = send.shape[0] - data_rows
    send[data_rows:, :] = jnp.zeros((rest, LANES), F32)
    for index, row in enumerate(rows):
        at = data_rows + index * BLOCKS
        send[at : at + 1, :] = row


def scalar(ref, row):
    return jnp.sum(ref[row : row + 1, :], axis=1, keepdims=True)


def first_kernel(share, mine, after, before, across, own, jac_cam, jac_pt, lane, slot,
                 masks, inverse, send, start, hot, error):
    per = mine.shape[0]
    for block, part in enumerate((mine, after, before, across)):
        start[pl.ds(block, per, stride=BLOCKS), :] = part[...]
    energy = schur(start[...], send, jac_cam, jac_pt, lane, slot, masks, inverse, hot, error)
    vector = mine[...]
    energy = energy + share * lane_sums(own_part(own, DAMPING) * vector * vector)
    gamma = share * lane_sums(own_part(own, RIGHT) * vector)
    send_scalars(send, start.shape[0], (energy, gamma))


def second_kernel(share, received, start, own, jac_cam, jac_pt, lane, slot, masks, inverse,
                  send, step, hot, error):
    data_rows = start.shape[0]
    per = data_rows // BLOCKS
    alpha = scalar(received, data_rows + BLOCKS) / scalar(received, data_rows)
    step[...] = start[...] - alpha * received[0:data_rows, :]
    energy = schur(step[...], send, jac_cam, jac_pt, lane, slot, masks, inverse, hot, error)
    vector = step[pl.ds(0, per, stride=BLOCKS), :]
    change = received[pl.ds(0, per, stride=BLOCKS), :]
    residual = own_part(own, UNWEIGH) * vector
    energy = energy + share * lane_sums(own_part(own, DAMPING) * vector * vector)
    fresh = share * lane_sums(residual * vector)
    cross = share * lane_sums(residual * change)
    send_scalars(send, data_rows, (energy, fresh, cross))


def last_kernel(first, second, start, step, own, solution, residual):
    params, width = solution.shape
    tiles = width // LANES
    per = params * tiles
    data_rows = per * BLOCKS
    curve, gamma = scalar(first, data_rows), scalar(first, data_rows + BLOCKS)
    energy, fresh, cross = (scalar(second, per + i) for i in range(3))
    alpha = gamma / curve
    beta = fresh / gamma
    alpha_next = fresh / (energy + 2.0 * beta * cross + beta * beta * curve)
    for t in range(tiles):
        spread = pl.ds(t * BLOCKS, params, stride=tiles * BLOCKS)
        begin, vector, change = start[spread, :], step[spread, :], first[spread, :]
        terms = second[pl.ds(t, params, stride=tiles), :]
        damping, unweigh = (
            own[pl.ds(which * per + t, params, stride=tiles), :] for which in (DAMPING, UNWEIGH)
        )
        direction = vector + beta * begin
        image = jnp.where(unweigh > 0.0, damping * vector + terms, 0.0)
        image = image + beta * (unweigh * change)
        lanes = slice(t * LANES, (t + 1) * LANES)
        solution[:, lanes] = alpha * begin + alpha_next * direction
        residual[:, lanes] = unweigh * vector - alpha_next * image


def chunk_sum(received):
    total = received[0:8, :]
    for at in range(8, received.shape[0], 8):
        total = total + received[at : at + 8, :]
    return total[0:BLOCKS] + total[BLOCKS:]


def spread_kernel(position, received, own, send):
    total = chunk_sum(received)
    per = own.shape[0] // 5
    rows = [own[pl.ds(which * per + position[2], 1), :] for which in (WEIGHTS, PULL)]
    total = jnp.concatenate([total, *rows, jnp.zeros((2, LANES), F32)], axis=0)
    for at in range(0, send.shape[0], 8):
        send[at : at + 8, :] = total


def combine_kernel(position, received, send):
    owners = received.shape[0] // 8
    me = position[0]

    def row(owner, at):
        spot = lax.rem(owner + 2 * owners, owners) * 8 + at
        return received[pl.ds(spot, 1), :]

    def block_change(owner):
        terms = (row(owner, 0) + row(owner - 1, 1)) + (
            row(owner + 1, 2) + row(owner + owners // 2, 3)
        )
        return row(owner, BLOCKS + 1) + row(owner, BLOCKS) * terms

    joined = [block_change(me + shift) for shift in (0, 1, -1, owners // 2)]
    joined = jnp.concatenate(joined, axis=0)
    total = received[0:8, :]
    for owner in range(1, owners):
        total = total + received[owner * 8 : (owner + 1) * 8, :]
    joined = jnp.where(position[1] == 1, total[0:BLOCKS], joined)
    joined = jnp.concatenate([joined, joined], axis=0)
    for at in range(0, send.shape[0], 8):
        send[at : at + 8, :] = joined


def spread_own_kernel(position, received, send):
    total = chunk_sum(received)
    owners = send.shape[0]
    scalars = jnp.broadcast_to(total[0:1], send.shape)
    send[...] = jnp.where(position[1] == 1, scalars, 0.0)

    @pl.when(position[1] == 0)
    def _():
        for block, shift in enumerate((0, 1, -1, owners // 2)):
            spot = lax.rem(position[0] + shift + owners, owners)
            send[pl.ds(spot, 1), :] = total[block : block + 1]


def combine_own_kernel(received, send):
    total = received[0:8, :]
    for at in range(8, received.shape[0], 8):
        total = total + received[at : at + 8, :]
    send[...] = jnp.broadcast_to(lane_sums(total), send.shape)


def call(kernel, outs, specs, *args, scratch=(), name=None):
    shapes = [jax.ShapeDtypeStruct(shape, dtype) for shape, dtype in outs]
    single = len(shapes) == 1
    return pl.pallas_call(
        kernel,
        out_shape=shapes[0] if single else shapes,
        in_specs=specs,
        out_specs=VMEM if single else [VMEM] * len(shapes),
        scratch_shapes=list(scratch),
        compiler_params=PARAMS,
        name=name,
    )(*args)


def swap(value, axis, size):
    rows = value.shape[0] // size
    value = value.reshape(size, rows, LANES)
    return lax.all_to_all(value, axis, 0, 0).reshape(size * rows, LANES)


def on_device(right_side, camera_damping, preconditioner, jac_cam, jac_pt, camera_index,
              point_index, point_damping, anchors):
    params, width = right_side.shape
    owners, rows = lax.axis_size("cam"), lax.axis_size("pts")
    per = params * width // LANES
    count = camera_index.shape[1]
    me = lax.axis_index("cam").astype(jnp.int32)
    spot = lax.axis_index("pts").astype(jnp.int32)
    position = jnp.stack([me, (spot >= per).astype(jnp.int32), jnp.minimum(spot, per - 1)])
    jac_cam, jac_pt = jac_cam[0], jac_pt[0]
    share = 1.0 / rows

    mine, own = call(
        prepare_kernel, [((per, LANES), F32), ((5 * per, LANES), F32)],
        [SMEM, SMEM] + [HBM] * 3, position, anchors, right_side, camera_damping, preconditioner,
        scratch=[pltpu.VMEM((params, width), F32)] * 3 + [pltpu.SemaphoreType.DMA((3,))],
        name="prepare",
    )
    after, before, across = (
        lax.ppermute(mine, "cam", [(i, (i - d) % owners) for i in range(owners)])
        for d in (1, -1, owners // 2)
    )
    inverse, masks, lane, slot = call(
        functools.partial(setup_kernel, width, owners),
        [((8, count), F32), ((8, count), F32), ((1, count), jnp.int32), ((1, count), jnp.int32)],
        [SMEM] + [VMEM] * 4, position, jac_pt, point_index, point_damping[0], camera_index,
        name="invert",
    )
    fixed = (jac_cam, jac_pt, lane, slot, masks, inverse)
    half = width // (2 * LANES)
    scratch = (pltpu.VMEM((half * LANES, count), BF16), pltpu.VMEM((8, count), F32))
    sums = ((rows * BLOCKS, LANES), F32)
    vector = ((per * BLOCKS, LANES), F32)

    send, start = call(
        functools.partial(first_kernel, share), [sums, vector], [VMEM] * 11,
        mine, after, before, across, own, *fixed, scratch=scratch, name="apply_first",
    )
    chunks = swap(send, "pts", rows)
    chunks = call(
        spread_kernel, [((owners * 8, LANES), F32)], [SMEM, VMEM, VMEM], position, chunks, own,
        name="spread",
    )
    chunks = swap(chunks, "cam", owners)
    chunks = call(combine_kernel, [sums], [SMEM, VMEM], position, chunks, name="combine")
    first = swap(chunks, "pts", rows)

    send, step = call(
        functools.partial(second_kernel, share), [sums, vector], [VMEM] * 9,
        first, start, own, *fixed, scratch=scratch, name="apply_second",
    )
    chunks = swap(send, "pts", rows)
    chunks = call(
        spread_own_kernel, [((owners, LANES), F32)], [SMEM, VMEM], position, chunks,
        name="spread_own",
    )
    chunks = swap(chunks, "cam", owners)
    chunks = call(
        combine_own_kernel, [((rows, LANES), F32)], [VMEM], chunks, name="combine_own"
    )
    second = swap(chunks, "pts", rows)
    return tuple(
        call(
            last_kernel, [((params, width), F32)] * 2, [VMEM] * 5, first, second, start, step,
            own, name="finish",
        )
    )


def solution(mesh):
    return jax.shard_map(
        on_device,
        mesh=mesh,
        in_specs=(
            P(None, "cam"),
            P(None, "cam"),
            P(None, "cam"),
            P(("pts", "cam"), None, None),
            P(("pts", "cam"), None, None),
            P(("pts", "cam"), None),
            P(("pts", "cam"), None),
            P(("pts", "cam"), None, None),
            P(),
        ),
        out_specs=(P(None, "cam"), P(None, "cam")),
        check_vma=False,
    )
```

```python
import functools

import jax
import jax.numpy as jnp
from jax import lax
from jax.experimental import pallas as pl
from jax.experimental.pallas import tpu as pltpu
from jax.sharding import PartitionSpec as P

LANES = 128
BLOCKS = 4
STEPS = (1, 2, 4, 8)
CHUNK = 512
F32, BF16 = jnp.float32, jnp.bfloat16
VMEM = pl.BlockSpec(memory_space=pltpu.VMEM)
PARAMS = pltpu.CompilerParams(vmem_limit_bytes=40 * 1024 * 1024)


def one_hot(row, count):
    ids = lax.broadcasted_iota(jnp.int32, (count, row.shape[1]), 0)
    return jnp.where(ids == row, 1.0, 0.0)


def short_one_hot(row, count):
    ids = lax.broadcasted_iota(jnp.int16, (count, row.shape[1]), 0)
    return jnp.where(ids == row.astype(jnp.int16), BF16(1), BF16(0))


def neighbour_masks(point):
    count = point.shape[1]
    before = [jnp.where(pltpu.roll(point, s, 1) == point, 1.0, 0.0) for s in STEPS]
    after = [pltpu.roll(mask, count - s, 1) for mask, s in zip(before, STEPS)]
    return jnp.concatenate(before + after, axis=0)


def point_totals(value, masks):
    count = value.shape[1]
    before = value
    after = value
    for i, step in enumerate(STEPS):
        j = len(STEPS) + i
        before = before + masks[i : i + 1] * pltpu.roll(before, step, 1)
        after = after + masks[j : j + 1] * pltpu.roll(after, count - step, 1)
    return before + (after - value)


def setup_kernel(owners, jac_pt, point_ref, damping, camera_ref, right_side, camera_damping,
                 preconditioner, keep, inverse, masks, lane, slot, own):
    width = right_side.shape[1]
    own_arrays(right_side[...], camera_damping[...], preconditioner[...], keep[...], own)
    camera = camera_ref[...]
    shift = lax.rem(lax.div(camera, width) - lax.axis_index("cam") + owners, owners)
    block = jnp.where(shift == 1, 1, jnp.where(shift == owners - 1, 2, 3))
    block = jnp.where(shift == 0, 0, block)
    inner = lax.rem(camera, width)
    tile = lax.div(inner, LANES)
    lane[...] = lax.div(tile, 2) * LANES + lax.rem(inner, LANES)
    slot[...] = lax.rem(tile, 2) * BLOCKS + block

    point = point_ref[...]
    count = point.shape[1]
    tiles = damping.shape[1] // LANES
    masks[...] = neighbour_masks(point)
    rows = [jac_pt[r : r + 1, :] for r in range(6)]
    pairs = [(0, 0), (0, 1), (0, 2), (1, 1), (1, 2), (2, 2)]
    prods = [rows[a] * rows[b] + rows[3 + a] * rows[3 + b] for a, b in pairs]
    prods = jnp.concatenate(prods + [jnp.zeros((2, count), F32)], axis=0)
    summed = point_totals(prods, masks[...])

    hot = one_hot(lax.rem(point, LANES), LANES).astype(BF16)
    tile_mask = one_hot(lax.div(point, LANES), tiles)
    table = jnp.concatenate(
        [damping[k : k + 1, t * LANES : (t + 1) * LANES] for k in range(3) for t in range(tiles)],
        axis=0,
    )
    high = table.astype(BF16)
    rest = table - high.astype(F32)
    mid = rest.astype(BF16)
    low = (rest - mid.astype(F32)).astype(BF16)
    picked = sum(
        jnp.dot(part, hot, preferred_element_type=F32) for part in (high, mid, low)
    )
    damp = [
        jnp.sum(picked[k * tiles : (k + 1) * tiles] * tile_mask, axis=0, keepdims=True)
        for k in range(3)
    ]
    xx = summed[0:1] + damp[0]
    xy = summed[1:2]
    xz = summed[2:3]
    yy = summed[3:4] + damp[1]
    yz = summed[4:5]
    zz = summed[5:6] + damp[2]
    cof_xx = yy * zz - yz * yz
    cof_xy = xz * yz - xy * zz
    cof_xz = xy * yz - xz * yy
    cof_yy = xx * zz - xz * xz
    cof_yz = xy * xz - xx * yz
    cof_zz = xx * yy - xy * xy
    det = xx * cof_xx + xy * cof_xy + xz * cof_xz
    inverse[0:1] = cof_xx / det
    inverse[1:2] = cof_xy / det
    inverse[2:3] = cof_xz / det
    inverse[3:4] = cof_yy / det
    inverse[4:5] = cof_yz / det
    inverse[5:6] = cof_zz / det
    inverse[6:8] = jnp.zeros((2, count), F32)


def lane_sums(value):
    return jnp.sum(value, axis=0, keepdims=True)


def schur(vector, send, jac_cam, jac_pt, lane, slot, masks, inverse, hot, error):
    count = lane.shape[1]
    params = jac_cam.shape[0] // 2
    slots = 2 * BLOCKS
    half = hot.shape[0] // LANES
    rows = params * slots
    table = vector.reshape(params, half, slots, LANES)
    table = jnp.concatenate([table[:, h].reshape(rows, LANES) for h in range(half)], axis=1)
    high = table.astype(BF16)
    low = (table - high.astype(F32)).astype(BF16)
    table = jnp.concatenate([high, low], axis=0)

    def predict(i, _):
        span = pl.ds(pl.multiple_of(i * CHUNK, CHUNK), CHUNK)
        spot = short_one_hot(lane[:, span], half * LANES)
        hot[:, span] = spot
        got = jnp.dot(table, spot, preferred_element_type=F32)
        got = got[:rows] + got[rows:]
        mask = one_hot(slot[:, span], slots)
        for r in range(2):
            total = jnp.zeros((slots, CHUNK), F32)
            for a in range(params):
                jac = jac_cam[r * params + a : r * params + a + 1, span]
                total = total + jac * got[a * slots : (a + 1) * slots]
            error[r : r + 1, span] = lane_sums(total * mask)
        return 0

    lax.fori_loop(0, count // CHUNK, predict, 0, unroll=count // CHUNK)

    e0, e1 = error[0:1, :], error[1:2, :]
    jp = [jac_pt[r : r + 1, :] for r in range(6)]
    pulled = [jp[k] * e0 + jp[3 + k] * e1 for k in range(3)]
    pulled = jnp.concatenate(pulled + [jnp.zeros((5, count), F32)], axis=0)
    sums = point_totals(pulled, masks[...])
    y0, y1, y2 = sums[0:1], sums[1:2], sums[2:3]
    inv = [inverse[r : r + 1, :] for r in range(6)]
    z = (
        inv[0] * y0 + inv[1] * y1 + inv[2] * y2,
        inv[1] * y0 + inv[3] * y1 + inv[4] * y2,
        inv[2] * y0 + inv[4] * y1 + inv[5] * y2,
    )
    left0 = e0 - (jp[0] * z[0] + jp[1] * z[1] + jp[2] * z[2])
    left1 = e1 - (jp[3] * z[0] + jp[4] * z[1] + jp[5] * z[2])
    energy = e0 * left0 + e1 * left1
    error[0:1, :] = left0
    error[1:2, :] = left1

    def push(i, total):
        span = pl.ds(pl.multiple_of(i * CHUNK, CHUNK), CHUNK)
        mask = one_hot(slot[:, span], slots)
        first, second = error[0:1, span], error[1:2, span]
        highs, lows = [], []
        for a in range(params):
            value = jac_cam[a : a + 1, span] * first
            value = value + jac_cam[params + a : params + a + 1, span] * second
            near = value.astype(BF16).astype(F32)
            highs.append(near * mask)
            lows.append((value - near) * mask)
        both = jnp.concatenate(highs + lows, axis=0).astype(BF16)
        return total + lax.dot_general(
            both, hot[:, span], (((1,), (1,)), ((), ())), preferred_element_type=F32
        )

    total = jnp.zeros((2 * rows, half * LANES), F32)
    total = lax.fori_loop(0, count // CHUNK, push, total, unroll=count // CHUNK)
    total = total[:rows] + total[rows:]
    for a in range(params):
        for h in range(half):
            start = (a * half + h) * slots
            send[start : start + slots, :] = total[
                a * slots : (a + 1) * slots, h * LANES : (h + 1) * LANES
            ]
    return sum(energy[:, t * LANES : (t + 1) * LANES] for t in range(count // LANES))


RIGHT, DAMPING, WEIGHTS, PULL, UNWEIGH = range(5)


def own_part(own, which):
    per = own.shape[0] // 5
    return own[which * per : (which + 1) * per, :]


def own_arrays(right, damping, precond, keep, own):
    params, width = right.shape
    tiles = width // LANES
    weights = precond * keep
    parts = (right, damping, weights, weights * damping * weights * right, keep / precond)
    for t in range(tiles):
        lanes = slice(t * LANES, (t + 1) * LANES)
        for which, value in enumerate(parts):
            place = pl.ds(which * params * tiles + t, params, stride=tiles)
            own[place, :] = value[:, lanes]


def send_scalars(send, data_rows, rows):
    rest = send.shape[0] - data_rows
    send[data_rows:, :] = jnp.zeros((rest, LANES), F32)
    for index, row in enumerate(rows):
        at = data_rows + index * BLOCKS
        send[at : at + 1, :] = row


def scalar(ref, row):
    return jnp.sum(ref[row : row + 1, :], axis=1, keepdims=True)


def first_kernel(share, mine, after, before, across, own, jac_cam, jac_pt, lane, slot,
                 masks, inverse, send, start, hot, error):
    params, width = mine.shape
    tiles = width // LANES
    for block, part in enumerate((mine, after, before, across)):
        for t in range(tiles):
            place = pl.ds(t * BLOCKS + block, params, stride=tiles * BLOCKS)
            start[place, :] = part[:, t * LANES : (t + 1) * LANES]
    energy = schur(start[...], send, jac_cam, jac_pt, lane, slot, masks, inverse, hot, error)
    vector = start[pl.ds(0, params * tiles, stride=BLOCKS), :]
    energy = energy + share * lane_sums(own_part(own, DAMPING) * vector * vector)
    gamma = share * lane_sums(own_part(own, RIGHT) * vector)
    send_scalars(send, start.shape[0], (energy, gamma))


def second_kernel(share, received, start, own, jac_cam, jac_pt, lane, slot, masks, inverse,
                  send, step, hot, error):
    data_rows = start.shape[0]
    per = data_rows // BLOCKS
    alpha = scalar(received, data_rows + BLOCKS) / scalar(received, data_rows)
    step[...] = start[...] - alpha * received[0:data_rows, :]
    energy = schur(step[...], send, jac_cam, jac_pt, lane, slot, masks, inverse, hot, error)
    vector = step[pl.ds(0, per, stride=BLOCKS), :]
    change = received[pl.ds(0, per, stride=BLOCKS), :]
    residual = own_part(own, UNWEIGH) * vector
    energy = energy + share * lane_sums(own_part(own, DAMPING) * vector * vector)
    fresh = share * lane_sums(residual * vector)
    cross = share * lane_sums(residual * change)
    send_scalars(send, data_rows, (energy, fresh, cross))


def last_kernel(first, second, start, step, own, solution, residual):
    params, width = solution.shape
    tiles = width // LANES
    per = params * tiles
    data_rows = per * BLOCKS
    curve, gamma = scalar(first, data_rows), scalar(first, data_rows + BLOCKS)
    energy, fresh, cross = (scalar(second, per + i) for i in range(3))
    alpha = gamma / curve
    beta = fresh / gamma
    alpha_next = fresh / (energy + 2.0 * beta * cross + beta * beta * curve)
    for t in range(tiles):
        spread = pl.ds(t * BLOCKS, params, stride=tiles * BLOCKS)
        begin, vector, change = start[spread, :], step[spread, :], first[spread, :]
        terms = second[pl.ds(t, params, stride=tiles), :]
        damping, unweigh = (
            own[pl.ds(which * per + t, params, stride=tiles), :] for which in (DAMPING, UNWEIGH)
        )
        direction = vector + beta * begin
        image = jnp.where(unweigh > 0.0, damping * vector + terms, 0.0)
        image = image + beta * (unweigh * change)
        lanes = slice(t * LANES, (t + 1) * LANES)
        solution[:, lanes] = alpha * begin + alpha_next * direction
        residual[:, lanes] = unweigh * vector - alpha_next * image


def chunk_sum(received):
    total = received[0:8, :]
    for at in range(8, received.shape[0], 8):
        total = total + received[at : at + 8, :]
    return total[0:BLOCKS] + total[BLOCKS:]


def spread_kernel(received, own, send):
    total = chunk_sum(received)
    per = own.shape[0] // 5
    at = jnp.minimum(lax.axis_index("pts"), per - 1)
    rows = [own[pl.ds(which * per + at, 1), :] for which in (WEIGHTS, PULL)]
    total = jnp.concatenate([total, *rows, jnp.zeros((2, LANES), F32)], axis=0)
    for at in range(0, send.shape[0], 8):
        send[at : at + 8, :] = total


def combine_kernel(per, received, send):
    owners = received.shape[0] // 8
    me = lax.axis_index("cam")

    def row(owner, at):
        spot = lax.rem(owner + 2 * owners, owners) * 8 + at
        return received[pl.ds(spot, 1), :]

    def block_change(owner):
        terms = (row(owner, 0) + row(owner - 1, 1)) + (
            row(owner + 1, 2) + row(owner + owners // 2, 3)
        )
        return row(owner, BLOCKS + 1) + row(owner, BLOCKS) * terms

    joined = [block_change(me + shift) for shift in (0, 1, -1, owners // 2)]
    joined = jnp.concatenate(joined, axis=0)
    total = received[0:8, :]
    for owner in range(1, owners):
        total = total + received[owner * 8 : (owner + 1) * 8, :]
    joined = jnp.where(lax.axis_index("pts") >= per, total[0:BLOCKS], joined)
    joined = jnp.concatenate([joined, joined], axis=0)
    for at in range(0, send.shape[0], 8):
        send[at : at + 8, :] = joined


def spread_own_kernel(per, received, send):
    total = chunk_sum(received)
    owners = send.shape[0]
    scalars = jnp.broadcast_to(total[0:1], send.shape)
    chunk = lax.axis_index("pts")
    send[...] = jnp.where(chunk >= per, scalars, 0.0)

    @pl.when(chunk < per)
    def _():
        for block, shift in enumerate((0, 1, -1, owners // 2)):
            spot = lax.rem(lax.axis_index("cam") + shift + owners, owners)
            send[pl.ds(spot, 1), :] = total[block : block + 1]


def combine_own_kernel(received, send):
    total = received[0:8, :]
    for at in range(8, received.shape[0], 8):
        total = total + received[at : at + 8, :]
    send[...] = jnp.broadcast_to(lane_sums(total), send.shape)


def call(kernel, outs, *args, scratch=(), name=None):
    single = not isinstance(outs, list)
    return pl.pallas_call(
        kernel,
        out_shape=outs,
        in_specs=[VMEM] * len(args),
        out_specs=VMEM if single else [VMEM] * len(outs),
        scratch_shapes=list(scratch),
        compiler_params=PARAMS,
        name=name,
    )(*args)


def swap(value, axis, size):
    rows = value.shape[0] // size
    value = value.reshape(size, rows, LANES)
    return lax.all_to_all(value, axis, 0, 0).reshape(size * rows, LANES)


def on_device(right_side, camera_damping, preconditioner, jac_cam, jac_pt, camera_index,
              point_index, point_damping, anchors):
    params, width = right_side.shape
    owners, rows = lax.axis_size("cam"), lax.axis_size("pts")
    per = params * width // LANES
    count = camera_index.shape[1]
    jac_cam, jac_pt = jac_cam[0], jac_pt[0]
    share = 1.0 / rows

    ids = lax.axis_index("cam") * width + jnp.arange(width, dtype=jnp.int32)
    keep = 1.0 - jnp.any(anchors[:, None] == ids[None, :], axis=0).astype(F32)
    mine = keep * (preconditioner * right_side)
    after, before, across = (
        lax.ppermute(mine, "cam", [(i, (i - d) % owners) for i in range(owners)])
        for d in (1, -1, owners // 2)
    )
    whole = jax.ShapeDtypeStruct((8, count), F32)
    index = jax.ShapeDtypeStruct((1, count), jnp.int32)
    inverse, masks, lane, slot, own = call(
        functools.partial(setup_kernel, owners),
        [whole, whole, index, index, jax.ShapeDtypeStruct((5 * per, LANES), F32)],
        jac_pt, point_index, point_damping[0], camera_index, right_side, camera_damping,
        preconditioner, keep[None], name="invert",
    )
    fixed = (jac_cam, jac_pt, lane, slot, masks, inverse)
    half = width // (2 * LANES)
    scratch = (pltpu.VMEM((half * LANES, count), BF16), pltpu.VMEM((8, count), F32))
    sums = jax.ShapeDtypeStruct((rows * BLOCKS, LANES), F32)
    vector = jax.ShapeDtypeStruct((per * BLOCKS, LANES), F32)

    send, start = call(
        functools.partial(first_kernel, share), [sums, vector],
        mine, after, before, across, own, *fixed, scratch=scratch, name="apply_first",
    )
    chunks = swap(send, "pts", rows)
    shape = jax.ShapeDtypeStruct((owners * 8, LANES), F32)
    chunks = call(spread_kernel, shape, chunks, own, name="spread")
    chunks = swap(chunks, "cam", owners)
    chunks = call(functools.partial(combine_kernel, per), sums, chunks, name="combine")
    first = swap(chunks, "pts", rows)

    send, step = call(
        functools.partial(second_kernel, share), [sums, vector],
        first, start, own, *fixed, scratch=scratch, name="apply_second",
    )
    chunks = swap(send, "pts", rows)
    shape = jax.ShapeDtypeStruct((owners, LANES), F32)
    chunks = call(functools.partial(spread_own_kernel, per), shape, chunks, name="spread_own")
    chunks = swap(chunks, "cam", owners)
    shape = jax.ShapeDtypeStruct((rows, LANES), F32)
    chunks = call(combine_own_kernel, shape, chunks, name="combine_own")
    second = swap(chunks, "pts", rows)
    shape = jax.ShapeDtypeStruct((params, width), F32)
    return tuple(call(last_kernel, [shape, shape], first, second, start, step, own, name="finish"))


def solution(mesh):
    return jax.shard_map(
        on_device,
        mesh=mesh,
        in_specs=(
            P(None, "cam"),
            P(None, "cam"),
            P(None, "cam"),
            P(("pts", "cam"), None, None),
            P(("pts", "cam"), None, None),
            P(("pts", "cam"), None),
            P(("pts", "cam"), None),
            P(("pts", "cam"), None, None),
            P(),
        ),
        out_specs=(P(None, "cam"), P(None, "cam")),
        check_vma=False,
    )
```

```python
import functools

import jax
import jax.numpy as jnp
from jax import lax
from jax.experimental import pallas as pl
from jax.experimental.pallas import tpu as pltpu
from jax.sharding import PartitionSpec as P

LANES = 128
BLOCKS = 4
STEPS = (1, 2, 4, 8)
CHUNK = 512
FOLDS = 8
F32, BF16 = jnp.float32, jnp.bfloat16
VMEM = pl.BlockSpec(memory_space=pltpu.VMEM)
PARAMS = pltpu.CompilerParams(vmem_limit_bytes=40 * 1024 * 1024)


def one_hot(row, count):
    ids = lax.broadcasted_iota(jnp.int32, (count, row.shape[1]), 0)
    return jnp.where(ids == row, 1.0, 0.0)


def short_one_hot(row, count):
    ids = lax.broadcasted_iota(jnp.int16, (count, row.shape[1]), 0)
    return jnp.where(ids == row.astype(jnp.int16), BF16(1), BF16(0))


def fold(ref, row):
    parts = [ref[row : row + 1, i * CHUNK : (i + 1) * CHUNK] for i in range(FOLDS)]
    return jnp.concatenate(parts, axis=0)


def shifted(value, step):
    ids = lax.broadcasted_iota(jnp.int32, value.shape, 1)
    rolled = pltpu.roll(value, step % CHUNK, 1)
    if step > 0:
        return jnp.where(ids < step, pltpu.roll(rolled, 1, 0), rolled)
    return jnp.where(ids >= CHUNK + step, pltpu.roll(rolled, FOLDS - 1, 0), rolled)


def part(ref, index):
    return ref[index * FOLDS : (index + 1) * FOLDS, :]


def point_totals(value, masks):
    before = value
    after = value
    for i, step in enumerate(STEPS):
        before = before + part(masks, i) * shifted(before, step)
        after = after + part(masks, len(STEPS) + i) * shifted(after, -step)
    return before + (after - value)


def setup_kernel(owners, jac_pt, point_ref, damping, camera_ref, right_side, camera_damping,
                 preconditioner, keep, inverse, masks, folded, lane, slot, own):
    width = right_side.shape[1]
    own_arrays(right_side[...], camera_damping[...], preconditioner[...], keep[...], own)
    camera = fold(camera_ref, 0)
    shift = lax.rem(lax.div(camera, width) - lax.axis_index("cam") + owners, owners)
    block = jnp.where(shift == 1, 1, jnp.where(shift == owners - 1, 2, 3))
    block = jnp.where(shift == 0, 0, block)
    inner = lax.rem(camera, width)
    tile = lax.div(inner, LANES)
    lane[...] = lax.div(tile, 2) * LANES + lax.rem(inner, LANES)
    slot[...] = lax.rem(tile, 2) * BLOCKS + block

    point = fold(point_ref, 0)
    for i, step in enumerate(STEPS + tuple(-step for step in STEPS)):
        same = jnp.where(shifted(point, step) == point, 1.0, 0.0)
        masks[i * FOLDS : (i + 1) * FOLDS, :] = same
    rows = [fold(jac_pt, r) for r in range(6)]
    for r in range(6):
        folded[r * FOLDS : (r + 1) * FOLDS, :] = rows[r]
    pairs = [(0, 0), (0, 1), (0, 2), (1, 1), (1, 2), (2, 2)]
    xx, xy, xz, yy, yz, zz = (
        point_totals(rows[a] * rows[b] + rows[3 + a] * rows[3 + b], masks) for a, b in pairs
    )

    tiles = damping.shape[1] // LANES
    table = jnp.concatenate(
        [damping[k : k + 1, t * LANES : (t + 1) * LANES] for k in range(3) for t in range(tiles)],
        axis=0,
    )
    high = table.astype(BF16)
    rest = table - high.astype(F32)
    mid = rest.astype(BF16)
    low = (rest - mid.astype(F32)).astype(BF16)
    damp = [[], [], []]
    for i in range(FOLDS):
        spot = point[i : i + 1]
        hot = short_one_hot(lax.rem(spot, LANES), LANES)
        mask = one_hot(lax.div(spot, LANES), tiles)
        picked = sum(jnp.dot(piece, hot, preferred_element_type=F32) for piece in (high, mid, low))
        for k in range(3):
            damp[k].append(lane_sums(picked[k * tiles : (k + 1) * tiles] * mask))
    damp = [jnp.concatenate(rows_of, axis=0) for rows_of in damp]
    xx, yy, zz = xx + damp[0], yy + damp[1], zz + damp[2]
    cof_xx = yy * zz - yz * yz
    cof_xy = xz * yz - xy * zz
    cof_xz = xy * yz - xz * yy
    cof_yy = xx * zz - xz * xz
    cof_yz = xy * xz - xx * yz
    cof_zz = xx * yy - xy * xy
    det = xx * cof_xx + xy * cof_xy + xz * cof_xz
    for r, cof in enumerate((cof_xx, cof_xy, cof_xz, cof_yy, cof_yz, cof_zz)):
        inverse[r * FOLDS : (r + 1) * FOLDS, :] = cof / det


def lane_sums(value):
    return jnp.sum(value, axis=0, keepdims=True)


def schur(vector, send, jac_cam, folded, lane, slot, masks, inverse, hot, error):
    params = jac_cam.shape[0] // 2
    slots = 2 * BLOCKS
    half = hot.shape[0] // LANES
    rows = params * slots
    table = vector.reshape(params, half, slots, LANES)
    table = jnp.concatenate([table[:, h].reshape(rows, LANES) for h in range(half)], axis=1)
    high = table.astype(BF16)
    low = (table - high.astype(F32)).astype(BF16)
    table = jnp.concatenate([high, low], axis=0)

    for i in range(FOLDS):
        span = slice(i * CHUNK, (i + 1) * CHUNK)
        spot = short_one_hot(lane[i : i + 1, :], half * LANES)
        hot[:, span] = spot
        got = jnp.dot(table, spot, preferred_element_type=F32)
        got = got[:rows] + got[rows:]
        mask = one_hot(slot[i : i + 1, :], slots)
        for r in range(2):
            total = jnp.zeros((slots, CHUNK), F32)
            for a in range(params):
                jac = jac_cam[r * params + a : r * params + a + 1, span]
                total = total + jac * got[a * slots : (a + 1) * slots]
            error[r * FOLDS + i : r * FOLDS + i + 1, :] = lane_sums(total * mask)

    e0, e1 = part(error, 0), part(error, 1)
    jp = [part(folded, r) for r in range(6)]
    inv = [part(inverse, r) for r in range(6)]
    y0, y1, y2 = (point_totals(jp[k] * e0 + jp[3 + k] * e1, masks) for k in range(3))
    z = (
        inv[0] * y0 + inv[1] * y1 + inv[2] * y2,
        inv[1] * y0 + inv[3] * y1 + inv[4] * y2,
        inv[2] * y0 + inv[4] * y1 + inv[5] * y2,
    )
    left0 = e0 - (jp[0] * z[0] + jp[1] * z[1] + jp[2] * z[2])
    left1 = e1 - (jp[3] * z[0] + jp[4] * z[1] + jp[5] * z[2])
    energy = e0 * left0 + e1 * left1

    total = jnp.zeros((2 * rows, half * LANES), F32)
    for i in range(FOLDS):
        span = slice(i * CHUNK, (i + 1) * CHUNK)
        mask = one_hot(slot[i : i + 1, :], slots)
        first, second = mask * left0[i : i + 1], mask * left1[i : i + 1]
        highs, lows = [], []
        for a in range(params):
            value = jac_cam[a : a + 1, span] * first
            value = value + jac_cam[params + a : params + a + 1, span] * second
            near = value.astype(BF16)
            highs.append(near)
            lows.append((value - near.astype(F32)).astype(BF16))
        both = jnp.concatenate(highs + lows, axis=0)
        total = total + lax.dot_general(
            both, hot[:, span], (((1,), (1,)), ((), ())), preferred_element_type=F32
        )
    total = total[:rows] + total[rows:]
    for a in range(params):
        for h in range(half):
            start = (a * half + h) * slots
            send[start : start + slots, :] = total[
                a * slots : (a + 1) * slots, h * LANES : (h + 1) * LANES
            ]
    return lane_sums(sum(energy[:, t * LANES : (t + 1) * LANES] for t in range(CHUNK // LANES)))


RIGHT, DAMPING, WEIGHTS, PULL, UNWEIGH = range(5)


def own_part(own, which):
    per = own.shape[0] // 5
    return own[which * per : (which + 1) * per, :]


def own_arrays(right, damping, precond, keep, own):
    params, width = right.shape
    tiles = width // LANES
    weights = precond * keep
    parts = (right, damping, weights, weights * damping * weights * right, keep / precond)
    for t in range(tiles):
        lanes = slice(t * LANES, (t + 1) * LANES)
        for which, value in enumerate(parts):
            place = pl.ds(which * params * tiles + t, params, stride=tiles)
            own[place, :] = value[:, lanes]


def send_scalars(send, data_rows, rows):
    rest = send.shape[0] - data_rows
    send[data_rows:, :] = jnp.zeros((rest, LANES), F32)
    for index, row in enumerate(rows):
        at = data_rows + index * BLOCKS
        send[at : at + 1, :] = row


def scalar(ref, row):
    return jnp.sum(ref[row : row + 1, :], axis=1, keepdims=True)


def first_kernel(share, mine, after, before, across, keep, own, jac_cam, folded, lane, slot,
                 masks, inverse, send, start, hot, error):
    params, width = mine.shape
    tiles = width // LANES
    for block, ref in enumerate((mine, after, before, across)):
        value = ref[...] * keep[block : block + 1, :]
        for t in range(tiles):
            place = pl.ds(t * BLOCKS + block, params, stride=tiles * BLOCKS)
            start[place, :] = value[:, t * LANES : (t + 1) * LANES]
    energy = schur(start[...], send, jac_cam, folded, lane, slot, masks, inverse, hot, error)
    vector = start[pl.ds(0, params * tiles, stride=BLOCKS), :]
    energy = energy + share * lane_sums(own_part(own, DAMPING) * vector * vector)
    gamma = share * lane_sums(own_part(own, RIGHT) * vector)
    send_scalars(send, start.shape[0], (energy, gamma))


def second_kernel(share, received, start, own, jac_cam, folded, lane, slot, masks, inverse,
                  send, step, hot, error):
    data_rows = start.shape[0]
    per = data_rows // BLOCKS
    alpha = scalar(received, data_rows + BLOCKS) / scalar(received, data_rows)
    step[...] = start[...] - alpha * received[0:data_rows, :]
    energy = schur(step[...], send, jac_cam, folded, lane, slot, masks, inverse, hot, error)
    vector = step[pl.ds(0, per, stride=BLOCKS), :]
    change = received[pl.ds(0, per, stride=BLOCKS), :]
    residual = own_part(own, UNWEIGH) * vector
    energy = energy + share * lane_sums(own_part(own, DAMPING) * vector * vector)
    fresh = share * lane_sums(residual * vector)
    cross = share * lane_sums(residual * change)
    send_scalars(send, data_rows, (energy, fresh, cross))


def last_kernel(first, second, start, step, own, solution, residual):
    params, width = solution.shape
    tiles = width // LANES
    per = params * tiles
    data_rows = per * BLOCKS
    curve, gamma = scalar(first, data_rows), scalar(first, data_rows + BLOCKS)
    energy, fresh, cross = (scalar(second, per + i) for i in range(3))
    alpha = gamma / curve
    beta = fresh / gamma
    alpha_next = fresh / (energy + 2.0 * beta * cross + beta * beta * curve)
    for t in range(tiles):
        spread = pl.ds(t * BLOCKS, params, stride=tiles * BLOCKS)
        begin, vector, change = start[spread, :], step[spread, :], first[spread, :]
        terms = second[pl.ds(t, params, stride=tiles), :]
        damping, unweigh = (
            own[pl.ds(which * per + t, params, stride=tiles), :] for which in (DAMPING, UNWEIGH)
        )
        direction = vector + beta * begin
        image = jnp.where(unweigh > 0.0, damping * vector + terms, 0.0)
        image = image + beta * (unweigh * change)
        lanes = slice(t * LANES, (t + 1) * LANES)
        solution[:, lanes] = alpha * begin + alpha_next * direction
        residual[:, lanes] = unweigh * vector - alpha_next * image


def chunk_sum(received):
    total = received[0:8, :]
    for at in range(8, received.shape[0], 8):
        total = total + received[at : at + 8, :]
    return total[0:BLOCKS] + total[BLOCKS:]


def spread_kernel(received, own, send):
    total = chunk_sum(received)
    per = own.shape[0] // 5
    at = jnp.minimum(lax.axis_index("pts"), per - 1)
    rows = [own[pl.ds(which * per + at, 1), :] for which in (WEIGHTS, PULL)]
    total = jnp.concatenate([total, *rows, jnp.zeros((2, LANES), F32)], axis=0)
    for at in range(0, send.shape[0], 8):
        send[at : at + 8, :] = total


def combine_kernel(per, received, send):
    owners = received.shape[0] // 8
    me = lax.axis_index("cam")

    def row(owner, at):
        spot = lax.rem(owner + 2 * owners, owners) * 8 + at
        return received[pl.ds(spot, 1), :]

    def block_change(owner):
        terms = (row(owner, 0) + row(owner - 1, 1)) + (
            row(owner + 1, 2) + row(owner + owners // 2, 3)
        )
        return row(owner, BLOCKS + 1) + row(owner, BLOCKS) * terms

    joined = [block_change(me + shift) for shift in (0, 1, -1, owners // 2)]
    joined = jnp.concatenate(joined, axis=0)
    total = received[0:8, :]
    for owner in range(1, owners):
        total = total + received[owner * 8 : (owner + 1) * 8, :]
    joined = jnp.where(lax.axis_index("pts") >= per, total[0:BLOCKS], joined)
    joined = jnp.concatenate([joined, joined], axis=0)
    for at in range(0, send.shape[0], 8):
        send[at : at + 8, :] = joined


def spread_own_kernel(per, received, send):
    total = chunk_sum(received)
    owners = send.shape[0]
    scalars = jnp.broadcast_to(total[0:1], send.shape)
    chunk = lax.axis_index("pts")
    send[...] = jnp.where(chunk >= per, scalars, 0.0)

    @pl.when(chunk < per)
    def _():
        for block, shift in enumerate((0, 1, -1, owners // 2)):
            spot = lax.rem(lax.axis_index("cam") + shift + owners, owners)
            send[pl.ds(spot, 1), :] = total[block : block + 1]


def combine_own_kernel(received, send):
    total = received[0:8, :]
    for at in range(8, received.shape[0], 8):
        total = total + received[at : at + 8, :]
    send[...] = jnp.broadcast_to(lane_sums(total), send.shape)


def call(kernel, outs, *args, scratch=(), name=None):
    single = not isinstance(outs, list)
    return pl.pallas_call(
        kernel,
        out_shape=outs,
        in_specs=[VMEM] * len(args),
        out_specs=VMEM if single else [VMEM] * len(outs),
        scratch_shapes=list(scratch),
        compiler_params=PARAMS,
        name=name,
    )(*args)


def swap(value, axis, size):
    rows = value.shape[0] // size
    value = value.reshape(size, rows, LANES)
    return lax.all_to_all(value, axis, 0, 0).reshape(size * rows, LANES)


def on_device(right_side, camera_damping, preconditioner, jac_cam, jac_pt, camera_index,
              point_index, point_damping, anchors):
    params, width = right_side.shape
    owners, rows = lax.axis_size("cam"), lax.axis_size("pts")
    per = params * width // LANES
    count = camera_index.shape[1]
    jac_cam, jac_pt = jac_cam[0], jac_pt[0]
    share = 1.0 / rows

    mine = preconditioner * right_side
    shifts = (0, 1, -1, owners // 2)
    after, before, across = (
        lax.ppermute(mine, "cam", [(i, (i - d) % owners) for i in range(owners)])
        for d in shifts[1:]
    )
    firsts = (lax.axis_index("cam") + jnp.array(shifts) + owners) % owners * width
    ids = firsts[:, None] + jnp.arange(width, dtype=jnp.int32)[None]
    keep = 1.0 - jnp.any(anchors[:, None, None] == ids[None], axis=0).astype(F32)
    folds = [
        jax.ShapeDtypeStruct((count_of * FOLDS, CHUNK), kind)
        for count_of, kind in ((6, F32), (8, F32), (6, F32), (1, jnp.int32), (1, jnp.int32))
    ]
    inverse, masks, folded, lane, slot, own = call(
        functools.partial(setup_kernel, owners),
        folds + [jax.ShapeDtypeStruct((5 * per, LANES), F32)],
        jac_pt, point_index, point_damping[0], camera_index, right_side, camera_damping,
        preconditioner, keep[:1], name="invert",
    )
    fixed = (jac_cam, folded, lane, slot, masks, inverse)
    half = width // (2 * LANES)
    scratch = (pltpu.VMEM((half * LANES, count), BF16), pltpu.VMEM((2 * FOLDS, CHUNK), F32))
    sums = jax.ShapeDtypeStruct((rows * BLOCKS, LANES), F32)
    vector = jax.ShapeDtypeStruct((per * BLOCKS, LANES), F32)

    send, start = call(
        functools.partial(first_kernel, share), [sums, vector],
        mine, after, before, across, keep, own, *fixed, scratch=scratch, name="apply_first",
    )
    chunks = swap(send, "pts", rows)
    shape = jax.ShapeDtypeStruct((owners * 8, LANES), F32)
    chunks = call(spread_kernel, shape, chunks, own, name="spread")
    chunks = swap(chunks, "cam", owners)
    chunks = call(functools.partial(combine_kernel, per), sums, chunks, name="combine")
    first = swap(chunks, "pts", rows)

    send, step = call(
        functools.partial(second_kernel, share), [sums, vector],
        first, start, own, *fixed, scratch=scratch, name="apply_second",
    )
    chunks = swap(send, "pts", rows)
    shape = jax.ShapeDtypeStruct((owners, LANES), F32)
    chunks = call(functools.partial(spread_own_kernel, per), shape, chunks, name="spread_own")
    chunks = swap(chunks, "cam", owners)
    shape = jax.ShapeDtypeStruct((rows, LANES), F32)
    chunks = call(combine_own_kernel, shape, chunks, name="combine_own")
    second = swap(chunks, "pts", rows)
    shape = jax.ShapeDtypeStruct((params, width), F32)
    return tuple(call(last_kernel, [shape, shape], first, second, start, step, own, name="finish"))


def solution(mesh):
    return jax.shard_map(
        on_device,
        mesh=mesh,
        in_specs=(
            P(None, "cam"),
            P(None, "cam"),
            P(None, "cam"),
            P(("pts", "cam"), None, None),
            P(("pts", "cam"), None, None),
            P(("pts", "cam"), None),
            P(("pts", "cam"), None),
            P(("pts", "cam"), None, None),
            P(),
        ),
        out_specs=(P(None, "cam"), P(None, "cam")),
        check_vma=False,
    )
```

```python
import functools

import jax
import jax.numpy as jnp
from jax import lax
from jax.experimental import pallas as pl
from jax.experimental.pallas import tpu as pltpu
from jax.sharding import Mesh, PartitionSpec as P

LANES = 128
BLOCKS = 4
STEPS = (1, 2, 4, 8)
CHUNK = 512
FOLDS = 8
PAIR = 5
SCALARS = 64
F32, BF16 = jnp.float32, jnp.bfloat16
VMEM = pl.BlockSpec(memory_space=pltpu.VMEM)
PARAMS = pltpu.CompilerParams(vmem_limit_bytes=40 * 1024 * 1024)


def one_hot(row, count):
    ids = lax.broadcasted_iota(jnp.int32, (count, row.shape[1]), 0)
    return jnp.where(ids == row, 1.0, 0.0)


def cam_index():
    return lax.axis_index("z") * 2 + lax.axis_index("core")


def pts_index():
    return lax.axis_index("x") * lax.axis_size("y") + lax.axis_index("y")


def short_one_hot(row, count):
    ids = lax.broadcasted_iota(jnp.int16, (count, row.shape[1]), 0)
    return jnp.where(ids == row.astype(jnp.int16), BF16(1), BF16(0))


def fold(ref, row):
    parts = [ref[row : row + 1, i * CHUNK : (i + 1) * CHUNK] for i in range(FOLDS)]
    return jnp.concatenate(parts, axis=0)


def shifted(value, step):
    ids = lax.broadcasted_iota(jnp.int32, value.shape, 1)
    rolled = pltpu.roll(value, step % CHUNK, 1)
    if step > 0:
        return jnp.where(ids < step, pltpu.roll(rolled, 1, 0), rolled)
    return jnp.where(ids >= CHUNK + step, pltpu.roll(rolled, FOLDS - 1, 0), rolled)


def part(ref, index):
    return ref[index * FOLDS : (index + 1) * FOLDS, :]


def point_totals(value, masks):
    before = value
    after = value
    for i, step in enumerate(STEPS):
        before = before + part(masks, i) * shifted(before, step)
        after = after + part(masks, len(STEPS) + i) * shifted(after, -step)
    return before + (after - value)


def setup_kernel(owners, jac_pt, point_ref, damping, camera_ref, right_side, camera_damping,
                 preconditioner, keep, inverse, masks, folded, lane, slot, own):
    width = right_side.shape[1]
    own_arrays(right_side[...], camera_damping[...], preconditioner[...], keep[...], own)
    camera = fold(camera_ref, 0)
    shift = lax.rem(lax.div(camera, width) - cam_index() + owners, owners)
    block = jnp.where(shift == 1, 1, jnp.where(shift == owners - 1, 2, 3))
    block = jnp.where(shift == 0, 0, block)
    inner = lax.rem(camera, width)
    tile = lax.div(inner, LANES)
    lane[...] = lax.div(tile, 2) * LANES + lax.rem(inner, LANES)
    slot[...] = lax.rem(tile, 2) * BLOCKS + block

    point = fold(point_ref, 0)
    for i, step in enumerate(STEPS + tuple(-step for step in STEPS)):
        same = jnp.where(shifted(point, step) == point, 1.0, 0.0)
        masks[i * FOLDS : (i + 1) * FOLDS, :] = same
    rows = [fold(jac_pt, r) for r in range(6)]
    for r in range(6):
        folded[r * FOLDS : (r + 1) * FOLDS, :] = rows[r]
    pairs = [(0, 0), (0, 1), (0, 2), (1, 1), (1, 2), (2, 2)]
    xx, xy, xz, yy, yz, zz = (
        point_totals(rows[a] * rows[b] + rows[3 + a] * rows[3 + b], masks) for a, b in pairs
    )

    tiles = damping.shape[1] // LANES
    table = jnp.concatenate(
        [damping[k : k + 1, t * LANES : (t + 1) * LANES] for k in range(3) for t in range(tiles)],
        axis=0,
    )
    high = table.astype(BF16)
    rest = table - high.astype(F32)
    mid = rest.astype(BF16)
    low = (rest - mid.astype(F32)).astype(BF16)
    damp = [[], [], []]
    for i in range(FOLDS):
        spot = point[i : i + 1]
        hot = short_one_hot(lax.rem(spot, LANES), LANES)
        mask = one_hot(lax.div(spot, LANES), tiles)
        picked = sum(jnp.dot(piece, hot, preferred_element_type=F32) for piece in (high, mid, low))
        for k in range(3):
            damp[k].append(lane_sums(picked[k * tiles : (k + 1) * tiles] * mask))
    damp = [jnp.concatenate(rows_of, axis=0) for rows_of in damp]
    xx, yy, zz = xx + damp[0], yy + damp[1], zz + damp[2]
    cof_xx = yy * zz - yz * yz
    cof_xy = xz * yz - xy * zz
    cof_xz = xy * yz - xz * yy
    cof_yy = xx * zz - xz * xz
    cof_yz = xy * xz - xx * yz
    cof_zz = xx * yy - xy * xy
    det = xx * cof_xx + xy * cof_xy + xz * cof_xz
    for r, cof in enumerate((cof_xx, cof_xy, cof_xz, cof_yy, cof_yz, cof_zz)):
        inverse[r * FOLDS : (r + 1) * FOLDS, :] = cof / det


def lane_sums(value):
    return jnp.sum(value, axis=0, keepdims=True)


def schur(vector, send, jac_cam, folded, lane, slot, masks, inverse, hot, error):
    params = jac_cam.shape[0] // 2
    slots = 2 * BLOCKS
    half = hot.shape[0] // LANES
    rows = params * slots
    table = vector.reshape(params, half, slots, LANES)
    table = jnp.concatenate([table[:, h].reshape(rows, LANES) for h in range(half)], axis=1)
    high = table.astype(BF16)
    low = (table - high.astype(F32)).astype(BF16)
    table = jnp.concatenate([high, low], axis=0)

    for i in range(FOLDS):
        span = slice(i * CHUNK, (i + 1) * CHUNK)
        spot = short_one_hot(lane[i : i + 1, :], half * LANES)
        hot[:, span] = spot
        got = jnp.dot(table, spot, preferred_element_type=F32)
        got = got[:rows] + got[rows:]
        mask = one_hot(slot[i : i + 1, :], slots)
        for r in range(2):
            total = jnp.zeros((slots, CHUNK), F32)
            for a in range(params):
                jac = jac_cam[r * params + a : r * params + a + 1, span]
                total = total + jac * got[a * slots : (a + 1) * slots]
            error[r * FOLDS + i : r * FOLDS + i + 1, :] = lane_sums(total * mask)

    e0, e1 = part(error, 0), part(error, 1)
    jp = [part(folded, r) for r in range(6)]
    inv = [part(inverse, r) for r in range(6)]
    y0, y1, y2 = (point_totals(jp[k] * e0 + jp[3 + k] * e1, masks) for k in range(3))
    z = (
        inv[0] * y0 + inv[1] * y1 + inv[2] * y2,
        inv[1] * y0 + inv[3] * y1 + inv[4] * y2,
        inv[2] * y0 + inv[4] * y1 + inv[5] * y2,
    )
    left0 = e0 - (jp[0] * z[0] + jp[1] * z[1] + jp[2] * z[2])
    left1 = e1 - (jp[3] * z[0] + jp[4] * z[1] + jp[5] * z[2])
    energy = e0 * left0 + e1 * left1

    total = jnp.zeros((2 * rows, half * LANES), F32)
    for i in range(FOLDS):
        span = slice(i * CHUNK, (i + 1) * CHUNK)
        mask = one_hot(slot[i : i + 1, :], slots)
        first, second = mask * left0[i : i + 1], mask * left1[i : i + 1]
        highs, lows = [], []
        for a in range(params):
            value = jac_cam[a : a + 1, span] * first
            value = value + jac_cam[params + a : params + a + 1, span] * second
            near = value.astype(BF16)
            highs.append(near)
            lows.append((value - near.astype(F32)).astype(BF16))
        both = jnp.concatenate(highs + lows, axis=0)
        total = total + lax.dot_general(
            both, hot[:, span], (((1,), (1,)), ((), ())), preferred_element_type=F32
        )
    total = total[:rows] + total[rows:]
    for a in range(params):
        for h in range(half):
            start = (a * half + h) * slots
            send[start : start + slots, :] = total[
                a * slots : (a + 1) * slots, h * LANES : (h + 1) * LANES
            ]
    return lane_sums(sum(energy[:, t * LANES : (t + 1) * LANES] for t in range(CHUNK // LANES)))


RIGHT, DAMPING, WEIGHTS, PULL, UNWEIGH = range(5)


def own_part(own, which):
    per = own.shape[0] // 5
    return own[which * per : (which + 1) * per, :]


def own_arrays(right, damping, precond, keep, own):
    params, width = right.shape
    tiles = width // LANES
    weights = precond * keep
    parts = (right, damping, weights, weights * damping * weights * right, keep / precond)
    for t in range(tiles):
        lanes = slice(t * LANES, (t + 1) * LANES)
        for which, value in enumerate(parts):
            place = pl.ds(which * params * tiles + t, params, stride=tiles)
            own[place, :] = value[:, lanes]


def send_scalars(send, data_rows, rows):
    rest = send.shape[0] - data_rows
    send[data_rows:, :] = jnp.zeros((rest, LANES), F32)
    for index, row in enumerate(rows):
        at = data_rows + index * BLOCKS
        send[at : at + 1, :] = row


def scalar(ref, row):
    return jnp.sum(ref[row : row + 1, :], axis=1, keepdims=True)


def first_kernel(share, mine, after, before, across, keep, own, jac_cam, folded, lane, slot,
                 masks, inverse, send, start, hot, error):
    params, width = mine.shape
    tiles = width // LANES
    for block, ref in enumerate((mine, after, before, across)):
        value = ref[...] * keep[block : block + 1, :]
        for t in range(tiles):
            place = pl.ds(t * BLOCKS + block, params, stride=tiles * BLOCKS)
            start[place, :] = value[:, t * LANES : (t + 1) * LANES]
    energy = schur(start[...], send, jac_cam, folded, lane, slot, masks, inverse, hot, error)
    vector = start[pl.ds(0, params * tiles, stride=BLOCKS), :]
    energy = energy + share * lane_sums(own_part(own, DAMPING) * vector * vector)
    gamma = share * lane_sums(own_part(own, RIGHT) * vector)
    send_scalars(send, start.shape[0], (energy, gamma))


def lane_ids(rows=1):
    return lax.broadcasted_iota(jnp.int32, (rows, LANES), 1)


def second_kernel(share, received, start, own, jac_cam, folded, lane, slot, masks, inverse,
                  send, step, sums, hot, error):
    data_rows = start.shape[0]
    per = data_rows // BLOCKS
    alpha = scalar(received, data_rows + BLOCKS) / scalar(received, data_rows)
    step[...] = start[...] - alpha * received[0:data_rows, :]
    energy = schur(step[...], sums, jac_cam, folded, lane, slot, masks, inverse, hot, error)
    vector = step[pl.ds(0, per, stride=BLOCKS), :]
    change = received[pl.ds(0, per, stride=BLOCKS), :]
    residual = own_part(own, UNWEIGH) * vector
    energy = energy + share * lane_sums(own_part(own, DAMPING) * vector * vector)
    fresh = share * lane_sums(residual * vector)
    cross = share * lane_sums(residual * change)
    ids = lane_ids(BLOCKS)
    extra = jnp.zeros((BLOCKS, LANES), F32)
    for index, row in enumerate((energy, fresh, cross)):
        extra = jnp.where(ids == SCALARS + index, jnp.sum(row, axis=1, keepdims=True), extra)
    extra = jnp.where(lax.broadcasted_iota(jnp.int32, extra.shape, 0) == 0, extra, 0.0)
    for chunk in range(16):
        base = chunk * 3 * BLOCKS
        send[base : base + 2 * BLOCKS, :] = sums[chunk * 2 * BLOCKS : (chunk + 1) * 2 * BLOCKS, :]
        third = (32 + chunk // 4) * BLOCKS
        third = sums[third : third + BLOCKS, :]
        if chunk % 4:
            third = pltpu.roll(third, LANES - 32 * (chunk % 4), 1)
        send[base + 2 * BLOCKS : base + 3 * BLOCKS, :] = jnp.where(ids < 32, third, extra)


def pair_kernel(received, send):
    rows = 3 * BLOCKS
    first = received[0:rows, :]
    second = received[rows : 2 * rows, :]
    for source in range(2, received.shape[0] // rows, 2):
        first = first + received[source * rows : (source + 1) * rows, :]
        second = second + received[(source + 1) * rows : (source + 2) * rows, :]

    def rows_of(value, block):
        return [value[r * BLOCKS + block : r * BLOCKS + block + 1] for r in range(3)]

    zero = [jnp.zeros((1, LANES), F32)] * 3
    ids = lane_ids()
    scalars = first[2 * BLOCKS : 2 * BLOCKS + 1] + second[2 * BLOCKS : 2 * BLOCKS + 1]
    own_even = [a + b for a, b in zip(rows_of(first, 0), rows_of(second, 2))]
    own_odd = [a + b for a, b in zip(rows_of(first, 1), rows_of(second, 0))]
    pairs = (
        (0, own_even, own_odd),
        (1, rows_of(second, 1), zero),
        (-1, zero, rows_of(first, 2)),
        (4, rows_of(first, 3), rows_of(second, 3)),
    )

    def joined(even, odd):
        mixed = jnp.where(ids < 32, even[2], pltpu.roll(odd[2], 32, 1))
        mixed = jnp.where(ids < SCALARS, mixed, scalars)
        return jnp.concatenate(even[:2] + odd[:2] + [mixed], axis=0)

    size = lax.axis_size("z")
    columns = send.shape[0] // (size * PAIR)
    nothing = joined(zero, zero)
    for spot in range(columns * size):
        send[spot * PAIR : (spot + 1) * PAIR, :] = nothing
    for shift, even, odd in pairs:
        value = joined(even, odd)
        place = lax.rem(lax.axis_index("z") + shift + size, size)
        for x in range(columns):
            send[pl.ds((x * size + place) * PAIR, PAIR), :] = value


def pair_sum_kernel(received, send):
    total = received[0:PAIR, :]
    for source in range(1, received.shape[0] // PAIR):
        total = total + received[source * PAIR : (source + 1) * PAIR, :]
    for spot in range(send.shape[0] // PAIR):
        send[spot * PAIR : (spot + 1) * PAIR, :] = total


def last_kernel(first, second, start, step, own, solution, residual, sums):
    params, width = solution.shape
    tiles = width // LANES
    per = params * tiles
    data_rows = per * BLOCKS
    odd = lax.axis_index("core") == 1
    ids = lane_ids()
    for chunk in range(16):
        base = chunk * PAIR
        even_rows, odd_rows = second[base : base + 2, :], second[base + 2 : base + 4, :]
        sums[2 * chunk : 2 * chunk + 2, :] = jnp.where(odd, odd_rows, even_rows)
    for q in range(4):
        third = jnp.zeros((1, LANES), F32)
        for i in range(4):
            row = second[(4 * q + i) * PAIR + 4 : (4 * q + i) * PAIR + 5, :]
            even_row = pltpu.roll(row, 32 * i, 1) if i else row
            odd_row = pltpu.roll(row, (32 * i - 32) % LANES, 1) if i != 1 else row
            place = jnp.logical_and(ids >= 32 * i, ids < 32 * (i + 1))
            third = jnp.where(place, jnp.where(odd, odd_row, even_row), third)
        sums[32 + q : 33 + q, :] = third

    curve, gamma = scalar(first, data_rows), scalar(first, data_rows + BLOCKS)
    mixed = second[PAIR - 1 : PAIR, :]
    energy, fresh, cross = (
        jnp.sum(jnp.where(ids == SCALARS + i, mixed, 0.0), axis=1, keepdims=True) for i in range(3)
    )
    alpha = gamma / curve
    beta = fresh / gamma
    alpha_next = fresh / (energy + 2.0 * beta * cross + beta * beta * curve)
    for t in range(tiles):
        spread = pl.ds(t * BLOCKS, params, stride=tiles * BLOCKS)
        begin, vector, change = start[spread, :], step[spread, :], first[spread, :]
        terms = sums[pl.ds(t, params, stride=tiles), :]
        damping, unweigh = (
            own[pl.ds(which * per + t, params, stride=tiles), :] for which in (DAMPING, UNWEIGH)
        )
        direction = vector + beta * begin
        image = jnp.where(unweigh > 0.0, damping * vector + terms, 0.0)
        image = image + beta * (unweigh * change)
        lanes = slice(t * LANES, (t + 1) * LANES)
        solution[:, lanes] = alpha * begin + alpha_next * direction
        residual[:, lanes] = unweigh * vector - alpha_next * image


def chunk_sum(received):
    total = received[0:8, :]
    for at in range(8, received.shape[0], 8):
        total = total + received[at : at + 8, :]
    return total[0:BLOCKS] + total[BLOCKS:]


def spread_kernel(received, own, send):
    total = chunk_sum(received)
    per = own.shape[0] // 5
    at = jnp.minimum(pts_index(), per - 1)
    rows = [own[pl.ds(which * per + at, 1), :] for which in (WEIGHTS, PULL)]
    total = jnp.concatenate([total, *rows, jnp.zeros((2, LANES), F32)], axis=0)
    for at in range(0, send.shape[0], 8):
        send[at : at + 8, :] = total


def combine_kernel(per, received, send):
    owners = received.shape[0] // 8
    me = cam_index()

    def row(owner, at):
        spot = lax.rem(owner + 2 * owners, owners) * 8 + at
        return received[pl.ds(spot, 1), :]

    def block_change(owner):
        terms = (row(owner, 0) + row(owner - 1, 1)) + (
            row(owner + 1, 2) + row(owner + owners // 2, 3)
        )
        return row(owner, BLOCKS + 1) + row(owner, BLOCKS) * terms

    joined = [block_change(me + shift) for shift in (0, 1, -1, owners // 2)]
    joined = jnp.concatenate(joined, axis=0)
    total = received[0:8, :]
    for owner in range(1, owners):
        total = total + received[owner * 8 : (owner + 1) * 8, :]
    joined = jnp.where(pts_index() >= per, total[0:BLOCKS], joined)
    joined = jnp.concatenate([joined, joined], axis=0)
    for at in range(0, send.shape[0], 8):
        send[at : at + 8, :] = joined


def call(kernel, outs, *args, scratch=(), name=None):
    single = not isinstance(outs, list)
    return pl.pallas_call(
        kernel,
        out_shape=outs,
        in_specs=[VMEM] * len(args),
        out_specs=VMEM if single else [VMEM] * len(outs),
        scratch_shapes=list(scratch),
        compiler_params=PARAMS,
        name=name,
    )(*args)


def swap(value, axes, tile=BLOCKS):
    size = lax.axis_size(axes)
    rows = value.shape[0] // size
    chunks = value.reshape(size, rows // tile, tile, LANES)
    return lax.all_to_all(chunks, axes, 0, 0).reshape(value.shape)


def on_device(right_side, camera_damping, preconditioner, jac_cam, jac_pt, camera_index,
              point_index, point_damping, anchors):
    params, width = right_side.shape
    pts, cam, line, plane = ("x", "y"), ("z", "core"), ("y", "core"), ("x", "z")
    owners, rows = lax.axis_size(cam), lax.axis_size(pts)
    per = params * width // LANES
    count = camera_index.shape[1]
    jac_cam, jac_pt = jac_cam[0], jac_pt[0]
    share = 1.0 / rows

    mine = preconditioner * right_side
    shifts = (0, 1, -1, owners // 2)
    after, before, across = (
        lax.ppermute(mine, cam, [(i, (i - d) % owners) for i in range(owners)])
        for d in shifts[1:]
    )
    firsts = (cam_index() + jnp.array(shifts) + owners) % owners * width
    ids = firsts[:, None] + jnp.arange(width, dtype=jnp.int32)[None]
    keep = 1.0 - jnp.any(anchors[:, None, None] == ids[None], axis=0).astype(F32)
    folds = [
        jax.ShapeDtypeStruct((count_of * FOLDS, CHUNK), kind)
        for count_of, kind in ((6, F32), (8, F32), (6, F32), (1, jnp.int32), (1, jnp.int32))
    ]
    inverse, masks, folded, lane, slot, own = call(
        functools.partial(setup_kernel, owners),
        folds + [jax.ShapeDtypeStruct((5 * per, LANES), F32)],
        jac_pt, point_index, point_damping[0], camera_index, right_side, camera_damping,
        preconditioner, keep[:1], name="invert",
    )
    fixed = (jac_cam, folded, lane, slot, masks, inverse)
    half = width // (2 * LANES)
    scratch = (pltpu.VMEM((half * LANES, count), BF16), pltpu.VMEM((2 * FOLDS, CHUNK), F32))
    sums = jax.ShapeDtypeStruct((rows * BLOCKS, LANES), F32)
    vector = jax.ShapeDtypeStruct((per * BLOCKS, LANES), F32)

    send, start = call(
        functools.partial(first_kernel, share), [sums, vector],
        mine, after, before, across, keep, own, *fixed, scratch=scratch, name="apply_first",
    )
    chunks = swap(send, pts)
    shape = jax.ShapeDtypeStruct((owners * 8, LANES), F32)
    chunks = call(spread_kernel, shape, chunks, own, name="spread")
    chunks = swap(chunks, cam)
    chunks = call(functools.partial(combine_kernel, per), sums, chunks, name="combine")
    first = swap(chunks, pts)

    thirds = jax.ShapeDtypeStruct((16 * 3 * BLOCKS, LANES), F32)
    send, step = call(
        functools.partial(second_kernel, share), [thirds, vector], first, start, own, *fixed,
        scratch=(pltpu.VMEM(vector.shape, F32), *scratch), name="apply_second",
    )
    chunks = swap(send, line)
    shape = jax.ShapeDtypeStruct((lax.axis_size(plane) * PAIR, LANES), F32)
    chunks = call(pair_kernel, shape, chunks, name="pair")
    chunks = swap(chunks, plane, 1)
    shape = jax.ShapeDtypeStruct((lax.axis_size(line) * PAIR, LANES), F32)
    chunks = call(pair_sum_kernel, shape, chunks, name="pair_sum")
    second = swap(chunks, line, 1)
    shape = jax.ShapeDtypeStruct((params, width), F32)
    return tuple(
        call(
            last_kernel, [shape, shape], first, second, start, step, own,
            scratch=[pltpu.VMEM((per, LANES), F32)], name="finish",
        )
    )


def solution(mesh):
    cores = 2
    high = mesh.shape["cam"] // cores
    side = int(mesh.shape["pts"] ** 0.5)
    grid = mesh.devices.reshape(side, mesh.shape["pts"] // side, high, cores)
    mesh = Mesh(grid, ("x", "y", "z", "core"))
    cam, whole = ("z", "core"), ("x", "y", "z", "core")
    return jax.shard_map(
        on_device,
        mesh=mesh,
        in_specs=(
            P(None, cam),
            P(None, cam),
            P(None, cam),
            P(whole, None, None),
            P(whole, None, None),
            P(whole, None),
            P(whole, None),
            P(whole, None, None),
            P(),
        ),
        out_specs=(P(None, cam), P(None, cam)),
        check_vma=False,
    )
```

```python
import functools

import jax
import jax.numpy as jnp
from jax import lax
from jax.experimental import pallas as pl
from jax.experimental.pallas import tpu as pltpu
from jax.sharding import Mesh, PartitionSpec as P

LANES = 128
BLOCKS = 4
STEPS = (1, 2, 4, 8)
CHUNK = 512
FOLDS = 8
QUARTER = 32
LINE = 10
PAIR = 5
SCALARS = 64
F32, BF16 = jnp.float32, jnp.bfloat16
VMEM = pl.BlockSpec(memory_space=pltpu.VMEM)
PARAMS = pltpu.CompilerParams(vmem_limit_bytes=40 * 1024 * 1024)


def one_hot(row, count):
    ids = lax.broadcasted_iota(jnp.int32, (count, row.shape[1]), 0)
    return jnp.where(ids == row, 1.0, 0.0)


def cam_index():
    return lax.axis_index("z") * 2 + lax.axis_index("core")


def pts_index():
    return lax.axis_index("x") * lax.axis_size("y") + lax.axis_index("y")


def short_one_hot(row, count):
    ids = lax.broadcasted_iota(jnp.int16, (count, row.shape[1]), 0)
    return jnp.where(ids == row.astype(jnp.int16), BF16(1), BF16(0))


def fold(ref, row):
    parts = [ref[row : row + 1, i * CHUNK : (i + 1) * CHUNK] for i in range(FOLDS)]
    return jnp.concatenate(parts, axis=0)


def shifted(value, step):
    ids = lax.broadcasted_iota(jnp.int32, value.shape, 1)
    rolled = pltpu.roll(value, step % CHUNK, 1)
    if step > 0:
        return jnp.where(ids < step, pltpu.roll(rolled, 1, 0), rolled)
    return jnp.where(ids >= CHUNK + step, pltpu.roll(rolled, FOLDS - 1, 0), rolled)


def part(ref, index):
    return ref[index * FOLDS : (index + 1) * FOLDS, :]


def point_totals(value, masks):
    before = value
    after = value
    for i, step in enumerate(STEPS):
        before = before + part(masks, i) * shifted(before, step)
        after = after + part(masks, len(STEPS) + i) * shifted(after, -step)
    return before + (after - value)


def setup_kernel(owners, jac_pt, point_ref, damping, camera_ref, right_side, camera_damping,
                 preconditioner, keep, inverse, masks, folded, lane, slot, own):
    width = right_side.shape[1]
    own_arrays(right_side[...], camera_damping[...], preconditioner[...], keep[...], own)
    camera = fold(camera_ref, 0)
    shift = lax.rem(lax.div(camera, width) - cam_index() + owners, owners)
    block = jnp.where(shift == 1, 1, jnp.where(shift == owners - 1, 2, 3))
    block = jnp.where(shift == 0, 0, block)
    inner = lax.rem(camera, width)
    tile = lax.div(inner, LANES)
    lane[...] = lax.div(tile, 2) * LANES + lax.rem(inner, LANES)
    slot[...] = lax.rem(tile, 2) * BLOCKS + block

    point = fold(point_ref, 0)
    for i, step in enumerate(STEPS + tuple(-step for step in STEPS)):
        same = jnp.where(shifted(point, step) == point, 1.0, 0.0)
        masks[i * FOLDS : (i + 1) * FOLDS, :] = same
    rows = [fold(jac_pt, r) for r in range(6)]
    for r in range(6):
        folded[r * FOLDS : (r + 1) * FOLDS, :] = rows[r]
    pairs = [(0, 0), (0, 1), (0, 2), (1, 1), (1, 2), (2, 2)]
    xx, xy, xz, yy, yz, zz = (
        point_totals(rows[a] * rows[b] + rows[3 + a] * rows[3 + b], masks) for a, b in pairs
    )

    tiles = damping.shape[1] // LANES
    table = jnp.concatenate(
        [damping[k : k + 1, t * LANES : (t + 1) * LANES] for k in range(3) for t in range(tiles)],
        axis=0,
    )
    high = table.astype(BF16)
    rest = table - high.astype(F32)
    mid = rest.astype(BF16)
    low = (rest - mid.astype(F32)).astype(BF16)
    damp = [[], [], []]
    for i in range(FOLDS):
        spot = point[i : i + 1]
        hot = short_one_hot(lax.rem(spot, LANES), LANES)
        mask = one_hot(lax.div(spot, LANES), tiles)
        picked = sum(jnp.dot(piece, hot, preferred_element_type=F32) for piece in (high, mid, low))
        for k in range(3):
            damp[k].append(lane_sums(picked[k * tiles : (k + 1) * tiles] * mask))
    damp = [jnp.concatenate(rows_of, axis=0) for rows_of in damp]
    xx, yy, zz = xx + damp[0], yy + damp[1], zz + damp[2]
    cof_xx = yy * zz - yz * yz
    cof_xy = xz * yz - xy * zz
    cof_xz = xy * yz - xz * yy
    cof_yy = xx * zz - xz * xz
    cof_yz = xy * xz - xx * yz
    cof_zz = xx * yy - xy * xy
    det = xx * cof_xx + xy * cof_xy + xz * cof_xz
    for r, cof in enumerate((cof_xx, cof_xy, cof_xz, cof_yy, cof_yz, cof_zz)):
        inverse[r * FOLDS : (r + 1) * FOLDS, :] = cof / det


def lane_sums(value):
    return jnp.sum(value, axis=0, keepdims=True)


def schur(vector, send, jac_cam, folded, lane, slot, masks, inverse, hot, error):
    params = jac_cam.shape[0] // 2
    slots = 2 * BLOCKS
    half = hot.shape[0] // LANES
    rows = params * slots
    table = vector.reshape(params, half, slots, LANES)
    table = jnp.concatenate([table[:, h].reshape(rows, LANES) for h in range(half)], axis=1)
    high = table.astype(BF16)
    low = (table - high.astype(F32)).astype(BF16)
    table = jnp.concatenate([high, low], axis=0)

    for i in range(FOLDS):
        span = slice(i * CHUNK, (i + 1) * CHUNK)
        spot = short_one_hot(lane[i : i + 1, :], half * LANES)
        hot[:, span] = spot
        got = jnp.dot(table, spot, preferred_element_type=F32)
        got = got[:rows] + got[rows:]
        mask = one_hot(slot[i : i + 1, :], slots)
        for r in range(2):
            total = jnp.zeros((slots, CHUNK), F32)
            for a in range(params):
                jac = jac_cam[r * params + a : r * params + a + 1, span]
                total = total + jac * got[a * slots : (a + 1) * slots]
            error[r * FOLDS + i : r * FOLDS + i + 1, :] = lane_sums(total * mask)

    e0, e1 = part(error, 0), part(error, 1)
    jp = [part(folded, r) for r in range(6)]
    inv = [part(inverse, r) for r in range(6)]
    y0, y1, y2 = (point_totals(jp[k] * e0 + jp[3 + k] * e1, masks) for k in range(3))
    z = (
        inv[0] * y0 + inv[1] * y1 + inv[2] * y2,
        inv[1] * y0 + inv[3] * y1 + inv[4] * y2,
        inv[2] * y0 + inv[4] * y1 + inv[5] * y2,
    )
    left0 = e0 - (jp[0] * z[0] + jp[1] * z[1] + jp[2] * z[2])
    left1 = e1 - (jp[3] * z[0] + jp[4] * z[1] + jp[5] * z[2])
    energy = e0 * left0 + e1 * left1

    total = jnp.zeros((2 * rows, half * LANES), F32)
    for i in range(FOLDS):
        span = slice(i * CHUNK, (i + 1) * CHUNK)
        mask = one_hot(slot[i : i + 1, :], slots)
        first, second = mask * left0[i : i + 1], mask * left1[i : i + 1]
        highs, lows = [], []
        for a in range(params):
            value = jac_cam[a : a + 1, span] * first
            value = value + jac_cam[params + a : params + a + 1, span] * second
            near = value.astype(BF16)
            highs.append(near)
            lows.append((value - near.astype(F32)).astype(BF16))
        both = jnp.concatenate(highs + lows, axis=0)
        total = total + lax.dot_general(
            both, hot[:, span], (((1,), (1,)), ((), ())), preferred_element_type=F32
        )
    total = total[:rows] + total[rows:]
    for a in range(params):
        for h in range(half):
            start = (a * half + h) * slots
            send[start : start + slots, :] = total[
                a * slots : (a + 1) * slots, h * LANES : (h + 1) * LANES
            ]
    return lane_sums(sum(energy[:, t * LANES : (t + 1) * LANES] for t in range(CHUNK // LANES)))


RIGHT, DAMPING, WEIGHTS, PULL, UNWEIGH = range(5)


def own_part(own, which):
    per = own.shape[0] // 5
    return own[which * per : (which + 1) * per, :]


def own_arrays(right, damping, precond, keep, own):
    params, width = right.shape
    tiles = width // LANES
    weights = precond * keep
    parts = (right, damping, weights, weights * damping * weights * right, keep / precond)
    for t in range(tiles):
        lanes = slice(t * LANES, (t + 1) * LANES)
        for which, value in enumerate(parts):
            place = pl.ds(which * params * tiles + t, params, stride=tiles)
            own[place, :] = value[:, lanes]


def send_scalars(send, data_rows, rows):
    rest = send.shape[0] - data_rows
    send[data_rows:, :] = jnp.zeros((rest, LANES), F32)
    for index, row in enumerate(rows):
        at = data_rows + index * BLOCKS
        send[at : at + 1, :] = row


def scalar(ref, row):
    return jnp.sum(ref[row : row + 1, :], axis=1, keepdims=True)


def first_kernel(share, mine, after, before, across, keep, own, jac_cam, folded, lane, slot,
                 masks, inverse, send, start, hot, error):
    params, width = mine.shape
    tiles = width // LANES
    for block, ref in enumerate((mine, after, before, across)):
        value = ref[...] * keep[block : block + 1, :]
        for t in range(tiles):
            place = pl.ds(t * BLOCKS + block, params, stride=tiles * BLOCKS)
            start[place, :] = value[:, t * LANES : (t + 1) * LANES]
    energy = schur(start[...], send, jac_cam, folded, lane, slot, masks, inverse, hot, error)
    vector = start[pl.ds(0, params * tiles, stride=BLOCKS), :]
    energy = energy + share * lane_sums(own_part(own, DAMPING) * vector * vector)
    gamma = share * lane_sums(own_part(own, RIGHT) * vector)
    send_scalars(send, start.shape[0], (energy, gamma))


def lane_ids(rows=1):
    return lax.broadcasted_iota(jnp.int32, (rows, LANES), 1)


def second_kernel(share, received, start, own, jac_cam, folded, lane, slot, masks, inverse,
                  send, step, sums, hot, error):
    data_rows = start.shape[0]
    per = data_rows // BLOCKS
    alpha = scalar(received, data_rows + BLOCKS) / scalar(received, data_rows)
    step[...] = start[...] - alpha * received[0:data_rows, :]
    energy = schur(step[...], sums, jac_cam, folded, lane, slot, masks, inverse, hot, error)
    vector = step[pl.ds(0, per, stride=BLOCKS), :]
    change = received[pl.ds(0, per, stride=BLOCKS), :]
    residual = own_part(own, UNWEIGH) * vector
    energy = energy + share * lane_sums(own_part(own, DAMPING) * vector * vector)
    fresh = share * lane_sums(residual * vector)
    cross = share * lane_sums(residual * change)
    ids = lane_ids()
    extra = jnp.zeros((1, LANES), F32)
    for index, row in enumerate((energy, fresh, cross)):
        extra = jnp.where(ids == SCALARS + index, jnp.sum(row, axis=1, keepdims=True), extra)
    for chunk in range(16):
        base = chunk * LINE
        send[base : base + 8, :] = sums[chunk * 8 : (chunk + 1) * 8, :]
        send[base + 9 : base + 10, :] = extra
    for q in range(4):
        thirds = sums[(32 + q) * BLOCKS : (33 + q) * BLOCKS, :]
        rolled = [thirds] + [pltpu.roll(thirds, QUARTER * k, 1) for k in range(1, 4)]
        for i in range(4):
            mixed = rolled[(0 - i) % 4][0:1]
            for block in range(1, BLOCKS):
                piece = rolled[(block - i) % 4][block : block + 1]
                mixed = jnp.where(ids >= QUARTER * block, piece, mixed)
            at = (4 * q + i) * LINE + 8
            send[at : at + 1, :] = mixed


def pair_kernel(received, send):
    first = received[0:LINE, :]
    second = received[LINE : 2 * LINE, :]
    for source in range(2, received.shape[0] // LINE, 2):
        first = first + received[source * LINE : (source + 1) * LINE, :]
        second = second + received[(source + 1) * LINE : (source + 2) * LINE, :]

    def rows_of(value, block):
        third = value[8:9]
        if block:
            third = pltpu.roll(third, LANES - QUARTER * block, 1)
        return [value[block : block + 1], value[BLOCKS + block : BLOCKS + block + 1], third]

    zero = [jnp.zeros((1, LANES), F32)] * 3
    ids = lane_ids()
    scalars = first[9:10] + second[9:10]
    own_even = [a + b for a, b in zip(rows_of(first, 0), rows_of(second, 2))]
    own_odd = [a + b for a, b in zip(rows_of(first, 1), rows_of(second, 0))]
    pairs = (
        (0, own_even, own_odd),
        (1, rows_of(second, 1), zero),
        (-1, zero, rows_of(first, 2)),
        (4, rows_of(first, 3), rows_of(second, 3)),
    )

    def joined(even, odd):
        mixed = jnp.where(ids < QUARTER, even[2], pltpu.roll(odd[2], QUARTER, 1))
        mixed = jnp.where(ids < SCALARS, mixed, scalars)
        return jnp.concatenate(even[:2] + odd[:2] + [mixed], axis=0)

    size = lax.axis_size("z")
    columns = send.shape[0] // (size * PAIR)
    nothing = joined(zero, zero)
    for spot in range(columns * size):
        send[spot * PAIR : (spot + 1) * PAIR, :] = nothing
    for shift, even, odd in pairs:
        value = joined(even, odd)
        place = lax.rem(lax.axis_index("z") + shift + size, size)
        for x in range(columns):
            send[pl.ds((x * size + place) * PAIR, PAIR), :] = value


def pair_sum_kernel(received, send):
    total = received[0:PAIR, :]
    for source in range(1, received.shape[0] // PAIR):
        total = total + received[source * PAIR : (source + 1) * PAIR, :]
    for spot in range(send.shape[0] // PAIR):
        send[spot * PAIR : (spot + 1) * PAIR, :] = total


def last_kernel(first, second, start, step, own, solution, residual, sums):
    params, width = solution.shape
    tiles = width // LANES
    per = params * tiles
    data_rows = per * BLOCKS
    odd = lax.axis_index("core") == 1
    ids = lane_ids()
    for chunk in range(16):
        base = chunk * PAIR
        even_rows, odd_rows = second[base : base + 2, :], second[base + 2 : base + 4, :]
        sums[2 * chunk : 2 * chunk + 2, :] = jnp.where(odd, odd_rows, even_rows)
    for q in range(4):
        third = jnp.zeros((1, LANES), F32)
        for i in range(4):
            row = second[(4 * q + i) * PAIR + 4 : (4 * q + i) * PAIR + 5, :]
            even_row = pltpu.roll(row, 32 * i, 1) if i else row
            odd_row = pltpu.roll(row, (32 * i - 32) % LANES, 1) if i != 1 else row
            place = jnp.logical_and(ids >= 32 * i, ids < 32 * (i + 1))
            third = jnp.where(place, jnp.where(odd, odd_row, even_row), third)
        sums[32 + q : 33 + q, :] = third

    curve, gamma = scalar(first, data_rows), scalar(first, data_rows + BLOCKS)
    mixed = second[PAIR - 1 : PAIR, :]
    energy, fresh, cross = (
        jnp.sum(jnp.where(ids == SCALARS + i, mixed, 0.0), axis=1, keepdims=True) for i in range(3)
    )
    alpha = gamma / curve
    beta = fresh / gamma
    alpha_next = fresh / (energy + 2.0 * beta * cross + beta * beta * curve)
    for t in range(tiles):
        spread = pl.ds(t * BLOCKS, params, stride=tiles * BLOCKS)
        begin, vector, change = start[spread, :], step[spread, :], first[spread, :]
        terms = sums[pl.ds(t, params, stride=tiles), :]
        damping, unweigh = (
            own[pl.ds(which * per + t, params, stride=tiles), :] for which in (DAMPING, UNWEIGH)
        )
        direction = vector + beta * begin
        image = jnp.where(unweigh > 0.0, damping * vector + terms, 0.0)
        image = image + beta * (unweigh * change)
        lanes = slice(t * LANES, (t + 1) * LANES)
        solution[:, lanes] = alpha * begin + alpha_next * direction
        residual[:, lanes] = unweigh * vector - alpha_next * image


def chunk_sum(received):
    total = received[0:8, :]
    for at in range(8, received.shape[0], 8):
        total = total + received[at : at + 8, :]
    return total[0:BLOCKS] + total[BLOCKS:]


def own_rows(own):
    per = own.shape[0] // 5
    at = jnp.minimum(pts_index(), per - 1)
    return [own[pl.ds(which * per + at, 1), :] for which in (WEIGHTS, PULL)]


def spread_kernel(received, own, send):
    total = chunk_sum(received)
    owners = send.shape[0] // BLOCKS
    mine, after, before, across = (total[b : b + 1] for b in range(BLOCKS))
    zero = jnp.zeros((1, LANES), F32)
    rows = own_rows(own)
    half = owners // 2
    parts = {
        0: (mine, after, before, across),
        1: (after, mine, *rows),
        -1: (before, mine, *rows),
        half: (across, mine, *rows),
        2: (after, zero, zero, zero),
        -2: (before, zero, zero, zero),
        half - 1: (across, before, zero, zero),
        half + 1: (across, after, zero, zero),
    }
    is_sums = pts_index() < own.shape[0] // 5
    twice = jnp.concatenate([total, total], axis=0)
    for at in range(0, send.shape[0], 8):
        send[at : at + 8, :] = jnp.where(is_sums, 0.0, twice)

    @pl.when(is_sums)
    def _():
        for shift, value in parts.items():
            spot = lax.rem(cam_index() + shift + owners, owners) * BLOCKS
            send[pl.ds(spot, BLOCKS), :] = jnp.concatenate(value, axis=0)


def combine_kernel(received, own, send):
    owners = received.shape[0] // BLOCKS
    half = owners // 2
    me = cam_index()

    def row(shift, at):
        spot = lax.rem(me + shift + owners, owners) * BLOCKS + at
        return received[pl.ds(spot, 1), :]

    sums = (
        (row(0, 0) + row(-1, 0)) + (row(1, 0) + row(half, 0)),
        (row(1, 1) + row(0, 1)) + (row(2, 0) + row(half + 1, 0)),
        (row(-1, 1) + row(-2, 0)) + (row(0, 2) + row(half - 1, 0)),
        (row(half, 1) + row(half - 1, 1)) + (row(half + 1, 1) + row(0, 3)),
    )
    joined = []
    for block, shift in enumerate((0, 1, -1, half)):
        weights, pull = (row(shift, 2), row(shift, 3)) if block else own_rows(own)
        joined.append(pull + weights * sums[block])
    joined = jnp.concatenate(joined, axis=0)
    total = received[0:8, :]
    for at in range(8, received.shape[0], 8):
        total = total + received[at : at + 8, :]
    total = total[0:BLOCKS] + total[BLOCKS:]
    joined = jnp.where(pts_index() < own.shape[0] // 5, joined, total)
    joined = jnp.concatenate([joined, joined], axis=0)
    for at in range(0, send.shape[0], 8):
        send[at : at + 8, :] = joined


def call(kernel, outs, *args, scratch=(), name=None):
    single = not isinstance(outs, list)
    return pl.pallas_call(
        kernel,
        out_shape=outs,
        in_specs=[VMEM] * len(args),
        out_specs=VMEM if single else [VMEM] * len(outs),
        scratch_shapes=list(scratch),
        compiler_params=PARAMS,
        name=name,
    )(*args)


def swap(value, axes, tile=BLOCKS):
    size = lax.axis_size(axes)
    rows = value.shape[0] // size
    chunks = value.reshape(size, rows // tile, tile, LANES)
    return lax.all_to_all(chunks, axes, 0, 0).reshape(value.shape)


def on_device(right_side, camera_damping, preconditioner, jac_cam, jac_pt, camera_index,
              point_index, point_damping, anchors):
    params, width = right_side.shape
    pts, cam, line, plane = ("x", "y"), ("z", "core"), ("y", "core"), ("x", "z")
    owners, rows = lax.axis_size(cam), lax.axis_size(pts)
    per = params * width // LANES
    count = camera_index.shape[1]
    jac_cam, jac_pt = jac_cam[0], jac_pt[0]
    share = 1.0 / rows

    mine = preconditioner * right_side
    shifts = (0, 1, -1, owners // 2)
    after, before, across = (
        lax.ppermute(mine, cam, [(i, (i - d) % owners) for i in range(owners)])
        for d in shifts[1:]
    )
    firsts = (cam_index() + jnp.array(shifts) + owners) % owners * width
    ids = firsts[:, None] + jnp.arange(width, dtype=jnp.int32)[None]
    keep = 1.0 - jnp.any(anchors[:, None, None] == ids[None], axis=0).astype(F32)
    folds = [
        jax.ShapeDtypeStruct((count_of * FOLDS, CHUNK), kind)
        for count_of, kind in ((6, F32), (8, F32), (6, F32), (1, jnp.int32), (1, jnp.int32))
    ]
    inverse, masks, folded, lane, slot, own = call(
        functools.partial(setup_kernel, owners),
        folds + [jax.ShapeDtypeStruct((5 * per, LANES), F32)],
        jac_pt, point_index, point_damping[0], camera_index, right_side, camera_damping,
        preconditioner, keep[:1], name="invert",
    )
    fixed = (jac_cam, folded, lane, slot, masks, inverse)
    half = width // (2 * LANES)
    scratch = (pltpu.VMEM((half * LANES, count), BF16), pltpu.VMEM((2 * FOLDS, CHUNK), F32))
    sums = jax.ShapeDtypeStruct((rows * BLOCKS, LANES), F32)
    vector = jax.ShapeDtypeStruct((per * BLOCKS, LANES), F32)

    send, start = call(
        functools.partial(first_kernel, share), [sums, vector],
        mine, after, before, across, keep, own, *fixed, scratch=scratch, name="apply_first",
    )
    chunks = swap(send, pts)
    shape = jax.ShapeDtypeStruct((owners * BLOCKS, LANES), F32)
    chunks = call(spread_kernel, shape, chunks, own, name="spread")
    chunks = swap(chunks, cam)
    chunks = call(combine_kernel, sums, chunks, own, name="combine")
    first = swap(chunks, pts)

    chunked = jax.ShapeDtypeStruct((16 * LINE, LANES), F32)
    send, step = call(
        functools.partial(second_kernel, share), [chunked, vector], first, start, own, *fixed,
        scratch=(pltpu.VMEM(vector.shape, F32), *scratch), name="apply_second",
    )
    chunks = swap(send, line, 1)
    shape = jax.ShapeDtypeStruct((lax.axis_size(plane) * PAIR, LANES), F32)
    chunks = call(pair_kernel, shape, chunks, name="pair")
    chunks = swap(chunks, plane, 1)
    shape = jax.ShapeDtypeStruct((lax.axis_size(line) * PAIR, LANES), F32)
    chunks = call(pair_sum_kernel, shape, chunks, name="pair_sum")
    second = swap(chunks, line, 1)
    shape = jax.ShapeDtypeStruct((params, width), F32)
    return tuple(
        call(
            last_kernel, [shape, shape], first, second, start, step, own,
            scratch=[pltpu.VMEM((per, LANES), F32)], name="finish",
        )
    )


def solution(mesh):
    cores = 2
    high = mesh.shape["cam"] // cores
    side = int(mesh.shape["pts"] ** 0.5)
    grid = mesh.devices.reshape(side, mesh.shape["pts"] // side, high, cores)
    mesh = Mesh(grid, ("x", "y", "z", "core"))
    cam, whole = ("z", "core"), ("x", "y", "z", "core")
    return jax.shard_map(
        on_device,
        mesh=mesh,
        in_specs=(
            P(None, cam),
            P(None, cam),
            P(None, cam),
            P(whole, None, None),
            P(whole, None, None),
            P(whole, None),
            P(whole, None),
            P(whole, None, None),
            P(),
        ),
        out_specs=(P(None, cam), P(None, cam)),
        check_vma=False,
    )
```

```python
import functools

import jax
import jax.numpy as jnp
from jax import lax
from jax.experimental import pallas as pl
from jax.experimental.pallas import tpu as pltpu
from jax.sharding import Mesh, PartitionSpec as P

LANES = 128
BLOCKS = 4
STEPS = (1, 2, 4, 8)
CHUNK = 512
FOLDS = 8
QUARTER = 32
LINE = 10
PAIR = 5
SCALARS = 64
F32, BF16 = jnp.float32, jnp.bfloat16
VMEM = pl.BlockSpec(memory_space=pltpu.VMEM)
PARAMS = pltpu.CompilerParams(vmem_limit_bytes=40 * 1024 * 1024)


def one_hot(row, count):
    ids = lax.broadcasted_iota(jnp.int32, (count, row.shape[1]), 0)
    return jnp.where(ids == row, 1.0, 0.0)


def cam_index():
    return lax.axis_index("z") * 2 + lax.axis_index("core")


def pts_index():
    return lax.axis_index("x") * lax.axis_size("y") + lax.axis_index("y")


def short_one_hot(row, count):
    ids = lax.broadcasted_iota(jnp.int16, (count, row.shape[1]), 0)
    return jnp.where(ids == row.astype(jnp.int16), BF16(1), BF16(0))


def fold(ref, row):
    parts = [ref[row : row + 1, i * CHUNK : (i + 1) * CHUNK] for i in range(FOLDS)]
    return jnp.concatenate(parts, axis=0)


def shifted(value, step):
    ids = lax.broadcasted_iota(jnp.int32, value.shape, 1)
    rolled = pltpu.roll(value, step % CHUNK, 1)
    if step > 0:
        return jnp.where(ids < step, pltpu.roll(rolled, 1, 0), rolled)
    return jnp.where(ids >= CHUNK + step, pltpu.roll(rolled, FOLDS - 1, 0), rolled)


def part(ref, index):
    return ref[index * FOLDS : (index + 1) * FOLDS, :]


def point_totals(value, masks):
    before = value
    after = value
    for i, step in enumerate(STEPS):
        before = before + part(masks, i) * shifted(before, step)
        after = after + part(masks, len(STEPS) + i) * shifted(after, -step)
    return before + (after - value)


def setup_kernel(owners, jac_pt, point_ref, damping, camera_ref, right_side, camera_damping,
                 preconditioner, keep, inverse, masks, folded, lane, slot, own):
    width = right_side.shape[1]
    own_arrays(right_side[...], camera_damping[...], preconditioner[...], keep[...], own)
    camera = fold(camera_ref, 0)
    shift = lax.rem(lax.div(camera, width) - cam_index() + owners, owners)
    block = jnp.where(shift == 1, 1, jnp.where(shift == owners - 1, 2, 3))
    block = jnp.where(shift == 0, 0, block)
    inner = lax.rem(camera, width)
    tile = lax.div(inner, LANES)
    lane[...] = lax.div(tile, 2) * LANES + lax.rem(inner, LANES)
    slot[...] = lax.rem(tile, 2) * BLOCKS + block

    point = fold(point_ref, 0)
    for i, step in enumerate(STEPS + tuple(-step for step in STEPS)):
        same = jnp.where(shifted(point, step) == point, 1.0, 0.0)
        masks[i * FOLDS : (i + 1) * FOLDS, :] = same
    rows = [fold(jac_pt, r) for r in range(6)]
    for r in range(6):
        folded[r * FOLDS : (r + 1) * FOLDS, :] = rows[r]
    pairs = [(0, 0), (0, 1), (0, 2), (1, 1), (1, 2), (2, 2)]
    xx, xy, xz, yy, yz, zz = (
        point_totals(rows[a] * rows[b] + rows[3 + a] * rows[3 + b], masks) for a, b in pairs
    )

    tiles = damping.shape[1] // LANES
    table = jnp.concatenate(
        [damping[k : k + 1, t * LANES : (t + 1) * LANES] for k in range(3) for t in range(tiles)],
        axis=0,
    )
    high = table.astype(BF16)
    rest = table - high.astype(F32)
    mid = rest.astype(BF16)
    low = (rest - mid.astype(F32)).astype(BF16)
    damp = [[], [], []]
    for i in range(FOLDS):
        spot = point[i : i + 1]
        hot = short_one_hot(lax.rem(spot, LANES), LANES)
        mask = one_hot(lax.div(spot, LANES), tiles)
        picked = sum(jnp.dot(piece, hot, preferred_element_type=F32) for piece in (high, mid, low))
        for k in range(3):
            damp[k].append(lane_sums(picked[k * tiles : (k + 1) * tiles] * mask))
    damp = [jnp.concatenate(rows_of, axis=0) for rows_of in damp]
    xx, yy, zz = xx + damp[0], yy + damp[1], zz + damp[2]
    cof_xx = yy * zz - yz * yz
    cof_xy = xz * yz - xy * zz
    cof_xz = xy * yz - xz * yy
    cof_yy = xx * zz - xz * xz
    cof_yz = xy * xz - xx * yz
    cof_zz = xx * yy - xy * xy
    det = xx * cof_xx + xy * cof_xy + xz * cof_xz
    for r, cof in enumerate((cof_xx, cof_xy, cof_xz, cof_yy, cof_yz, cof_zz)):
        inverse[r * FOLDS : (r + 1) * FOLDS, :] = cof / det


def lane_sums(value):
    return jnp.sum(value, axis=0, keepdims=True)


def schur(vector, send, jac_cam, folded, lane, slot, masks, inverse, hot, error):
    params = jac_cam.shape[0] // 2
    slots = 2 * BLOCKS
    half = hot.shape[0] // LANES
    rows = params * slots
    table = vector.reshape(params, half, slots, LANES)
    table = jnp.concatenate([table[:, h].reshape(rows, LANES) for h in range(half)], axis=1)
    high = table.astype(BF16)
    low = (table - high.astype(F32)).astype(BF16)
    table = jnp.concatenate([high, low], axis=0)

    for i in range(FOLDS):
        span = slice(i * CHUNK, (i + 1) * CHUNK)
        spot = short_one_hot(lane[i : i + 1, :], half * LANES)
        hot[:, span] = spot
        got = jnp.dot(table, spot, preferred_element_type=F32)
        got = got[:rows] + got[rows:]
        mask = one_hot(slot[i : i + 1, :], slots)
        for r in range(2):
            total = jnp.zeros((slots, CHUNK), F32)
            for a in range(params):
                jac = jac_cam[r * params + a : r * params + a + 1, span]
                total = total + jac * got[a * slots : (a + 1) * slots]
            error[r * FOLDS + i : r * FOLDS + i + 1, :] = lane_sums(total * mask)

    e0, e1 = part(error, 0), part(error, 1)
    jp = [part(folded, r) for r in range(6)]
    inv = [part(inverse, r) for r in range(6)]
    y0, y1, y2 = (point_totals(jp[k] * e0 + jp[3 + k] * e1, masks) for k in range(3))
    z = (
        inv[0] * y0 + inv[1] * y1 + inv[2] * y2,
        inv[1] * y0 + inv[3] * y1 + inv[4] * y2,
        inv[2] * y0 + inv[4] * y1 + inv[5] * y2,
    )
    left0 = e0 - (jp[0] * z[0] + jp[1] * z[1] + jp[2] * z[2])
    left1 = e1 - (jp[3] * z[0] + jp[4] * z[1] + jp[5] * z[2])
    energy = e0 * left0 + e1 * left1

    total = jnp.zeros((2 * rows, half * LANES), F32)
    for i in range(FOLDS):
        span = slice(i * CHUNK, (i + 1) * CHUNK)
        mask = one_hot(slot[i : i + 1, :], slots)
        first, second = mask * left0[i : i + 1], mask * left1[i : i + 1]
        highs, lows = [], []
        for a in range(params):
            value = jac_cam[a : a + 1, span] * first
            value = value + jac_cam[params + a : params + a + 1, span] * second
            near = value.astype(BF16)
            highs.append(near)
            lows.append((value - near.astype(F32)).astype(BF16))
        both = jnp.concatenate(highs + lows, axis=0)
        total = total + lax.dot_general(
            both, hot[:, span], (((1,), (1,)), ((), ())), preferred_element_type=F32
        )
    total = total[:rows] + total[rows:]
    for a in range(params):
        for h in range(half):
            start = (a * half + h) * slots
            send[start : start + slots, :] = total[
                a * slots : (a + 1) * slots, h * LANES : (h + 1) * LANES
            ]
    return lane_sums(sum(energy[:, t * LANES : (t + 1) * LANES] for t in range(CHUNK // LANES)))


RIGHT, DAMPING, WEIGHTS, PULL, UNWEIGH = range(5)


def own_part(own, which):
    per = own.shape[0] // 5
    return own[which * per : (which + 1) * per, :]


def own_arrays(right, damping, precond, keep, own):
    params, width = right.shape
    tiles = width // LANES
    weights = precond * keep
    parts = (right, damping, weights, weights * damping * weights * right, keep / precond)
    for t in range(tiles):
        lanes = slice(t * LANES, (t + 1) * LANES)
        for which, value in enumerate(parts):
            place = pl.ds(which * params * tiles + t, params, stride=tiles)
            own[place, :] = value[:, lanes]


def send_scalars(send, data_rows, rows):
    rest = send.shape[0] - data_rows
    send[data_rows:, :] = jnp.zeros((rest, LANES), F32)
    for index, row in enumerate(rows):
        at = data_rows + index * BLOCKS
        send[at : at + 1, :] = row


def scalar(ref, row):
    return jnp.sum(ref[row : row + 1, :], axis=1, keepdims=True)


def first_kernel(share, mine, after, before, across, keep, own, jac_cam, folded, lane, slot,
                 masks, inverse, send, start, hot, error):
    params, tiles, _ = mine.shape
    for block, ref in enumerate((mine, after, before, across)):
        for t in range(tiles):
            place = pl.ds(t * BLOCKS + block, params, stride=tiles * BLOCKS)
            kept = keep[block : block + 1, t * LANES : (t + 1) * LANES]
            start[place, :] = ref[:, t, :] * kept
    energy = schur(start[...], send, jac_cam, folded, lane, slot, masks, inverse, hot, error)
    vector = start[pl.ds(0, params * tiles, stride=BLOCKS), :]
    energy = energy + share * lane_sums(own_part(own, DAMPING) * vector * vector)
    gamma = share * lane_sums(own_part(own, RIGHT) * vector)
    send_scalars(send, start.shape[0], (energy, gamma))


def lane_ids(rows=1):
    return lax.broadcasted_iota(jnp.int32, (rows, LANES), 1)


def second_kernel(share, received, start, own, jac_cam, folded, lane, slot, masks, inverse,
                  send, step, sums, hot, error):
    data_rows = start.shape[0]
    per = data_rows // BLOCKS
    alpha = scalar(received, data_rows + BLOCKS) / scalar(received, data_rows)
    step[...] = start[...] - alpha * received[0:data_rows, :]
    energy = schur(step[...], sums, jac_cam, folded, lane, slot, masks, inverse, hot, error)
    vector = step[pl.ds(0, per, stride=BLOCKS), :]
    change = received[pl.ds(0, per, stride=BLOCKS), :]
    residual = own_part(own, UNWEIGH) * vector
    energy = energy + share * lane_sums(own_part(own, DAMPING) * vector * vector)
    fresh = share * lane_sums(residual * vector)
    cross = share * lane_sums(residual * change)
    ids = lane_ids()
    extra = jnp.zeros((1, LANES), F32)
    for index, row in enumerate((energy, fresh, cross)):
        extra = jnp.where(ids == SCALARS + index, jnp.sum(row, axis=1, keepdims=True), extra)
    for chunk in range(16):
        base = chunk * LINE
        send[base : base + 8, :] = sums[chunk * 8 : (chunk + 1) * 8, :]
        send[base + 9 : base + 10, :] = extra
    for q in range(4):
        thirds = sums[(32 + q) * BLOCKS : (33 + q) * BLOCKS, :]
        rolled = [thirds] + [pltpu.roll(thirds, QUARTER * k, 1) for k in range(1, 4)]
        for i in range(4):
            mixed = rolled[(0 - i) % 4][0:1]
            for block in range(1, BLOCKS):
                piece = rolled[(block - i) % 4][block : block + 1]
                mixed = jnp.where(ids >= QUARTER * block, piece, mixed)
            at = (4 * q + i) * LINE + 8
            send[at : at + 1, :] = mixed


def pair_kernel(received, send):
    first = received[0:LINE, :]
    second = received[LINE : 2 * LINE, :]
    for source in range(2, received.shape[0] // LINE, 2):
        first = first + received[source * LINE : (source + 1) * LINE, :]
        second = second + received[(source + 1) * LINE : (source + 2) * LINE, :]

    def rows_of(value, block):
        third = value[8:9]
        if block:
            third = pltpu.roll(third, LANES - QUARTER * block, 1)
        return [value[block : block + 1], value[BLOCKS + block : BLOCKS + block + 1], third]

    zero = [jnp.zeros((1, LANES), F32)] * 3
    ids = lane_ids()
    scalars = first[9:10] + second[9:10]
    own_even = [a + b for a, b in zip(rows_of(first, 0), rows_of(second, 2))]
    own_odd = [a + b for a, b in zip(rows_of(first, 1), rows_of(second, 0))]
    pairs = (
        (0, own_even, own_odd),
        (1, rows_of(second, 1), zero),
        (-1, zero, rows_of(first, 2)),
        (4, rows_of(first, 3), rows_of(second, 3)),
    )

    def joined(even, odd):
        mixed = jnp.where(ids < QUARTER, even[2], pltpu.roll(odd[2], QUARTER, 1))
        mixed = jnp.where(ids < SCALARS, mixed, scalars)
        return jnp.concatenate(even[:2] + odd[:2] + [mixed], axis=0)

    size = lax.axis_size("z")
    columns = send.shape[0] // (size * PAIR)
    nothing = joined(zero, zero)
    for spot in range(columns * size):
        send[spot * PAIR : (spot + 1) * PAIR, :] = nothing
    for shift, even, odd in pairs:
        value = joined(even, odd)
        place = lax.rem(lax.axis_index("z") + shift + size, size)
        for x in range(columns):
            send[pl.ds((x * size + place) * PAIR, PAIR), :] = value


def pair_sum_kernel(received, send):
    total = received[0:PAIR, :]
    for source in range(1, received.shape[0] // PAIR):
        total = total + received[source * PAIR : (source + 1) * PAIR, :]
    for spot in range(send.shape[0] // PAIR):
        send[spot * PAIR : (spot + 1) * PAIR, :] = total


def last_kernel(first, second, start, step, own, solution, residual, sums):
    params, width = solution.shape
    tiles = width // LANES
    per = params * tiles
    data_rows = per * BLOCKS
    odd = lax.axis_index("core") == 1
    ids = lane_ids()
    for chunk in range(16):
        base = chunk * PAIR
        even_rows, odd_rows = second[base : base + 2, :], second[base + 2 : base + 4, :]
        sums[2 * chunk : 2 * chunk + 2, :] = jnp.where(odd, odd_rows, even_rows)
    for q in range(4):
        third = jnp.zeros((1, LANES), F32)
        for i in range(4):
            row = second[(4 * q + i) * PAIR + 4 : (4 * q + i) * PAIR + 5, :]
            even_row = pltpu.roll(row, 32 * i, 1) if i else row
            odd_row = pltpu.roll(row, (32 * i - 32) % LANES, 1) if i != 1 else row
            place = jnp.logical_and(ids >= 32 * i, ids < 32 * (i + 1))
            third = jnp.where(place, jnp.where(odd, odd_row, even_row), third)
        sums[32 + q : 33 + q, :] = third

    curve, gamma = scalar(first, data_rows), scalar(first, data_rows + BLOCKS)
    mixed = second[PAIR - 1 : PAIR, :]
    energy, fresh, cross = (
        jnp.sum(jnp.where(ids == SCALARS + i, mixed, 0.0), axis=1, keepdims=True) for i in range(3)
    )
    alpha = gamma / curve
    beta = fresh / gamma
    alpha_next = fresh / (energy + 2.0 * beta * cross + beta * beta * curve)
    for t in range(tiles):
        spread = pl.ds(t * BLOCKS, params, stride=tiles * BLOCKS)
        begin, vector, change = start[spread, :], step[spread, :], first[spread, :]
        terms = sums[pl.ds(t, params, stride=tiles), :]
        damping, unweigh = (
            own[pl.ds(which * per + t, params, stride=tiles), :] for which in (DAMPING, UNWEIGH)
        )
        direction = vector + beta * begin
        image = jnp.where(unweigh > 0.0, damping * vector + terms, 0.0)
        image = image + beta * (unweigh * change)
        lanes = slice(t * LANES, (t + 1) * LANES)
        solution[:, lanes] = alpha * begin + alpha_next * direction
        residual[:, lanes] = unweigh * vector - alpha_next * image


def chunk_sum(received):
    total = received[0:8, :]
    for at in range(8, received.shape[0], 8):
        total = total + received[at : at + 8, :]
    return total[0:BLOCKS] + total[BLOCKS:]


def own_rows(own):
    per = own.shape[0] // 5
    at = jnp.minimum(pts_index(), per - 1)
    return [own[pl.ds(which * per + at, 1), :] for which in (WEIGHTS, PULL)]


def spread_kernel(received, own, send):
    total = chunk_sum(received)
    owners = send.shape[0] // BLOCKS
    mine, after, before, across = (total[b : b + 1] for b in range(BLOCKS))
    zero = jnp.zeros((1, LANES), F32)
    rows = own_rows(own)
    half = owners // 2
    parts = {
        0: (mine, after, before, across),
        1: (after, mine, *rows),
        -1: (before, mine, *rows),
        half: (across, mine, *rows),
        2: (after, zero, zero, zero),
        -2: (before, zero, zero, zero),
        half - 1: (across, before, zero, zero),
        half + 1: (across, after, zero, zero),
    }
    is_sums = pts_index() < own.shape[0] // 5
    twice = jnp.concatenate([total, total], axis=0)
    for at in range(0, send.shape[0], 8):
        send[at : at + 8, :] = jnp.where(is_sums, 0.0, twice)

    @pl.when(is_sums)
    def _():
        for shift, value in parts.items():
            spot = lax.rem(cam_index() + shift + owners, owners) * BLOCKS
            send[pl.ds(spot, BLOCKS), :] = jnp.concatenate(value, axis=0)


def combine_kernel(received, own, send):
    owners = received.shape[0] // BLOCKS
    half = owners // 2
    me = cam_index()

    def row(shift, at):
        spot = lax.rem(me + shift + owners, owners) * BLOCKS + at
        return received[pl.ds(spot, 1), :]

    sums = (
        (row(0, 0) + row(-1, 0)) + (row(1, 0) + row(half, 0)),
        (row(1, 1) + row(0, 1)) + (row(2, 0) + row(half + 1, 0)),
        (row(-1, 1) + row(-2, 0)) + (row(0, 2) + row(half - 1, 0)),
        (row(half, 1) + row(half - 1, 1)) + (row(half + 1, 1) + row(0, 3)),
    )
    joined = []
    for block, shift in enumerate((0, 1, -1, half)):
        weights, pull = (row(shift, 2), row(shift, 3)) if block else own_rows(own)
        joined.append(pull + weights * sums[block])
    joined = jnp.concatenate(joined, axis=0)
    total = received[0:8, :]
    for at in range(8, received.shape[0], 8):
        total = total + received[at : at + 8, :]
    total = total[0:BLOCKS] + total[BLOCKS:]
    joined = jnp.where(pts_index() < own.shape[0] // 5, joined, total)
    joined = jnp.concatenate([joined, joined], axis=0)
    for at in range(0, send.shape[0], 8):
        send[at : at + 8, :] = joined


def call(kernel, outs, *args, scratch=(), name=None):
    single = not isinstance(outs, list)
    return pl.pallas_call(
        kernel,
        out_shape=outs,
        in_specs=[VMEM] * len(args),
        out_specs=VMEM if single else [VMEM] * len(outs),
        scratch_shapes=list(scratch),
        compiler_params=PARAMS,
        name=name,
    )(*args)


def swap(value, axes, tile=BLOCKS):
    size = lax.axis_size(axes)
    rows = value.shape[0] // size
    chunks = value.reshape(size, rows // tile, tile, LANES)
    return lax.all_to_all(chunks, axes, 0, 0).reshape(value.shape)


def on_device(right_side, camera_damping, preconditioner, jac_cam, jac_pt, camera_index,
              point_index, point_damping, anchors):
    params, width = right_side.shape
    pts, cam, line, plane = ("x", "y"), ("z", "core"), ("y", "core"), ("x", "z")
    owners, rows = lax.axis_size(cam), lax.axis_size(pts)
    per = params * width // LANES
    count = camera_index.shape[1]
    jac_cam, jac_pt = jac_cam[0], jac_pt[0]
    share = 1.0 / rows

    tiles = width // LANES
    mine = preconditioner.reshape(params, tiles, LANES) * right_side.reshape(params, tiles, LANES)
    shifts = (0, 1, -1, owners // 2)
    after, before, across = (
        lax.ppermute(mine, cam, [(i, (i - d) % owners) for i in range(owners)])
        for d in shifts[1:]
    )
    firsts = (cam_index() + jnp.array(shifts) + owners) % owners * width
    ids = firsts[:, None] + jnp.arange(width, dtype=jnp.int32)[None]
    keep = 1.0 - jnp.any(anchors[:, None, None] == ids[None], axis=0).astype(F32)
    folds = [
        jax.ShapeDtypeStruct((count_of * FOLDS, CHUNK), kind)
        for count_of, kind in ((6, F32), (8, F32), (6, F32), (1, jnp.int32), (1, jnp.int32))
    ]
    inverse, masks, folded, lane, slot, own = call(
        functools.partial(setup_kernel, owners),
        folds + [jax.ShapeDtypeStruct((5 * per, LANES), F32)],
        jac_pt, point_index, point_damping[0], camera_index, right_side, camera_damping,
        preconditioner, keep[:1], name="invert",
    )
    fixed = (jac_cam, folded, lane, slot, masks, inverse)
    half = width // (2 * LANES)
    scratch = (pltpu.VMEM((half * LANES, count), BF16), pltpu.VMEM((2 * FOLDS, CHUNK), F32))
    sums = jax.ShapeDtypeStruct((rows * BLOCKS, LANES), F32)
    vector = jax.ShapeDtypeStruct((per * BLOCKS, LANES), F32)

    send, start = call(
        functools.partial(first_kernel, share), [sums, vector],
        mine, after, before, across, keep, own, *fixed, scratch=scratch, name="apply_first",
    )
    chunks = swap(send, pts)
    shape = jax.ShapeDtypeStruct((owners * BLOCKS, LANES), F32)
    chunks = call(spread_kernel, shape, chunks, own, name="spread")
    chunks = swap(chunks, cam)
    chunks = call(combine_kernel, sums, chunks, own, name="combine")
    first = swap(chunks, pts)

    chunked = jax.ShapeDtypeStruct((16 * LINE, LANES), F32)
    send, step = call(
        functools.partial(second_kernel, share), [chunked, vector], first, start, own, *fixed,
        scratch=(pltpu.VMEM(vector.shape, F32), *scratch), name="apply_second",
    )
    chunks = swap(send, line, 1)
    shape = jax.ShapeDtypeStruct((lax.axis_size(plane) * PAIR, LANES), F32)
    chunks = call(pair_kernel, shape, chunks, name="pair")
    chunks = swap(chunks, plane, 1)
    shape = jax.ShapeDtypeStruct((lax.axis_size(line) * PAIR, LANES), F32)
    chunks = call(pair_sum_kernel, shape, chunks, name="pair_sum")
    second = swap(chunks, line, 1)
    shape = jax.ShapeDtypeStruct((params, width), F32)
    return tuple(
        call(
            last_kernel, [shape, shape], first, second, start, step, own,
            scratch=[pltpu.VMEM((per, LANES), F32)], name="finish",
        )
    )


def solution(mesh):
    cores = 2
    high = mesh.shape["cam"] // cores
    side = int(mesh.shape["pts"] ** 0.5)
    grid = mesh.devices.reshape(side, mesh.shape["pts"] // side, high, cores)
    mesh = Mesh(grid, ("x", "y", "z", "core"))
    cam, whole = ("z", "core"), ("x", "y", "z", "core")
    return jax.shard_map(
        on_device,
        mesh=mesh,
        in_specs=(
            P(None, cam),
            P(None, cam),
            P(None, cam),
            P(whole, None, None),
            P(whole, None, None),
            P(whole, None),
            P(whole, None),
            P(whole, None, None),
            P(),
        ),
        out_specs=(P(None, cam), P(None, cam)),
        check_vma=False,
    )
```

```python
import functools

import jax
import jax.numpy as jnp
from jax import lax
from jax.experimental import pallas as pl
from jax.experimental.pallas import tpu as pltpu
from jax.sharding import Mesh, PartitionSpec as P

LANES = 128
BLOCKS = 4
STEPS = (1, 2, 4, 8)
CHUNK = 512
FOLDS = 8
QUARTER = 32
PAIR = 5
OWN = 3
SCALARS = 64
F32, BF16 = jnp.float32, jnp.bfloat16
VMEM = pl.BlockSpec(memory_space=pltpu.VMEM)
PARAMS = pltpu.CompilerParams(vmem_limit_bytes=40 * 1024 * 1024)


def one_hot(row, count):
    ids = lax.broadcasted_iota(jnp.int32, (count, row.shape[1]), 0)
    return jnp.where(ids == row, 1.0, 0.0)


def cam_index():
    return lax.axis_index("z") * 2 + lax.axis_index("core")


def pts_index():
    x = lax.axis_index("xa") * 2 + lax.axis_index("xb")
    return x * lax.axis_size("y") + lax.axis_index("y")


def short_one_hot(row, count):
    ids = lax.broadcasted_iota(jnp.int16, (count, row.shape[1]), 0)
    return jnp.where(ids == row.astype(jnp.int16), BF16(1), BF16(0))


def fold(ref, row):
    parts = [ref[row : row + 1, i * CHUNK : (i + 1) * CHUNK] for i in range(FOLDS)]
    return jnp.concatenate(parts, axis=0)


def shifted(value, step):
    ids = lax.broadcasted_iota(jnp.int32, value.shape, 1)
    rolled = pltpu.roll(value, step % CHUNK, 1)
    if step > 0:
        return jnp.where(ids < step, pltpu.roll(rolled, 1, 0), rolled)
    return jnp.where(ids >= CHUNK + step, pltpu.roll(rolled, FOLDS - 1, 0), rolled)


def part(ref, index):
    return ref[index * FOLDS : (index + 1) * FOLDS, :]


def point_totals(value, masks):
    before = value
    after = value
    for i, step in enumerate(STEPS):
        before = before + part(masks, i) * shifted(before, step)
        after = after + part(masks, len(STEPS) + i) * shifted(after, -step)
    return before + (after - value)


def setup_kernel(owners, jac_pt, point_ref, damping, camera_ref, right_side, camera_damping,
                 preconditioner, keep, inverse, masks, folded, lane, slot, own):
    width = right_side.shape[1]
    own_arrays(right_side[...], camera_damping[...], preconditioner[...], keep[...], own)
    camera = fold(camera_ref, 0)
    shift = lax.rem(lax.div(camera, width) - cam_index() + owners, owners)
    block = jnp.where(shift == 1, 1, jnp.where(shift == owners - 1, 2, 3))
    block = jnp.where(shift == 0, 0, block)
    inner = lax.rem(camera, width)
    tile = lax.div(inner, LANES)
    lane[...] = lax.div(tile, 2) * LANES + lax.rem(inner, LANES)
    slot[...] = lax.rem(tile, 2) * BLOCKS + block

    point = fold(point_ref, 0)
    for i, step in enumerate(STEPS + tuple(-step for step in STEPS)):
        same = jnp.where(shifted(point, step) == point, 1.0, 0.0)
        masks[i * FOLDS : (i + 1) * FOLDS, :] = same
    rows = [fold(jac_pt, r) for r in range(6)]
    for r in range(6):
        folded[r * FOLDS : (r + 1) * FOLDS, :] = rows[r]
    pairs = [(0, 0), (0, 1), (0, 2), (1, 1), (1, 2), (2, 2)]
    xx, xy, xz, yy, yz, zz = (
        point_totals(rows[a] * rows[b] + rows[3 + a] * rows[3 + b], masks) for a, b in pairs
    )

    tiles = damping.shape[1] // LANES
    table = jnp.concatenate(
        [damping[k : k + 1, t * LANES : (t + 1) * LANES] for k in range(3) for t in range(tiles)],
        axis=0,
    )
    high = table.astype(BF16)
    rest = table - high.astype(F32)
    mid = rest.astype(BF16)
    low = (rest - mid.astype(F32)).astype(BF16)
    damp = [[], [], []]
    for i in range(FOLDS):
        spot = point[i : i + 1]
        hot = short_one_hot(lax.rem(spot, LANES), LANES)
        mask = one_hot(lax.div(spot, LANES), tiles)
        picked = sum(jnp.dot(piece, hot, preferred_element_type=F32) for piece in (high, mid, low))
        for k in range(3):
            damp[k].append(lane_sums(picked[k * tiles : (k + 1) * tiles] * mask))
    damp = [jnp.concatenate(rows_of, axis=0) for rows_of in damp]
    xx, yy, zz = xx + damp[0], yy + damp[1], zz + damp[2]
    cof_xx = yy * zz - yz * yz
    cof_xy = xz * yz - xy * zz
    cof_xz = xy * yz - xz * yy
    cof_yy = xx * zz - xz * xz
    cof_yz = xy * xz - xx * yz
    cof_zz = xx * yy - xy * xy
    det = xx * cof_xx + xy * cof_xy + xz * cof_xz
    for r, cof in enumerate((cof_xx, cof_xy, cof_xz, cof_yy, cof_yz, cof_zz)):
        inverse[r * FOLDS : (r + 1) * FOLDS, :] = cof / det


def lane_sums(value):
    return jnp.sum(value, axis=0, keepdims=True)


def schur(vector, send, jac_cam, folded, lane, slot, masks, inverse, hot, error):
    params = jac_cam.shape[0] // 2
    slots = 2 * BLOCKS
    half = hot.shape[0] // LANES
    rows = params * slots
    table = vector.reshape(params, half, slots, LANES)
    table = jnp.concatenate([table[:, h].reshape(rows, LANES) for h in range(half)], axis=1)
    high = table.astype(BF16)
    low = (table - high.astype(F32)).astype(BF16)
    table = jnp.concatenate([high, low], axis=0)

    for i in range(FOLDS):
        span = slice(i * CHUNK, (i + 1) * CHUNK)
        spot = short_one_hot(lane[i : i + 1, :], half * LANES)
        hot[:, span] = spot
        got = jnp.dot(table, spot, preferred_element_type=F32)
        got = got[:rows] + got[rows:]
        mask = one_hot(slot[i : i + 1, :], slots)
        for r in range(2):
            total = jnp.zeros((slots, CHUNK), F32)
            for a in range(params):
                jac = jac_cam[r * params + a : r * params + a + 1, span]
                total = total + jac * got[a * slots : (a + 1) * slots]
            error[r * FOLDS + i : r * FOLDS + i + 1, :] = lane_sums(total * mask)

    e0, e1 = part(error, 0), part(error, 1)
    jp = [part(folded, r) for r in range(6)]
    inv = [part(inverse, r) for r in range(6)]
    y0, y1, y2 = (point_totals(jp[k] * e0 + jp[3 + k] * e1, masks) for k in range(3))
    z = (
        inv[0] * y0 + inv[1] * y1 + inv[2] * y2,
        inv[1] * y0 + inv[3] * y1 + inv[4] * y2,
        inv[2] * y0 + inv[4] * y1 + inv[5] * y2,
    )
    left0 = e0 - (jp[0] * z[0] + jp[1] * z[1] + jp[2] * z[2])
    left1 = e1 - (jp[3] * z[0] + jp[4] * z[1] + jp[5] * z[2])
    energy = e0 * left0 + e1 * left1

    total = jnp.zeros((2 * rows, half * LANES), F32)
    for i in range(FOLDS):
        span = slice(i * CHUNK, (i + 1) * CHUNK)
        mask = one_hot(slot[i : i + 1, :], slots)
        first, second = mask * left0[i : i + 1], mask * left1[i : i + 1]
        highs, lows = [], []
        for a in range(params):
            value = jac_cam[a : a + 1, span] * first
            value = value + jac_cam[params + a : params + a + 1, span] * second
            near = value.astype(BF16)
            highs.append(near)
            lows.append((value - near.astype(F32)).astype(BF16))
        both = jnp.concatenate(highs + lows, axis=0)
        total = total + lax.dot_general(
            both, hot[:, span], (((1,), (1,)), ((), ())), preferred_element_type=F32
        )
    total = total[:rows] + total[rows:]
    for a in range(params):
        for h in range(half):
            start = (a * half + h) * slots
            send[start : start + slots, :] = total[
                a * slots : (a + 1) * slots, h * LANES : (h + 1) * LANES
            ]
    return lane_sums(sum(energy[:, t * LANES : (t + 1) * LANES] for t in range(CHUNK // LANES)))


RIGHT, DAMPING, WEIGHTS, PULL, UNWEIGH = range(5)


def own_part(own, which):
    per = own.shape[0] // 5
    return own[which * per : (which + 1) * per, :]


def own_arrays(right, damping, precond, keep, own):
    params, width = right.shape
    tiles = width // LANES
    weights = precond * keep
    parts = (right, damping, weights, weights * damping * weights * right, keep / precond)
    for t in range(tiles):
        lanes = slice(t * LANES, (t + 1) * LANES)
        for which, value in enumerate(parts):
            place = pl.ds(which * params * tiles + t, params, stride=tiles)
            own[place, :] = value[:, lanes]


def send_scalars(send, data_rows, rows):
    rest = send.shape[0] - data_rows
    send[data_rows:, :] = jnp.zeros((rest, LANES), F32)
    for index, row in enumerate(rows):
        at = data_rows + index * BLOCKS
        send[at : at + 1, :] = row


def scalar(ref, row):
    return jnp.sum(ref[row : row + 1, :], axis=1, keepdims=True)


def first_kernel(share, mine, after, before, across, keep, own, jac_cam, folded, lane, slot,
                 masks, inverse, send, start, hot, error):
    params, tiles, _ = mine.shape
    for block, ref in enumerate((mine, after, before, across)):
        for t in range(tiles):
            place = pl.ds(t * BLOCKS + block, params, stride=tiles * BLOCKS)
            kept = keep[block : block + 1, t * LANES : (t + 1) * LANES]
            start[place, :] = ref[:, t, :] * kept
    energy = schur(start[...], send, jac_cam, folded, lane, slot, masks, inverse, hot, error)
    vector = start[pl.ds(0, params * tiles, stride=BLOCKS), :]
    energy = energy + share * lane_sums(own_part(own, DAMPING) * vector * vector)
    gamma = share * lane_sums(own_part(own, RIGHT) * vector)
    send_scalars(send, start.shape[0], (energy, gamma))


def lane_ids(rows=1):
    return lax.broadcasted_iota(jnp.int32, (rows, LANES), 1)


def second_kernel(share, received, start, own, jac_cam, folded, lane, slot, masks, inverse,
                  send, step, sums, hot, error):
    data_rows = start.shape[0]
    per = data_rows // BLOCKS
    alpha = scalar(received, data_rows + BLOCKS) / scalar(received, data_rows)
    step[...] = start[...] - alpha * received[0:data_rows, :]
    energy = schur(step[...], sums, jac_cam, folded, lane, slot, masks, inverse, hot, error)
    vector = step[pl.ds(0, per, stride=BLOCKS), :]
    change = received[pl.ds(0, per, stride=BLOCKS), :]
    residual = own_part(own, UNWEIGH) * vector
    energy = energy + share * lane_sums(own_part(own, DAMPING) * vector * vector)
    fresh = share * lane_sums(residual * vector)
    cross = share * lane_sums(residual * change)
    ids = lane_ids()
    extra = jnp.zeros((1, LANES), F32)
    for index, row in enumerate((energy, fresh, cross)):
        extra = jnp.where(ids == SCALARS + index, jnp.sum(row, axis=1, keepdims=True), extra)
    odd = lax.axis_index("core") == 1
    for chunk in range(16):
        q, i = chunk // 4, chunk % 4
        thirds = sums[(32 + q) * BLOCKS : (33 + q) * BLOCKS, :]
        low = pltpu.roll(thirds, (-QUARTER * i) % LANES, 1) if i else thirds
        high = pltpu.roll(thirds, (QUARTER - QUARTER * i) % LANES, 1) if i != 1 else thirds
        rows = sums[chunk * 2 * BLOCKS : (chunk + 1) * 2 * BLOCKS, :]

        def two(a, b):
            mixed = jnp.where(ids < SCALARS, high[b : b + 1], extra)
            mixed = jnp.where(ids < QUARTER, low[a : a + 1], mixed)
            pieces = [rows[at : at + 1] for at in (a, BLOCKS + a, b, BLOCKS + b)]
            return jnp.concatenate(pieces + [mixed], axis=0)

        same, other = two(0, 3), two(1, 2)
        base = 2 * chunk * PAIR
        send[base : base + PAIR, :] = jnp.where(odd, other, same)
        send[base + PAIR : base + 2 * PAIR, :] = jnp.where(odd, same, other)


def own_block_kernel(received, send):
    evens = received[0:PAIR, :]
    odds = received[PAIR : 2 * PAIR, :]
    for source in range(2, received.shape[0] // PAIR, 2):
        evens = evens + received[source * PAIR : (source + 1) * PAIR, :]
        odds = odds + received[(source + 1) * PAIR : (source + 2) * PAIR, :]
    odd = lax.axis_index("core") == 1
    ids = lane_ids()
    scalars = evens[PAIR - 1 : PAIR] + odds[PAIR - 1 : PAIR]
    same = jnp.where(odd, odds, evens)
    other = jnp.where(odd, evens, odds)

    def block(value, which):
        third = value[PAIR - 1 : PAIR]
        if which:
            third = pltpu.roll(third, LANES - QUARTER, 1)
        return jnp.concatenate([value[2 * which : 2 * which + 2], third], axis=0)

    other_first, other_second = block(other, 0), block(other, 1)
    own = block(same, 0) + jnp.where(odd, other_first, other_second)
    beside = jnp.where(odd, other_second, other_first)
    across = block(same, 1)
    is_third = lax.broadcasted_iota(jnp.int32, (OWN, LANES), 0) == OWN - 1
    is_rest = jnp.logical_and(is_third, lane_ids(OWN) >= SCALARS)

    def with_scalars(value):
        return jnp.where(is_rest, scalars, value)

    size = lax.axis_size("z")
    columns = send.shape[0] // (size * OWN)
    nothing = with_scalars(jnp.zeros((OWN, LANES), F32))
    for spot in range(columns * size):
        send[spot * OWN : (spot + 1) * OWN, :] = nothing
    step = 1 - 2 * lax.axis_index("core")
    for shift, value in ((0, own), (step, beside), (size // 2, across)):
        place = lax.rem(lax.axis_index("z") + shift + size, size)
        value = with_scalars(value)
        for x in range(columns):
            send[pl.ds((x * size + place) * OWN, OWN), :] = value


def own_sum_kernel(received, send):
    total = received[0:OWN, :]
    for source in range(1, received.shape[0] // OWN):
        total = total + received[source * OWN : (source + 1) * OWN, :]
    for spot in range(send.shape[0] // OWN):
        send[spot * OWN : (spot + 1) * OWN, :] = total


def last_kernel(first, second, start, step, own, solution, residual, sums):
    params, width = solution.shape
    tiles = width // LANES
    per = params * tiles
    data_rows = per * BLOCKS
    ids = lane_ids()
    for chunk in range(16):
        sums[2 * chunk : 2 * chunk + 2, :] = second[chunk * OWN : chunk * OWN + 2, :]
    for q in range(4):
        third = jnp.zeros((1, LANES), F32)
        for i in range(4):
            at = (4 * q + i) * OWN + 2
            row = second[at : at + 1, :]
            row = pltpu.roll(row, QUARTER * i, 1) if i else row
            third = jnp.where(ids >= QUARTER * i, row, third)
        sums[32 + q : 33 + q, :] = third

    curve, gamma = scalar(first, data_rows), scalar(first, data_rows + BLOCKS)
    mixed = second[OWN - 1 : OWN, :]
    energy, fresh, cross = (
        jnp.sum(jnp.where(ids == SCALARS + i, mixed, 0.0), axis=1, keepdims=True) for i in range(3)
    )
    alpha = gamma / curve
    beta = fresh / gamma
    alpha_next = fresh / (energy + 2.0 * beta * cross + beta * beta * curve)
    for t in range(tiles):
        spread = pl.ds(t * BLOCKS, params, stride=tiles * BLOCKS)
        begin, vector, change = start[spread, :], step[spread, :], first[spread, :]
        terms = sums[pl.ds(t, params, stride=tiles), :]
        damping, unweigh = (
            own[pl.ds(which * per + t, params, stride=tiles), :] for which in (DAMPING, UNWEIGH)
        )
        direction = vector + beta * begin
        image = jnp.where(unweigh > 0.0, damping * vector + terms, 0.0)
        image = image + beta * (unweigh * change)
        lanes = slice(t * LANES, (t + 1) * LANES)
        solution[:, lanes] = alpha * begin + alpha_next * direction
        residual[:, lanes] = unweigh * vector - alpha_next * image


def chunk_sum(received):
    total = received[0:8, :]
    for at in range(8, received.shape[0], 8):
        total = total + received[at : at + 8, :]
    return total[0:BLOCKS] + total[BLOCKS:]


def own_rows(own):
    per = own.shape[0] // 5
    at = jnp.minimum(pts_index(), per - 1)
    return [own[pl.ds(which * per + at, 1), :] for which in (WEIGHTS, PULL)]


def spread_kernel(received, own, send):
    total = chunk_sum(received)
    owners = send.shape[0] // BLOCKS
    mine, after, before, across = (total[b : b + 1] for b in range(BLOCKS))
    zero = jnp.zeros((1, LANES), F32)
    rows = own_rows(own)
    half = owners // 2
    parts = {
        0: (mine, after, before, across),
        1: (after, mine, *rows),
        -1: (before, mine, *rows),
        half: (across, mine, *rows),
        2: (after, zero, zero, zero),
        -2: (before, zero, zero, zero),
        half - 1: (across, before, zero, zero),
        half + 1: (across, after, zero, zero),
    }
    is_sums = pts_index() < own.shape[0] // 5
    twice = jnp.concatenate([total, total], axis=0)
    for at in range(0, send.shape[0], 8):
        send[at : at + 8, :] = jnp.where(is_sums, 0.0, twice)

    @pl.when(is_sums)
    def _():
        for shift, value in parts.items():
            spot = lax.rem(cam_index() + shift + owners, owners) * BLOCKS
            send[pl.ds(spot, BLOCKS), :] = jnp.concatenate(value, axis=0)


def combine_kernel(received, own, send):
    owners = received.shape[0] // BLOCKS
    half = owners // 2
    me = cam_index()

    def row(shift, at):
        spot = lax.rem(me + shift + owners, owners) * BLOCKS + at
        return received[pl.ds(spot, 1), :]

    sums = (
        (row(0, 0) + row(-1, 0)) + (row(1, 0) + row(half, 0)),
        (row(1, 1) + row(0, 1)) + (row(2, 0) + row(half + 1, 0)),
        (row(-1, 1) + row(-2, 0)) + (row(0, 2) + row(half - 1, 0)),
        (row(half, 1) + row(half - 1, 1)) + (row(half + 1, 1) + row(0, 3)),
    )
    joined = []
    for block, shift in enumerate((0, 1, -1, half)):
        weights, pull = (row(shift, 2), row(shift, 3)) if block else own_rows(own)
        joined.append(pull + weights * sums[block])
    joined = jnp.concatenate(joined, axis=0)
    total = received[0:8, :]
    for at in range(8, received.shape[0], 8):
        total = total + received[at : at + 8, :]
    total = total[0:BLOCKS] + total[BLOCKS:]
    joined = jnp.where(pts_index() < own.shape[0] // 5, joined, total)
    joined = jnp.concatenate([joined, joined], axis=0)
    for at in range(0, send.shape[0], 8):
        send[at : at + 8, :] = joined


def call(kernel, outs, *args, scratch=(), name=None):
    single = not isinstance(outs, list)
    return pl.pallas_call(
        kernel,
        out_shape=outs,
        in_specs=[VMEM] * len(args),
        out_specs=VMEM if single else [VMEM] * len(outs),
        scratch_shapes=list(scratch),
        compiler_params=PARAMS,
        name=name,
    )(*args)


def swap(value, axes, tile=BLOCKS):
    size = lax.axis_size(axes)
    rows = value.shape[0] // size
    chunks = value.reshape(size, rows // tile, tile, LANES)
    return lax.all_to_all(chunks, axes, 0, 0).reshape(value.shape)


def on_device(right_side, camera_damping, preconditioner, jac_cam, jac_pt, camera_index,
              point_index, point_damping, anchors):
    params, width = right_side.shape
    pts, cam = ("xa", "xb", "y"), ("z", "core")
    near, wide, last = ("xb", "y", "core"), ("xa", "z"), ("xb", "y")
    owners, rows = lax.axis_size(cam), lax.axis_size(pts)
    per = params * width // LANES
    count = camera_index.shape[1]
    jac_cam, jac_pt = jac_cam[0], jac_pt[0]
    share = 1.0 / rows

    tiles = width // LANES
    mine = preconditioner.reshape(params, tiles, LANES) * right_side.reshape(params, tiles, LANES)
    shifts = (0, 1, -1, owners // 2)
    after, before, across = (
        lax.ppermute(mine, cam, [(i, (i - d) % owners) for i in range(owners)])
        for d in shifts[1:]
    )
    firsts = (cam_index() + jnp.array(shifts) + owners) % owners * width
    ids = firsts[:, None] + jnp.arange(width, dtype=jnp.int32)[None]
    keep = 1.0 - jnp.any(anchors[:, None, None] == ids[None], axis=0).astype(F32)
    folds = [
        jax.ShapeDtypeStruct((count_of * FOLDS, CHUNK), kind)
        for count_of, kind in ((6, F32), (8, F32), (6, F32), (1, jnp.int32), (1, jnp.int32))
    ]
    inverse, masks, folded, lane, slot, own = call(
        functools.partial(setup_kernel, owners),
        folds + [jax.ShapeDtypeStruct((5 * per, LANES), F32)],
        jac_pt, point_index, point_damping[0], camera_index, right_side, camera_damping,
        preconditioner, keep[:1], name="invert",
    )
    fixed = (jac_cam, folded, lane, slot, masks, inverse)
    half = width // (2 * LANES)
    scratch = (pltpu.VMEM((half * LANES, count), BF16), pltpu.VMEM((2 * FOLDS, CHUNK), F32))
    sums = jax.ShapeDtypeStruct((rows * BLOCKS, LANES), F32)
    vector = jax.ShapeDtypeStruct((per * BLOCKS, LANES), F32)

    send, start = call(
        functools.partial(first_kernel, share), [sums, vector],
        mine, after, before, across, keep, own, *fixed, scratch=scratch, name="apply_first",
    )
    chunks = swap(send, pts)
    shape = jax.ShapeDtypeStruct((owners * BLOCKS, LANES), F32)
    chunks = call(spread_kernel, shape, chunks, own, name="spread")
    chunks = swap(chunks, cam)
    chunks = call(combine_kernel, sums, chunks, own, name="combine")
    first = swap(chunks, pts)

    chunked = jax.ShapeDtypeStruct((lax.axis_size(near) * PAIR, LANES), F32)
    send, step = call(
        functools.partial(second_kernel, share), [chunked, vector], first, start, own, *fixed,
        scratch=(pltpu.VMEM(vector.shape, F32), *scratch), name="apply_second",
    )
    chunks = swap(send, near, 1)
    shape = jax.ShapeDtypeStruct((lax.axis_size(wide) * OWN, LANES), F32)
    chunks = call(own_block_kernel, shape, chunks, name="own_block")
    chunks = swap(chunks, wide, 1)
    shape = jax.ShapeDtypeStruct((lax.axis_size(last) * OWN, LANES), F32)
    chunks = call(own_sum_kernel, shape, chunks, name="own_sum")
    second = swap(chunks, last, 1)
    shape = jax.ShapeDtypeStruct((params, width), F32)
    return tuple(
        call(
            last_kernel, [shape, shape], first, second, start, step, own,
            scratch=[pltpu.VMEM((per, LANES), F32)], name="finish",
        )
    )


def solution(mesh):
    cores = 2
    high = mesh.shape["cam"] // cores
    side = int(mesh.shape["pts"] ** 0.5)
    grid = mesh.devices.reshape(side // 2, 2, mesh.shape["pts"] // side, high, cores)
    cam, whole = ("z", "core"), ("xa", "xb", "y", "z", "core")
    mesh = Mesh(grid, whole)
    return jax.shard_map(
        on_device,
        mesh=mesh,
        in_specs=(
            P(None, cam),
            P(None, cam),
            P(None, cam),
            P(whole, None, None),
            P(whole, None, None),
            P(whole, None),
            P(whole, None),
            P(whole, None, None),
            P(),
        ),
        out_specs=(P(None, cam), P(None, cam)),
        check_vma=False,
    )
```

```python
import functools

import jax
import jax.numpy as jnp
from jax import lax
from jax.experimental import pallas as pl
from jax.experimental.pallas import tpu as pltpu
from jax.sharding import Mesh, PartitionSpec as P

LANES = 128
BLOCKS = 4
STEPS = (1, 2, 4, 8)
CHUNK = 512
FOLDS = 8
QUARTER = 32
PAIR = 5
OWN = 3
TRIPLE = 7
WIDE = 10
FIRST_SCALARS = 96
SCALARS = 64
F32, BF16 = jnp.float32, jnp.bfloat16
VMEM = pl.BlockSpec(memory_space=pltpu.VMEM)
PARAMS = pltpu.CompilerParams(vmem_limit_bytes=40 * 1024 * 1024)


def one_hot(row, count):
    ids = lax.broadcasted_iota(jnp.int32, (count, row.shape[1]), 0)
    return jnp.where(ids == row, 1.0, 0.0)


def cam_index():
    return lax.axis_index("z") * 2 + lax.axis_index("core")


def pts_index():
    x = lax.axis_index("xa") * 2 + lax.axis_index("xb")
    return x * lax.axis_size("y") + lax.axis_index("y")


def short_one_hot(row, count):
    ids = lax.broadcasted_iota(jnp.int16, (count, row.shape[1]), 0)
    return jnp.where(ids == row.astype(jnp.int16), BF16(1), BF16(0))


def fold(ref, row):
    parts = [ref[row : row + 1, i * CHUNK : (i + 1) * CHUNK] for i in range(FOLDS)]
    return jnp.concatenate(parts, axis=0)


def shifted(value, step):
    ids = lax.broadcasted_iota(jnp.int32, value.shape, 1)
    rolled = pltpu.roll(value, step % CHUNK, 1)
    if step > 0:
        return jnp.where(ids < step, pltpu.roll(rolled, 1, 0), rolled)
    return jnp.where(ids >= CHUNK + step, pltpu.roll(rolled, FOLDS - 1, 0), rolled)


def part(ref, index):
    return ref[index * FOLDS : (index + 1) * FOLDS, :]


def point_totals(value, masks):
    before = value
    after = value
    for i, step in enumerate(STEPS):
        before = before + part(masks, i) * shifted(before, step)
        after = after + part(masks, len(STEPS) + i) * shifted(after, -step)
    return before + (after - value)


def setup_kernel(owners, jac_pt, point_ref, damping, camera_ref, right_side, camera_damping,
                 preconditioner, keep, inverse, masks, folded, lane, slot, own):
    width = right_side.shape[1]
    own_arrays(right_side[...], camera_damping[...], preconditioner[...], keep[...], own)
    camera = fold(camera_ref, 0)
    shift = lax.rem(lax.div(camera, width) - cam_index() + owners, owners)
    block = jnp.where(shift == 1, 1, jnp.where(shift == owners - 1, 2, 3))
    block = jnp.where(shift == 0, 0, block)
    inner = lax.rem(camera, width)
    tile = lax.div(inner, LANES)
    lane[...] = lax.div(tile, 2) * LANES + lax.rem(inner, LANES)
    slot[...] = lax.rem(tile, 2) * BLOCKS + block

    point = fold(point_ref, 0)
    for i, step in enumerate(STEPS + tuple(-step for step in STEPS)):
        same = jnp.where(shifted(point, step) == point, 1.0, 0.0)
        masks[i * FOLDS : (i + 1) * FOLDS, :] = same
    rows = [fold(jac_pt, r) for r in range(6)]
    for r in range(6):
        folded[r * FOLDS : (r + 1) * FOLDS, :] = rows[r]
    pairs = [(0, 0), (0, 1), (0, 2), (1, 1), (1, 2), (2, 2)]
    xx, xy, xz, yy, yz, zz = (
        point_totals(rows[a] * rows[b] + rows[3 + a] * rows[3 + b], masks) for a, b in pairs
    )

    tiles = damping.shape[1] // LANES
    table = jnp.concatenate(
        [damping[k : k + 1, t * LANES : (t + 1) * LANES] for k in range(3) for t in range(tiles)],
        axis=0,
    )
    high = table.astype(BF16)
    rest = table - high.astype(F32)
    mid = rest.astype(BF16)
    low = (rest - mid.astype(F32)).astype(BF16)
    damp = [[], [], []]
    for i in range(FOLDS):
        spot = point[i : i + 1]
        hot = short_one_hot(lax.rem(spot, LANES), LANES)
        mask = one_hot(lax.div(spot, LANES), tiles)
        picked = sum(jnp.dot(piece, hot, preferred_element_type=F32) for piece in (high, mid, low))
        for k in range(3):
            damp[k].append(lane_sums(picked[k * tiles : (k + 1) * tiles] * mask))
    damp = [jnp.concatenate(rows_of, axis=0) for rows_of in damp]
    xx, yy, zz = xx + damp[0], yy + damp[1], zz + damp[2]
    cof_xx = yy * zz - yz * yz
    cof_xy = xz * yz - xy * zz
    cof_xz = xy * yz - xz * yy
    cof_yy = xx * zz - xz * xz
    cof_yz = xy * xz - xx * yz
    cof_zz = xx * yy - xy * xy
    det = xx * cof_xx + xy * cof_xy + xz * cof_xz
    for r, cof in enumerate((cof_xx, cof_xy, cof_xz, cof_yy, cof_yz, cof_zz)):
        inverse[r * FOLDS : (r + 1) * FOLDS, :] = cof / det


def lane_sums(value):
    return jnp.sum(value, axis=0, keepdims=True)


def schur(vector, send, jac_cam, folded, lane, slot, masks, inverse, hot, error):
    params = jac_cam.shape[0] // 2
    slots = 2 * BLOCKS
    half = hot.shape[0] // LANES
    rows = params * slots
    table = vector.reshape(params, half, slots, LANES)
    table = jnp.concatenate([table[:, h].reshape(rows, LANES) for h in range(half)], axis=1)
    high = table.astype(BF16)
    low = (table - high.astype(F32)).astype(BF16)
    table = jnp.concatenate([high, low], axis=0)

    for i in range(FOLDS):
        span = slice(i * CHUNK, (i + 1) * CHUNK)
        spot = short_one_hot(lane[i : i + 1, :], half * LANES)
        hot[:, span] = spot
        got = jnp.dot(table, spot, preferred_element_type=F32)
        got = got[:rows] + got[rows:]
        mask = one_hot(slot[i : i + 1, :], slots)
        for r in range(2):
            total = jnp.zeros((slots, CHUNK), F32)
            for a in range(params):
                jac = jac_cam[r * params + a : r * params + a + 1, span]
                total = total + jac * got[a * slots : (a + 1) * slots]
            error[r * FOLDS + i : r * FOLDS + i + 1, :] = lane_sums(total * mask)

    e0, e1 = part(error, 0), part(error, 1)
    jp = [part(folded, r) for r in range(6)]
    inv = [part(inverse, r) for r in range(6)]
    y0, y1, y2 = (point_totals(jp[k] * e0 + jp[3 + k] * e1, masks) for k in range(3))
    z = (
        inv[0] * y0 + inv[1] * y1 + inv[2] * y2,
        inv[1] * y0 + inv[3] * y1 + inv[4] * y2,
        inv[2] * y0 + inv[4] * y1 + inv[5] * y2,
    )
    left0 = e0 - (jp[0] * z[0] + jp[1] * z[1] + jp[2] * z[2])
    left1 = e1 - (jp[3] * z[0] + jp[4] * z[1] + jp[5] * z[2])
    energy = e0 * left0 + e1 * left1

    total = jnp.zeros((2 * rows, half * LANES), F32)
    for i in range(FOLDS):
        span = slice(i * CHUNK, (i + 1) * CHUNK)
        mask = one_hot(slot[i : i + 1, :], slots)
        first, second = mask * left0[i : i + 1], mask * left1[i : i + 1]
        highs, lows = [], []
        for a in range(params):
            value = jac_cam[a : a + 1, span] * first
            value = value + jac_cam[params + a : params + a + 1, span] * second
            near = value.astype(BF16)
            highs.append(near)
            lows.append((value - near.astype(F32)).astype(BF16))
        both = jnp.concatenate(highs + lows, axis=0)
        total = total + lax.dot_general(
            both, hot[:, span], (((1,), (1,)), ((), ())), preferred_element_type=F32
        )
    total = total[:rows] + total[rows:]
    for a in range(params):
        for h in range(half):
            start = (a * half + h) * slots
            send[start : start + slots, :] = total[
                a * slots : (a + 1) * slots, h * LANES : (h + 1) * LANES
            ]
    return lane_sums(sum(energy[:, t * LANES : (t + 1) * LANES] for t in range(CHUNK // LANES)))


RIGHT, DAMPING, WEIGHTS, PULL, UNWEIGH = range(5)


def own_part(own, which):
    per = own.shape[0] // 5
    return own[which * per : (which + 1) * per, :]


def own_arrays(right, damping, precond, keep, own):
    params, width = right.shape
    tiles = width // LANES
    weights = precond * keep
    parts = (right, damping, weights, weights * damping * weights * right, keep / precond)
    for t in range(tiles):
        lanes = slice(t * LANES, (t + 1) * LANES)
        for which, value in enumerate(parts):
            place = pl.ds(which * params * tiles + t, params, stride=tiles)
            own[place, :] = value[:, lanes]


def lane_ids(rows=1):
    return lax.broadcasted_iota(jnp.int32, (rows, LANES), 1)


def send_pairs(sums, scalars, send):
    ids = lane_ids()
    extra = jnp.zeros((1, LANES), F32)
    for index, row in enumerate(scalars):
        extra = jnp.where(ids == SCALARS + index, jnp.sum(row, axis=1, keepdims=True), extra)
    odd = lax.axis_index("core") == 1
    for chunk in range(16):
        q, i = chunk // 4, chunk % 4
        thirds = sums[(32 + q) * BLOCKS : (33 + q) * BLOCKS, :]
        low = pltpu.roll(thirds, (-QUARTER * i) % LANES, 1) if i else thirds
        high = pltpu.roll(thirds, (QUARTER - QUARTER * i) % LANES, 1) if i != 1 else thirds
        rows = sums[chunk * 2 * BLOCKS : (chunk + 1) * 2 * BLOCKS, :]

        def two(a, b):
            mixed = jnp.where(ids < SCALARS, high[b : b + 1], extra)
            mixed = jnp.where(ids < QUARTER, low[a : a + 1], mixed)
            pieces = [rows[at : at + 1] for at in (a, BLOCKS + a, b, BLOCKS + b)]
            return jnp.concatenate(pieces + [mixed], axis=0)

        same, other = two(0, 3), two(1, 2)
        base = 2 * chunk * PAIR
        send[base : base + PAIR, :] = jnp.where(odd, other, same)
        send[base + PAIR : base + 2 * PAIR, :] = jnp.where(odd, same, other)


def scalar(row, lane):
    return jnp.sum(jnp.where(lane_ids() == lane, row, 0.0), axis=1, keepdims=True)


def first_kernel(share, mine, after, before, across, keep, own, jac_cam, folded, lane, slot,
                 masks, inverse, send, start, sums, hot, error):
    params, tiles, _ = mine.shape
    for block, ref in enumerate((mine, after, before, across)):
        for t in range(tiles):
            place = pl.ds(t * BLOCKS + block, params, stride=tiles * BLOCKS)
            kept = keep[block : block + 1, t * LANES : (t + 1) * LANES]
            start[place, :] = ref[:, t, :] * kept
    energy = schur(start[...], sums, jac_cam, folded, lane, slot, masks, inverse, hot, error)
    vector = start[pl.ds(0, params * tiles, stride=BLOCKS), :]
    energy = energy + share * lane_sums(own_part(own, DAMPING) * vector * vector)
    gamma = share * lane_sums(own_part(own, RIGHT) * vector)
    send_pairs(sums, (energy, gamma), send)


def unpack(received, change):
    odd = lax.axis_index("core") == 1
    ids = lane_ids()
    for q in range(4):
        thirds = [jnp.zeros((1, LANES), F32)] * BLOCKS
        for i in range(4):
            chunk = 4 * q + i
            even = received[2 * chunk * TRIPLE : (2 * chunk + 1) * TRIPLE, :]
            odds = received[(2 * chunk + 1) * TRIPLE : (2 * chunk + 2) * TRIPLE, :]
            same, other = jnp.where(odd, odds, even), jnp.where(odd, even, odds)
            near = jnp.where(odd, other[2:4], other[0:2])
            far = jnp.where(odd, other[0:2], other[2:4])
            rows = []
            for r in range(2):
                rows += [same[r : r + 1], near[r : r + 1], far[r : r + 1], same[4 + r : 5 + r]]
            change[chunk * 8 : (chunk + 1) * 8, :] = jnp.concatenate(rows, axis=0)

            def moved(row, quarter):
                by = (QUARTER * (i - quarter)) % LANES
                return pltpu.roll(row, by, 1) if by else row

            first, second = moved(other[6:7], 0), moved(other[6:7], 1)
            pieces = (
                moved(same[6:7], 0),
                jnp.where(odd, second, first),
                jnp.where(odd, first, second),
                moved(same[6:7], 2),
            )
            thirds = [jnp.where(ids >= QUARTER * i, p, t) for p, t in zip(pieces, thirds)]
        at = (32 + q) * BLOCKS
        change[at : at + BLOCKS, :] = jnp.concatenate(thirds, axis=0)


def second_kernel(share, received, start, own, jac_cam, folded, lane, slot, masks, inverse,
                  send, step, change_ref, sums, hot, error):
    per = start.shape[0] // BLOCKS
    unpack(received, change_ref)
    scalars = received[TRIPLE - 1 : TRIPLE, :]
    alpha = scalar(scalars, FIRST_SCALARS + 1) / scalar(scalars, FIRST_SCALARS)
    step[...] = start[...] - alpha * change_ref[...]
    energy = schur(step[...], sums, jac_cam, folded, lane, slot, masks, inverse, hot, error)
    vector = step[pl.ds(0, per, stride=BLOCKS), :]
    change = change_ref[pl.ds(0, per, stride=BLOCKS), :]
    residual = own_part(own, UNWEIGH) * vector
    energy = energy + share * lane_sums(own_part(own, DAMPING) * vector * vector)
    fresh = share * lane_sums(residual * vector)
    cross = share * lane_sums(residual * change)
    send_pairs(sums, (energy, fresh, cross), send)


def own_block_kernel(received, send):
    same, other = core_sums(received)
    own, beside, across = three_blocks(same, other)
    scalars = same[PAIR - 1 : PAIR] + other[PAIR - 1 : PAIR]
    is_third = lax.broadcasted_iota(jnp.int32, (OWN, LANES), 0) == OWN - 1
    is_rest = jnp.logical_and(is_third, lane_ids(OWN) >= SCALARS)

    def with_scalars(value):
        return jnp.where(is_rest, scalars, value)

    size = lax.axis_size("z")
    columns = send.shape[0] // (size * OWN)
    nothing = with_scalars(jnp.zeros((OWN, LANES), F32))
    for spot in range(columns * size):
        send[spot * OWN : (spot + 1) * OWN, :] = nothing
    step = 1 - 2 * lax.axis_index("core")
    for shift, value in ((0, own), (step, beside), (size // 2, across)):
        place = lax.rem(lax.axis_index("z") + shift + size, size)
        value = with_scalars(value)
        for x in range(columns):
            send[pl.ds((x * size + place) * OWN, OWN), :] = value


def own_sum_kernel(received, send):
    total = received[0:OWN, :]
    for source in range(1, received.shape[0] // OWN):
        total = total + received[source * OWN : (source + 1) * OWN, :]
    for spot in range(send.shape[0] // OWN):
        send[spot * OWN : (spot + 1) * OWN, :] = total


def last_kernel(first, second, start, step, change_ref, own, solution, residual, sums):
    params, width = solution.shape
    tiles = width // LANES
    per = params * tiles
    ids = lane_ids()
    for chunk in range(16):
        sums[2 * chunk : 2 * chunk + 2, :] = second[chunk * OWN : chunk * OWN + 2, :]
    for q in range(4):
        third = jnp.zeros((1, LANES), F32)
        for i in range(4):
            at = (4 * q + i) * OWN + 2
            row = second[at : at + 1, :]
            row = pltpu.roll(row, QUARTER * i, 1) if i else row
            third = jnp.where(ids >= QUARTER * i, row, third)
        sums[32 + q : 33 + q, :] = third

    row = first[TRIPLE - 1 : TRIPLE, :]
    curve, gamma = scalar(row, FIRST_SCALARS), scalar(row, FIRST_SCALARS + 1)
    row = second[OWN - 1 : OWN, :]
    energy, fresh, cross = (scalar(row, SCALARS + i) for i in range(3))
    alpha = gamma / curve
    beta = fresh / gamma
    alpha_next = fresh / (energy + 2.0 * beta * cross + beta * beta * curve)
    for t in range(tiles):
        spread = pl.ds(t * BLOCKS, params, stride=tiles * BLOCKS)
        begin, vector, change = start[spread, :], step[spread, :], change_ref[spread, :]
        terms = sums[pl.ds(t, params, stride=tiles), :]
        damping, unweigh = (
            own[pl.ds(which * per + t, params, stride=tiles), :] for which in (DAMPING, UNWEIGH)
        )
        direction = vector + beta * begin
        image = jnp.where(unweigh > 0.0, damping * vector + terms, 0.0)
        image = image + beta * (unweigh * change)
        lanes = slice(t * LANES, (t + 1) * LANES)
        solution[:, lanes] = alpha * begin + alpha_next * direction
        residual[:, lanes] = unweigh * vector - alpha_next * image


def core_sums(received):
    evens = received[0:PAIR, :]
    odds = received[PAIR : 2 * PAIR, :]
    for source in range(2, received.shape[0] // PAIR, 2):
        evens = evens + received[source * PAIR : (source + 1) * PAIR, :]
        odds = odds + received[(source + 1) * PAIR : (source + 2) * PAIR, :]
    odd = lax.axis_index("core") == 1
    return jnp.where(odd, odds, evens), jnp.where(odd, evens, odds)


def three_blocks(same, other):
    odd = lax.axis_index("core") == 1

    def block(value, which):
        third = value[PAIR - 1 : PAIR]
        if which:
            third = pltpu.roll(third, LANES - QUARTER, 1)
        return jnp.concatenate([value[2 * which : 2 * which + 2], third], axis=0)

    first, second = block(other, 0), block(other, 1)
    own = block(same, 0) + jnp.where(odd, first, second)
    return own, jnp.where(odd, second, first), block(same, 1)


def own_rows(own):
    per = own.shape[0] // 5
    chunk = lax.axis_index("xb") * lax.axis_size("y") + lax.axis_index("y")
    found = []
    for which in (WEIGHTS, PULL):
        two = own[pl.ds(which * per + 2 * chunk, 2), :]
        third = own[pl.ds(which * per + 32 + lax.div(chunk, 4), 1), :]
        turned = third
        for i in range(1, 4):
            moved = pltpu.roll(third, LANES - QUARTER * i, 1)
            turned = jnp.where(lax.rem(chunk, 4) == i, moved, turned)
        found.append(jnp.concatenate([two, turned], axis=0))
    return found


def spread_kernel(received, own, send):
    same, other = core_sums(received)
    mine, beside, across = three_blocks(same, other)
    weights, pull = own_rows(own)
    scalars = same[PAIR - 1 : PAIR] + other[PAIR - 1 : PAIR]
    scalars = jnp.where(lane_ids() >= SCALARS, scalars, 0.0)
    zero = jnp.zeros((OWN, LANES), F32)
    ids = lane_ids()

    def joined(*units):
        units = units + (zero,) * (BLOCKS - len(units))
        mixed = units[0][2:3]
        for u in range(1, BLOCKS):
            mixed = jnp.where(ids >= QUARTER * u, pltpu.roll(units[u][2:3], QUARTER * u, 1), mixed)
        return jnp.concatenate([unit[0:2] for unit in units] + [mixed, scalars], axis=0)

    size = lax.axis_size("z")
    columns = send.shape[0] // (size * WIDE)
    nothing = joined()
    for spot in range(columns * size):
        send[spot * WIDE : (spot + 1) * WIDE, :] = nothing
    step = 1 - 2 * lax.axis_index("core")
    half = size // 2
    parts = (
        (0, joined(mine, beside, across)),
        (step, joined(beside)),
        (half, joined(across, mine, weights, pull)),
        (-step, joined(mine, zero, weights, pull)),
        (half - step, joined(across)),
        (half + step, joined(beside)),
    )
    for shift, value in parts:
        place = lax.rem(lax.axis_index("z") + shift + size, size)
        for x in range(columns):
            send[pl.ds((x * size + place) * WIDE, WIDE), :] = value


def combine_kernel(received, own, send):
    size = lax.axis_size("z")
    columns = received.shape[0] // (size * WIDE)
    step = 1 - 2 * lax.axis_index("core")
    half = size // 2
    ids = lane_ids()

    def message(shift, x):
        place = lax.rem(lax.axis_index("z") - shift + 2 * size, size)
        return received[pl.ds((x * size + place) * WIDE, WIDE), :]

    def summed(shift):
        total = message(shift, 0)
        for x in range(1, columns):
            total = total + message(shift, x)
        return total

    def unit(value, which):
        third = value[8:9]
        if which:
            third = pltpu.roll(third, LANES - QUARTER * which, 1)
        return jnp.concatenate([value[2 * which : 2 * which + 2], third], axis=0)

    here, over, back = summed(0), summed(half), summed(-step)
    terms = (
        unit(here, 0) + (unit(summed(step), 0) + unit(over, 0)),
        unit(back, 0) + (unit(here, 1) + unit(summed(half - step), 0)),
        unit(over, 1) + (unit(summed(half + step), 0) + unit(here, 2)),
    )
    rows = (
        own_rows(own),
        [unit(message(-step, 0), u) for u in (2, 3)],
        [unit(message(half, 0), u) for u in (2, 3)],
    )
    changes = [pull + weights * term for (weights, pull), term in zip(rows, terms)]
    scalars = received[WIDE - 1 : WIDE, :]
    for source in range(1, received.shape[0] // WIDE):
        scalars = scalars + received[(source + 1) * WIDE - 1 : (source + 1) * WIDE, :]
    mixed = pltpu.roll(scalars, FIRST_SCALARS - SCALARS, 1)
    for u in (2, 1, 0):
        third = changes[u][2:3]
        third = pltpu.roll(third, QUARTER * u, 1) if u else third
        mixed = jnp.where(ids < QUARTER * (u + 1), third, mixed)
    joined = jnp.concatenate([change[0:2] for change in changes] + [mixed], axis=0)
    for spot in range(send.shape[0] // TRIPLE):
        send[spot * TRIPLE : (spot + 1) * TRIPLE, :] = joined


def call(kernel, outs, *args, scratch=(), name=None):
    single = not isinstance(outs, list)
    return pl.pallas_call(
        kernel,
        out_shape=outs,
        in_specs=[VMEM] * len(args),
        out_specs=VMEM if single else [VMEM] * len(outs),
        scratch_shapes=list(scratch),
        compiler_params=PARAMS,
        name=name,
    )(*args)


def swap(value, axes, tile=BLOCKS):
    size = lax.axis_size(axes)
    rows = value.shape[0] // size
    chunks = value.reshape(size, rows // tile, tile, LANES)
    return lax.all_to_all(chunks, axes, 0, 0).reshape(value.shape)


def on_device(right_side, camera_damping, preconditioner, jac_cam, jac_pt, camera_index,
              point_index, point_damping, anchors):
    params, width = right_side.shape
    pts, cam = ("xa", "xb", "y"), ("z", "core")
    near, wide, last = ("xb", "y", "core"), ("xa", "z"), ("xb", "y")
    owners, rows = lax.axis_size(cam), lax.axis_size(pts)
    per = params * width // LANES
    count = camera_index.shape[1]
    jac_cam, jac_pt = jac_cam[0], jac_pt[0]
    share = 1.0 / rows

    tiles = width // LANES
    mine = preconditioner.reshape(params, tiles, LANES) * right_side.reshape(params, tiles, LANES)
    shifts = (0, 1, -1, owners // 2)
    after, before, across = (
        lax.ppermute(mine, cam, [(i, (i - d) % owners) for i in range(owners)])
        for d in shifts[1:]
    )
    firsts = (cam_index() + jnp.array(shifts) + owners) % owners * width
    ids = firsts[:, None] + jnp.arange(width, dtype=jnp.int32)[None]
    keep = 1.0 - jnp.any(anchors[:, None, None] == ids[None], axis=0).astype(F32)
    folds = [
        jax.ShapeDtypeStruct((count_of * FOLDS, CHUNK), kind)
        for count_of, kind in ((6, F32), (8, F32), (6, F32), (1, jnp.int32), (1, jnp.int32))
    ]
    inverse, masks, folded, lane, slot, own = call(
        functools.partial(setup_kernel, owners),
        folds + [jax.ShapeDtypeStruct((5 * per, LANES), F32)],
        jac_pt, point_index, point_damping[0], camera_index, right_side, camera_damping,
        preconditioner, keep[:1], name="invert",
    )
    fixed = (jac_cam, folded, lane, slot, masks, inverse)
    half = width // (2 * LANES)
    scratch = (pltpu.VMEM((half * LANES, count), BF16), pltpu.VMEM((2 * FOLDS, CHUNK), F32))
    vector = jax.ShapeDtypeStruct((per * BLOCKS, LANES), F32)
    chunked = jax.ShapeDtypeStruct((lax.axis_size(near) * PAIR, LANES), F32)
    scratch = (pltpu.VMEM(vector.shape, F32), *scratch)

    send, start = call(
        functools.partial(first_kernel, share), [chunked, vector],
        mine, after, before, across, keep, own, *fixed, scratch=scratch, name="apply_first",
    )
    chunks = swap(send, near, 1)
    shape = jax.ShapeDtypeStruct((lax.axis_size(wide) * WIDE, LANES), F32)
    chunks = call(spread_kernel, shape, chunks, own, name="spread")
    chunks = swap(chunks, wide, 1)
    shape = jax.ShapeDtypeStruct((lax.axis_size(near) * TRIPLE, LANES), F32)
    chunks = call(combine_kernel, shape, chunks, own, name="combine")
    first = swap(chunks, near, 1)

    send, step, change = call(
        functools.partial(second_kernel, share), [chunked, vector, vector], first, start, own,
        *fixed, scratch=scratch, name="apply_second",
    )
    chunks = swap(send, near, 1)
    shape = jax.ShapeDtypeStruct((lax.axis_size(wide) * OWN, LANES), F32)
    chunks = call(own_block_kernel, shape, chunks, name="own_block")
    chunks = swap(chunks, wide, 1)
    shape = jax.ShapeDtypeStruct((lax.axis_size(last) * OWN, LANES), F32)
    chunks = call(own_sum_kernel, shape, chunks, name="own_sum")
    second = swap(chunks, last, 1)
    shape = jax.ShapeDtypeStruct((params, width), F32)
    return tuple(
        call(
            last_kernel, [shape, shape], first, second, start, step, change, own,
            scratch=[pltpu.VMEM((per, LANES), F32)], name="finish",
        )
    )


def solution(mesh):
    cores = 2
    high = mesh.shape["cam"] // cores
    side = int(mesh.shape["pts"] ** 0.5)
    grid = mesh.devices.reshape(side // 2, 2, mesh.shape["pts"] // side, high, cores)
    cam, whole = ("z", "core"), ("xa", "xb", "y", "z", "core")
    mesh = Mesh(grid, whole)
    return jax.shard_map(
        on_device,
        mesh=mesh,
        in_specs=(
            P(None, cam),
            P(None, cam),
            P(None, cam),
            P(whole, None, None),
            P(whole, None, None),
            P(whole, None),
            P(whole, None),
            P(whole, None, None),
            P(),
        ),
        out_specs=(P(None, cam), P(None, cam)),
        check_vma=False,
    )
```

```python
import functools

import jax
import jax.numpy as jnp
from jax import lax
from jax.experimental import pallas as pl
from jax.experimental.pallas import tpu as pltpu
from jax.sharding import Mesh, PartitionSpec as P

LANES = 128
BLOCKS = 4
STEPS = (1, 2, 4, 8)
CHUNK = 512
FOLDS = 8
QUARTER = 32
PAIR = 5
OWN = 3
TRIPLE = 7
FIRST_SCALARS = 96
SCALARS = 64
F32, BF16 = jnp.float32, jnp.bfloat16
VMEM = pl.BlockSpec(memory_space=pltpu.VMEM)
PARAMS = pltpu.CompilerParams(vmem_limit_bytes=40 * 1024 * 1024)


def one_hot(row, count):
    ids = lax.broadcasted_iota(jnp.int32, (count, row.shape[1]), 0)
    return jnp.where(ids == row, 1.0, 0.0)


def cam_index():
    return lax.axis_index("z") * 2 + lax.axis_index("core")


def pts_index():
    x = lax.axis_index("xa") * 2 + lax.axis_index("xb")
    return x * lax.axis_size("y") + lax.axis_index("y")


def short_one_hot(row, count):
    ids = lax.broadcasted_iota(jnp.int16, (count, row.shape[1]), 0)
    return jnp.where(ids == row.astype(jnp.int16), BF16(1), BF16(0))


def fold(ref, row):
    parts = [ref[row : row + 1, i * CHUNK : (i + 1) * CHUNK] for i in range(FOLDS)]
    return jnp.concatenate(parts, axis=0)


def shifted(value, step):
    ids = lax.broadcasted_iota(jnp.int32, value.shape, 1)
    rolled = pltpu.roll(value, step % CHUNK, 1)
    if step > 0:
        return jnp.where(ids < step, pltpu.roll(rolled, 1, 0), rolled)
    return jnp.where(ids >= CHUNK + step, pltpu.roll(rolled, FOLDS - 1, 0), rolled)


def part(ref, index):
    return ref[index * FOLDS : (index + 1) * FOLDS, :]


def point_totals(value, masks):
    before = value
    after = value
    for i, step in enumerate(STEPS):
        before = before + part(masks, i) * shifted(before, step)
        after = after + part(masks, len(STEPS) + i) * shifted(after, -step)
    return before + (after - value)


def setup_kernel(owners, jac_pt, point_ref, damping, camera_ref, right_side, camera_damping,
                 preconditioner, keep, inverse, masks, folded, lane, slot, own):
    width = right_side.shape[1]
    own_arrays(right_side[...], camera_damping[...], preconditioner[...], keep[...], own)
    camera = fold(camera_ref, 0)
    shift = lax.rem(lax.div(camera, width) - cam_index() + owners, owners)
    block = jnp.where(shift == 1, 1, jnp.where(shift == owners - 1, 2, 3))
    block = jnp.where(shift == 0, 0, block)
    inner = lax.rem(camera, width)
    tile = lax.div(inner, LANES)
    lane[...] = lax.div(tile, 2) * LANES + lax.rem(inner, LANES)
    slot[...] = lax.rem(tile, 2) * BLOCKS + block

    point = fold(point_ref, 0)
    for i, step in enumerate(STEPS + tuple(-step for step in STEPS)):
        same = jnp.where(shifted(point, step) == point, 1.0, 0.0)
        masks[i * FOLDS : (i + 1) * FOLDS, :] = same
    rows = [fold(jac_pt, r) for r in range(6)]
    for r in range(6):
        folded[r * FOLDS : (r + 1) * FOLDS, :] = rows[r]
    pairs = [(0, 0), (0, 1), (0, 2), (1, 1), (1, 2), (2, 2)]
    xx, xy, xz, yy, yz, zz = (
        point_totals(rows[a] * rows[b] + rows[3 + a] * rows[3 + b], masks) for a, b in pairs
    )

    tiles = damping.shape[1] // LANES
    table = jnp.concatenate(
        [damping[k : k + 1, t * LANES : (t + 1) * LANES] for k in range(3) for t in range(tiles)],
        axis=0,
    )
    high = table.astype(BF16)
    rest = table - high.astype(F32)
    mid = rest.astype(BF16)
    low = (rest - mid.astype(F32)).astype(BF16)
    damp = [[], [], []]
    for i in range(FOLDS):
        spot = point[i : i + 1]
        hot = short_one_hot(lax.rem(spot, LANES), LANES)
        mask = one_hot(lax.div(spot, LANES), tiles)
        picked = sum(jnp.dot(piece, hot, preferred_element_type=F32) for piece in (high, mid, low))
        for k in range(3):
            damp[k].append(lane_sums(picked[k * tiles : (k + 1) * tiles] * mask))
    damp = [jnp.concatenate(rows_of, axis=0) for rows_of in damp]
    xx, yy, zz = xx + damp[0], yy + damp[1], zz + damp[2]
    cof_xx = yy * zz - yz * yz
    cof_xy = xz * yz - xy * zz
    cof_xz = xy * yz - xz * yy
    cof_yy = xx * zz - xz * xz
    cof_yz = xy * xz - xx * yz
    cof_zz = xx * yy - xy * xy
    det = xx * cof_xx + xy * cof_xy + xz * cof_xz
    for r, cof in enumerate((cof_xx, cof_xy, cof_xz, cof_yy, cof_yz, cof_zz)):
        inverse[r * FOLDS : (r + 1) * FOLDS, :] = cof / det


def lane_sums(value):
    return jnp.sum(value, axis=0, keepdims=True)


def schur(vector, send, jac_cam, folded, lane, slot, masks, inverse, hot, error):
    params = jac_cam.shape[0] // 2
    slots = 2 * BLOCKS
    half = hot.shape[0] // LANES
    rows = params * slots
    table = vector.reshape(params, half, slots, LANES)
    table = jnp.concatenate([table[:, h].reshape(rows, LANES) for h in range(half)], axis=1)
    high = table.astype(BF16)
    low = (table - high.astype(F32)).astype(BF16)
    table = jnp.concatenate([high, low], axis=0)

    for i in range(FOLDS):
        span = slice(i * CHUNK, (i + 1) * CHUNK)
        spot = short_one_hot(lane[i : i + 1, :], half * LANES)
        hot[:, span] = spot
        got = jnp.dot(table, spot, preferred_element_type=F32)
        got = got[:rows] + got[rows:]
        mask = one_hot(slot[i : i + 1, :], slots)
        for r in range(2):
            total = jnp.zeros((slots, CHUNK), F32)
            for a in range(params):
                jac = jac_cam[r * params + a : r * params + a + 1, span]
                total = total + jac * got[a * slots : (a + 1) * slots]
            error[r * FOLDS + i : r * FOLDS + i + 1, :] = lane_sums(total * mask)

    e0, e1 = part(error, 0), part(error, 1)
    jp = [part(folded, r) for r in range(6)]
    inv = [part(inverse, r) for r in range(6)]
    y0, y1, y2 = (point_totals(jp[k] * e0 + jp[3 + k] * e1, masks) for k in range(3))
    z = (
        inv[0] * y0 + inv[1] * y1 + inv[2] * y2,
        inv[1] * y0 + inv[3] * y1 + inv[4] * y2,
        inv[2] * y0 + inv[4] * y1 + inv[5] * y2,
    )
    left0 = e0 - (jp[0] * z[0] + jp[1] * z[1] + jp[2] * z[2])
    left1 = e1 - (jp[3] * z[0] + jp[4] * z[1] + jp[5] * z[2])
    energy = e0 * left0 + e1 * left1

    total = jnp.zeros((2 * rows, half * LANES), F32)
    for i in range(FOLDS):
        span = slice(i * CHUNK, (i + 1) * CHUNK)
        mask = one_hot(slot[i : i + 1, :], slots)
        first, second = mask * left0[i : i + 1], mask * left1[i : i + 1]
        highs, lows = [], []
        for a in range(params):
            value = jac_cam[a : a + 1, span] * first
            value = value + jac_cam[params + a : params + a + 1, span] * second
            near = value.astype(BF16)
            highs.append(near)
            lows.append((value - near.astype(F32)).astype(BF16))
        both = jnp.concatenate(highs + lows, axis=0)
        total = total + lax.dot_general(
            both, hot[:, span], (((1,), (1,)), ((), ())), preferred_element_type=F32
        )
    total = total[:rows] + total[rows:]
    for a in range(params):
        for h in range(half):
            start = (a * half + h) * slots
            send[start : start + slots, :] = total[
                a * slots : (a + 1) * slots, h * LANES : (h + 1) * LANES
            ]
    return lane_sums(sum(energy[:, t * LANES : (t + 1) * LANES] for t in range(CHUNK // LANES)))


RIGHT, DAMPING, WEIGHTS, PULL, UNWEIGH = range(5)


def own_part(own, which):
    per = own.shape[0] // 5
    return own[which * per : (which + 1) * per, :]


def own_arrays(right, damping, precond, keep, own):
    params, width = right.shape
    tiles = width // LANES
    weights = precond * keep
    parts = (right, damping, weights, weights * damping * weights * right, keep / precond)
    for t in range(tiles):
        lanes = slice(t * LANES, (t + 1) * LANES)
        for which, value in enumerate(parts):
            place = pl.ds(which * params * tiles + t, params, stride=tiles)
            own[place, :] = value[:, lanes]


def lane_ids(rows=1):
    return lax.broadcasted_iota(jnp.int32, (rows, LANES), 1)


def send_pairs(sums, scalars, send):
    ids = lane_ids()
    extra = jnp.zeros((1, LANES), F32)
    for index, row in enumerate(scalars):
        extra = jnp.where(ids == SCALARS + index, jnp.sum(row, axis=1, keepdims=True), extra)
    odd = lax.axis_index("core") == 1
    for chunk in range(16):
        q, i = chunk // 4, chunk % 4
        thirds = sums[(32 + q) * BLOCKS : (33 + q) * BLOCKS, :]
        low = pltpu.roll(thirds, (-QUARTER * i) % LANES, 1) if i else thirds
        high = pltpu.roll(thirds, (QUARTER - QUARTER * i) % LANES, 1) if i != 1 else thirds
        rows = sums[chunk * 2 * BLOCKS : (chunk + 1) * 2 * BLOCKS, :]

        def two(a, b):
            mixed = jnp.where(ids < SCALARS, high[b : b + 1], extra)
            mixed = jnp.where(ids < QUARTER, low[a : a + 1], mixed)
            pieces = [rows[at : at + 1] for at in (a, BLOCKS + a, b, BLOCKS + b)]
            return jnp.concatenate(pieces + [mixed], axis=0)

        same, other = two(0, 3), two(1, 2)
        base = 2 * chunk * PAIR
        send[base : base + PAIR, :] = jnp.where(odd, other, same)
        send[base + PAIR : base + 2 * PAIR, :] = jnp.where(odd, same, other)


def scalar(row, lane):
    return jnp.sum(jnp.where(lane_ids() == lane, row, 0.0), axis=1, keepdims=True)


def first_kernel(share, mine, after, before, across, keep, own, jac_cam, folded, lane, slot,
                 masks, inverse, send, start, sums, hot, error):
    params, tiles, _ = mine.shape
    for block, ref in enumerate((mine, after, before, across)):
        for t in range(tiles):
            place = pl.ds(t * BLOCKS + block, params, stride=tiles * BLOCKS)
            kept = keep[block : block + 1, t * LANES : (t + 1) * LANES]
            start[place, :] = ref[:, t, :] * kept
    energy = schur(start[...], sums, jac_cam, folded, lane, slot, masks, inverse, hot, error)
    vector = start[pl.ds(0, params * tiles, stride=BLOCKS), :]
    energy = energy + share * lane_sums(own_part(own, DAMPING) * vector * vector)
    gamma = share * lane_sums(own_part(own, RIGHT) * vector)
    send_pairs(sums, (energy, gamma), send)


def unpack(received, change):
    odd = lax.axis_index("core") == 1
    ids = lane_ids()
    for q in range(4):
        thirds = [jnp.zeros((1, LANES), F32)] * BLOCKS
        for i in range(4):
            chunk = 4 * q + i
            even = received[2 * chunk * TRIPLE : (2 * chunk + 1) * TRIPLE, :]
            odds = received[(2 * chunk + 1) * TRIPLE : (2 * chunk + 2) * TRIPLE, :]
            same, other = jnp.where(odd, odds, even), jnp.where(odd, even, odds)
            near = jnp.where(odd, other[2:4], other[0:2])
            far = jnp.where(odd, other[0:2], other[2:4])
            rows = []
            for r in range(2):
                rows += [same[r : r + 1], near[r : r + 1], far[r : r + 1], same[4 + r : 5 + r]]
            change[chunk * 8 : (chunk + 1) * 8, :] = jnp.concatenate(rows, axis=0)

            def moved(row, quarter):
                by = (QUARTER * (i - quarter)) % LANES
                return pltpu.roll(row, by, 1) if by else row

            first, second = moved(other[6:7], 0), moved(other[6:7], 1)
            pieces = (
                moved(same[6:7], 0),
                jnp.where(odd, second, first),
                jnp.where(odd, first, second),
                moved(same[6:7], 2),
            )
            thirds = [jnp.where(ids >= QUARTER * i, p, t) for p, t in zip(pieces, thirds)]
        at = (32 + q) * BLOCKS
        change[at : at + BLOCKS, :] = jnp.concatenate(thirds, axis=0)


def second_kernel(share, received, start, own, jac_cam, folded, lane, slot, masks, inverse,
                  send, step, change_ref, sums, hot, error):
    per = start.shape[0] // BLOCKS
    unpack(received, change_ref)
    scalars = received[TRIPLE - 1 : TRIPLE, :]
    alpha = scalar(scalars, FIRST_SCALARS + 1) / scalar(scalars, FIRST_SCALARS)
    step[...] = start[...] - alpha * change_ref[...]
    energy = schur(step[...], sums, jac_cam, folded, lane, slot, masks, inverse, hot, error)
    vector = step[pl.ds(0, per, stride=BLOCKS), :]
    change = change_ref[pl.ds(0, per, stride=BLOCKS), :]
    residual = own_part(own, UNWEIGH) * vector
    energy = energy + share * lane_sums(own_part(own, DAMPING) * vector * vector)
    fresh = share * lane_sums(residual * vector)
    cross = share * lane_sums(residual * change)
    send_pairs(sums, (energy, fresh, cross), send)


def own_block_kernel(received, send):
    same, other = core_sums(received)
    own, beside, across = three_blocks(same, other)
    scalars = same[PAIR - 1 : PAIR] + other[PAIR - 1 : PAIR]
    is_third = lax.broadcasted_iota(jnp.int32, (OWN, LANES), 0) == OWN - 1
    is_rest = jnp.logical_and(is_third, lane_ids(OWN) >= SCALARS)

    def with_scalars(value):
        return jnp.where(is_rest, scalars, value)

    size = lax.axis_size("z")
    columns = send.shape[0] // (size * OWN)
    nothing = with_scalars(jnp.zeros((OWN, LANES), F32))
    for spot in range(columns * size):
        send[spot * OWN : (spot + 1) * OWN, :] = nothing
    step = 1 - 2 * lax.axis_index("core")
    for shift, value in ((0, own), (step, beside), (size // 2, across)):
        place = lax.rem(lax.axis_index("z") + shift + size, size)
        value = with_scalars(value)
        for x in range(columns):
            send[pl.ds((x * size + place) * OWN, OWN), :] = value


def own_sum_kernel(received, send):
    total = received[0:OWN, :]
    for source in range(1, received.shape[0] // OWN):
        total = total + received[source * OWN : (source + 1) * OWN, :]
    for spot in range(send.shape[0] // OWN):
        send[spot * OWN : (spot + 1) * OWN, :] = total


def last_kernel(first, second, start, step, change_ref, own, solution, residual, sums):
    params, width = solution.shape
    tiles = width // LANES
    per = params * tiles
    ids = lane_ids()
    for chunk in range(16):
        sums[2 * chunk : 2 * chunk + 2, :] = second[chunk * OWN : chunk * OWN + 2, :]
    for q in range(4):
        third = jnp.zeros((1, LANES), F32)
        for i in range(4):
            at = (4 * q + i) * OWN + 2
            row = second[at : at + 1, :]
            row = pltpu.roll(row, QUARTER * i, 1) if i else row
            third = jnp.where(ids >= QUARTER * i, row, third)
        sums[32 + q : 33 + q, :] = third

    row = first[TRIPLE - 1 : TRIPLE, :]
    curve, gamma = scalar(row, FIRST_SCALARS), scalar(row, FIRST_SCALARS + 1)
    row = second[OWN - 1 : OWN, :]
    energy, fresh, cross = (scalar(row, SCALARS + i) for i in range(3))
    alpha = gamma / curve
    beta = fresh / gamma
    alpha_next = fresh / (energy + 2.0 * beta * cross + beta * beta * curve)
    for t in range(tiles):
        spread = pl.ds(t * BLOCKS, params, stride=tiles * BLOCKS)
        begin, vector, change = start[spread, :], step[spread, :], change_ref[spread, :]
        terms = sums[pl.ds(t, params, stride=tiles), :]
        damping, unweigh = (
            own[pl.ds(which * per + t, params, stride=tiles), :] for which in (DAMPING, UNWEIGH)
        )
        direction = vector + beta * begin
        image = jnp.where(unweigh > 0.0, damping * vector + terms, 0.0)
        image = image + beta * (unweigh * change)
        lanes = slice(t * LANES, (t + 1) * LANES)
        solution[:, lanes] = alpha * begin + alpha_next * direction
        residual[:, lanes] = unweigh * vector - alpha_next * image


def core_sums(received):
    evens = received[0:PAIR, :]
    odds = received[PAIR : 2 * PAIR, :]
    for source in range(2, received.shape[0] // PAIR, 2):
        evens = evens + received[source * PAIR : (source + 1) * PAIR, :]
        odds = odds + received[(source + 1) * PAIR : (source + 2) * PAIR, :]
    odd = lax.axis_index("core") == 1
    return jnp.where(odd, odds, evens), jnp.where(odd, evens, odds)


def three_blocks(same, other):
    odd = lax.axis_index("core") == 1

    def block(value, which):
        third = value[PAIR - 1 : PAIR]
        if which:
            third = pltpu.roll(third, LANES - QUARTER, 1)
        return jnp.concatenate([value[2 * which : 2 * which + 2], third], axis=0)

    first, second = block(other, 0), block(other, 1)
    own = block(same, 0) + jnp.where(odd, first, second)
    return own, jnp.where(odd, second, first), block(same, 1)


def own_rows(own):
    per = own.shape[0] // 5
    chunk = lax.axis_index("xb") * lax.axis_size("y") + lax.axis_index("y")
    found = []
    for which in (WEIGHTS, PULL):
        two = own[pl.ds(which * per + 2 * chunk, 2), :]
        third = own[pl.ds(which * per + 32 + lax.div(chunk, 4), 1), :]
        turned = third
        for i in range(1, 4):
            moved = pltpu.roll(third, LANES - QUARTER * i, 1)
            turned = jnp.where(lax.rem(chunk, 4) == i, moved, turned)
        found.append(jnp.concatenate([two, turned], axis=0))
    return found


def spread_kernel(received, own, send):
    same, other = core_sums(received)
    mine, beside, across = three_blocks(same, other)
    weights, pull = own_rows(own)
    scalars = same[PAIR - 1 : PAIR] + other[PAIR - 1 : PAIR]
    scalars = pltpu.roll(scalars, FIRST_SCALARS - SCALARS, 1)
    zero = jnp.zeros((OWN, LANES), F32)
    ids = lane_ids()
    size = lax.axis_size("z")
    columns = send.shape[0] // (size * TRIPLE)
    joint = pull * (1.0 / columns) + weights * mine

    def joined(*units):
        units = units + (zero,) * (3 - len(units))
        mixed = units[0][2:3]
        for u in (1, 2):
            mixed = jnp.where(ids >= QUARTER * u, pltpu.roll(units[u][2:3], QUARTER * u, 1), mixed)
        mixed = jnp.where(ids >= FIRST_SCALARS, scalars, mixed)
        return jnp.concatenate([unit[0:2] for unit in units] + [mixed], axis=0)

    nothing = joined()
    for spot in range(columns * size):
        send[spot * TRIPLE : (spot + 1) * TRIPLE, :] = nothing
    step = 1 - 2 * lax.axis_index("core")
    half = size // 2
    parts = (
        (0, joined(mine, beside, across)),
        (step, joined(beside)),
        (half, joined(across, joint, weights)),
        (-step, joined(zero, joint, weights)),
        (half - step, joined(across)),
        (half + step, joined(beside)),
    )
    for shift, value in parts:
        place = lax.rem(lax.axis_index("z") + shift + size, size)
        for x in range(columns):
            send[pl.ds((x * size + place) * TRIPLE, TRIPLE), :] = value


def combine_kernel(received, own, send):
    size = lax.axis_size("z")
    columns = received.shape[0] // (size * TRIPLE)
    step = 1 - 2 * lax.axis_index("core")
    half = size // 2
    ids = lane_ids()

    def message(shift, x):
        place = lax.rem(lax.axis_index("z") - shift + 2 * size, size)
        return received[pl.ds((x * size + place) * TRIPLE, TRIPLE), :]

    def summed(shift):
        total = message(shift, 0)
        for x in range(1, columns):
            total = total + message(shift, x)
        return total

    def unit(value, which):
        third = value[6:7]
        if which:
            third = pltpu.roll(third, LANES - QUARTER * which, 1)
        return jnp.concatenate([value[2 * which : 2 * which + 2], third], axis=0)

    here, over, back = summed(0), summed(half), summed(-step)
    weights, pull = own_rows(own)
    near_weights = unit(message(-step, 0), 2)
    far_weights = unit(message(half, 0), 2)
    changes = (
        pull + weights * (unit(here, 0) + (unit(summed(step), 0) + unit(over, 0))),
        unit(back, 1) + near_weights * (unit(here, 1) + unit(summed(half - step), 0)),
        unit(over, 1) + far_weights * (unit(summed(half + step), 0) + unit(here, 2)),
    )
    mixed = received[TRIPLE - 1 : TRIPLE, :]
    for source in range(1, received.shape[0] // TRIPLE):
        mixed = mixed + received[(source + 1) * TRIPLE - 1 : (source + 1) * TRIPLE, :]
    for u in (2, 1, 0):
        third = changes[u][2:3]
        third = pltpu.roll(third, QUARTER * u, 1) if u else third
        mixed = jnp.where(ids < QUARTER * (u + 1), third, mixed)
    joined = jnp.concatenate([change[0:2] for change in changes] + [mixed], axis=0)
    for spot in range(send.shape[0] // TRIPLE):
        send[spot * TRIPLE : (spot + 1) * TRIPLE, :] = joined


def call(kernel, outs, *args, scratch=(), name=None):
    single = not isinstance(outs, list)
    return pl.pallas_call(
        kernel,
        out_shape=outs,
        in_specs=[VMEM] * len(args),
        out_specs=VMEM if single else [VMEM] * len(outs),
        scratch_shapes=list(scratch),
        compiler_params=PARAMS,
        name=name,
    )(*args)


def swap(value, axes, tile=BLOCKS):
    size = lax.axis_size(axes)
    rows = value.shape[0] // size
    chunks = value.reshape(size, rows // tile, tile, LANES)
    return lax.all_to_all(chunks, axes, 0, 0).reshape(value.shape)


def on_device(right_side, camera_damping, preconditioner, jac_cam, jac_pt, camera_index,
              point_index, point_damping, anchors):
    params, width = right_side.shape
    pts, cam = ("xa", "xb", "y"), ("z", "core")
    near, wide, last = ("xb", "y", "core"), ("xa", "z"), ("xb", "y")
    owners, rows = lax.axis_size(cam), lax.axis_size(pts)
    per = params * width // LANES
    count = camera_index.shape[1]
    jac_cam, jac_pt = jac_cam[0], jac_pt[0]
    share = 1.0 / rows

    tiles = width // LANES
    mine = preconditioner.reshape(params, tiles, LANES) * right_side.reshape(params, tiles, LANES)
    shifts = (0, 1, -1, owners // 2)
    after, before, across = (
        lax.ppermute(mine, cam, [(i, (i - d) % owners) for i in range(owners)])
        for d in shifts[1:]
    )
    firsts = (cam_index() + jnp.array(shifts) + owners) % owners * width
    ids = firsts[:, None] + jnp.arange(width, dtype=jnp.int32)[None]
    keep = 1.0 - jnp.any(anchors[:, None, None] == ids[None], axis=0).astype(F32)
    folds = [
        jax.ShapeDtypeStruct((count_of * FOLDS, CHUNK), kind)
        for count_of, kind in ((6, F32), (8, F32), (6, F32), (1, jnp.int32), (1, jnp.int32))
    ]
    inverse, masks, folded, lane, slot, own = call(
        functools.partial(setup_kernel, owners),
        folds + [jax.ShapeDtypeStruct((5 * per, LANES), F32)],
        jac_pt, point_index, point_damping[0], camera_index, right_side, camera_damping,
        preconditioner, keep[:1], name="invert",
    )
    fixed = (jac_cam, folded, lane, slot, masks, inverse)
    half = width // (2 * LANES)
    scratch = (pltpu.VMEM((half * LANES, count), BF16), pltpu.VMEM((2 * FOLDS, CHUNK), F32))
    vector = jax.ShapeDtypeStruct((per * BLOCKS, LANES), F32)
    chunked = jax.ShapeDtypeStruct((lax.axis_size(near) * PAIR, LANES), F32)
    scratch = (pltpu.VMEM(vector.shape, F32), *scratch)

    send, start = call(
        functools.partial(first_kernel, share), [chunked, vector],
        mine, after, before, across, keep, own, *fixed, scratch=scratch, name="apply_first",
    )
    chunks = swap(send, near, 1)
    shape = jax.ShapeDtypeStruct((lax.axis_size(wide) * TRIPLE, LANES), F32)
    chunks = call(spread_kernel, shape, chunks, own, name="spread")
    chunks = swap(chunks, wide, 1)
    shape = jax.ShapeDtypeStruct((lax.axis_size(near) * TRIPLE, LANES), F32)
    chunks = call(combine_kernel, shape, chunks, own, name="combine")
    first = swap(chunks, near, 1)

    send, step, change = call(
        functools.partial(second_kernel, share), [chunked, vector, vector], first, start, own,
        *fixed, scratch=scratch, name="apply_second",
    )
    chunks = swap(send, near, 1)
    shape = jax.ShapeDtypeStruct((lax.axis_size(wide) * OWN, LANES), F32)
    chunks = call(own_block_kernel, shape, chunks, name="own_block")
    chunks = swap(chunks, wide, 1)
    shape = jax.ShapeDtypeStruct((lax.axis_size(last) * OWN, LANES), F32)
    chunks = call(own_sum_kernel, shape, chunks, name="own_sum")
    second = swap(chunks, last, 1)
    shape = jax.ShapeDtypeStruct((params, width), F32)
    return tuple(
        call(
            last_kernel, [shape, shape], first, second, start, step, change, own,
            scratch=[pltpu.VMEM((per, LANES), F32)], name="finish",
        )
    )


def solution(mesh):
    cores = 2
    high = mesh.shape["cam"] // cores
    side = int(mesh.shape["pts"] ** 0.5)
    grid = mesh.devices.reshape(side // 2, 2, mesh.shape["pts"] // side, high, cores)
    cam, whole = ("z", "core"), ("xa", "xb", "y", "z", "core")
    mesh = Mesh(grid, whole)
    return jax.shard_map(
        on_device,
        mesh=mesh,
        in_specs=(
            P(None, cam),
            P(None, cam),
            P(None, cam),
            P(whole, None, None),
            P(whole, None, None),
            P(whole, None),
            P(whole, None),
            P(whole, None, None),
            P(),
        ),
        out_specs=(P(None, cam), P(None, cam)),
        check_vma=False,
    )
```

```python
import functools

import jax
import jax.numpy as jnp
from jax import lax
from jax.experimental import pallas as pl
from jax.experimental.pallas import tpu as pltpu
from jax.sharding import Mesh, PartitionSpec as P

LANES = 128
BLOCKS = 4
STAGES = ((1, 2, 3), (4, 8, 12))
STEPS = STAGES[0] + STAGES[1]
CHUNK = 512
FOLDS = 8
QUARTER = 32
PAIR = 5
OWN = 3
TRIPLE = 7
FIRST_SCALARS = 96
SCALARS = 64
F32, BF16 = jnp.float32, jnp.bfloat16
VMEM = pl.BlockSpec(memory_space=pltpu.VMEM)
PARAMS = pltpu.CompilerParams(vmem_limit_bytes=40 * 1024 * 1024)


def one_hot(row, count):
    ids = lax.broadcasted_iota(jnp.int32, (count, row.shape[1]), 0)
    return jnp.where(ids == row, 1.0, 0.0)


def cam_index():
    return lax.axis_index("z") * 2 + lax.axis_index("core")


def pts_index():
    x = lax.axis_index("xa") * 2 + lax.axis_index("xb")
    return x * lax.axis_size("y") + lax.axis_index("y")


def short_one_hot(row, count):
    ids = lax.broadcasted_iota(jnp.int16, (count, row.shape[1]), 0)
    return jnp.where(ids == row.astype(jnp.int16), BF16(1), BF16(0))


def fold(ref, row):
    parts = [ref[row : row + 1, i * CHUNK : (i + 1) * CHUNK] for i in range(FOLDS)]
    return jnp.concatenate(parts, axis=0)


def shifted(value, step):
    ids = lax.broadcasted_iota(jnp.int32, value.shape, 1)
    rolled = pltpu.roll(value, step % CHUNK, 1)
    if step > 0:
        return jnp.where(ids < step, pltpu.roll(rolled, 1, 0), rolled)
    return jnp.where(ids >= CHUNK + step, pltpu.roll(rolled, FOLDS - 1, 0), rolled)


def part(ref, index):
    return ref[index * FOLDS : (index + 1) * FOLDS, :]


def point_totals(value, masks):
    before = value
    after = value
    index = 0
    for stage in STAGES:
        earlier, later = before, after
        for step in stage:
            before = before + part(masks, index) * shifted(earlier, step)
            after = after + part(masks, len(STEPS) + index) * shifted(later, -step)
            index += 1
    return before + (after - value)


def setup_kernel(owners, jac_pt, point_ref, damping, camera_ref, right_side, camera_damping,
                 preconditioner, keep, inverse, masks, folded, lane, slot, own):
    width = right_side.shape[1]
    own_arrays(right_side[...], camera_damping[...], preconditioner[...], keep[...], own)
    camera = fold(camera_ref, 0)
    shift = lax.rem(lax.div(camera, width) - cam_index() + owners, owners)
    block = jnp.where(shift == 1, 1, jnp.where(shift == owners - 1, 2, 3))
    block = jnp.where(shift == 0, 0, block)
    inner = lax.rem(camera, width)
    tile = lax.div(inner, LANES)
    lane[...] = lax.div(tile, 2) * LANES + lax.rem(inner, LANES)
    slot[...] = lax.rem(tile, 2) * BLOCKS + block

    point = fold(point_ref, 0)
    for i, step in enumerate(STEPS + tuple(-step for step in STEPS)):
        same = jnp.where(shifted(point, step) == point, 1.0, 0.0)
        masks[i * FOLDS : (i + 1) * FOLDS, :] = same
    rows = [fold(jac_pt, r) for r in range(6)]
    for r in range(6):
        folded[r * FOLDS : (r + 1) * FOLDS, :] = rows[r]
    pairs = [(0, 0), (0, 1), (0, 2), (1, 1), (1, 2), (2, 2)]
    xx, xy, xz, yy, yz, zz = (
        point_totals(rows[a] * rows[b] + rows[3 + a] * rows[3 + b], masks) for a, b in pairs
    )

    tiles = damping.shape[1] // LANES
    table = jnp.concatenate(
        [damping[k : k + 1, t * LANES : (t + 1) * LANES] for k in range(3) for t in range(tiles)],
        axis=0,
    )
    high = table.astype(BF16)
    rest = table - high.astype(F32)
    mid = rest.astype(BF16)
    low = (rest - mid.astype(F32)).astype(BF16)
    damp = [[], [], []]
    for i in range(FOLDS):
        spot = point[i : i + 1]
        hot = short_one_hot(lax.rem(spot, LANES), LANES)
        mask = one_hot(lax.div(spot, LANES), tiles)
        picked = sum(jnp.dot(piece, hot, preferred_element_type=F32) for piece in (high, mid, low))
        for k in range(3):
            damp[k].append(lane_sums(picked[k * tiles : (k + 1) * tiles] * mask))
    damp = [jnp.concatenate(rows_of, axis=0) for rows_of in damp]
    xx, yy, zz = xx + damp[0], yy + damp[1], zz + damp[2]
    cof_xx = yy * zz - yz * yz
    cof_xy = xz * yz - xy * zz
    cof_xz = xy * yz - xz * yy
    cof_yy = xx * zz - xz * xz
    cof_yz = xy * xz - xx * yz
    cof_zz = xx * yy - xy * xy
    det = xx * cof_xx + xy * cof_xy + xz * cof_xz
    for r, cof in enumerate((cof_xx, cof_xy, cof_xz, cof_yy, cof_yz, cof_zz)):
        inverse[r * FOLDS : (r + 1) * FOLDS, :] = cof / det


def lane_sums(value):
    return jnp.sum(value, axis=0, keepdims=True)


def schur(vector, send, jac_cam, folded, lane, slot, masks, inverse, hot, error):
    params = jac_cam.shape[0] // 2
    slots = 2 * BLOCKS
    half = hot.shape[0] // LANES
    rows = params * slots
    table = vector.reshape(params, half, slots, LANES)
    table = jnp.concatenate([table[:, h].reshape(rows, LANES) for h in range(half)], axis=1)
    high = table.astype(BF16)
    low = (table - high.astype(F32)).astype(BF16)
    table = jnp.concatenate([high, low], axis=0)

    for i in range(FOLDS):
        span = slice(i * CHUNK, (i + 1) * CHUNK)
        spot = short_one_hot(lane[i : i + 1, :], half * LANES)
        hot[:, span] = spot
        got = jnp.dot(table, spot, preferred_element_type=F32)
        got = got[:rows] + got[rows:]
        mask = one_hot(slot[i : i + 1, :], slots)
        for r in range(2):
            total = jnp.zeros((slots, CHUNK), F32)
            for a in range(params):
                jac = jac_cam[r * params + a : r * params + a + 1, span]
                total = total + jac * got[a * slots : (a + 1) * slots]
            error[r * FOLDS + i : r * FOLDS + i + 1, :] = lane_sums(total * mask)

    e0, e1 = part(error, 0), part(error, 1)
    jp = [part(folded, r) for r in range(6)]
    inv = [part(inverse, r) for r in range(6)]
    y0, y1, y2 = (point_totals(jp[k] * e0 + jp[3 + k] * e1, masks) for k in range(3))
    z = (
        inv[0] * y0 + inv[1] * y1 + inv[2] * y2,
        inv[1] * y0 + inv[3] * y1 + inv[4] * y2,
        inv[2] * y0 + inv[4] * y1 + inv[5] * y2,
    )
    left0 = e0 - (jp[0] * z[0] + jp[1] * z[1] + jp[2] * z[2])
    left1 = e1 - (jp[3] * z[0] + jp[4] * z[1] + jp[5] * z[2])
    energy = e0 * left0 + e1 * left1

    total = jnp.zeros((2 * rows, half * LANES), F32)
    for i in range(FOLDS):
        span = slice(i * CHUNK, (i + 1) * CHUNK)
        mask = one_hot(slot[i : i + 1, :], slots)
        first, second = mask * left0[i : i + 1], mask * left1[i : i + 1]
        highs, lows = [], []
        for a in range(params):
            value = jac_cam[a : a + 1, span] * first
            value = value + jac_cam[params + a : params + a + 1, span] * second
            near = value.astype(BF16)
            highs.append(near)
            lows.append((value - near.astype(F32)).astype(BF16))
        both = jnp.concatenate(highs + lows, axis=0)
        total = total + lax.dot_general(
            both, hot[:, span], (((1,), (1,)), ((), ())), preferred_element_type=F32
        )
    total = total[:rows] + total[rows:]
    for a in range(params):
        for h in range(half):
            start = (a * half + h) * slots
            send[start : start + slots, :] = total[
                a * slots : (a + 1) * slots, h * LANES : (h + 1) * LANES
            ]
    return lane_sums(sum(energy[:, t * LANES : (t + 1) * LANES] for t in range(CHUNK // LANES)))


RIGHT, DAMPING, WEIGHTS, PULL, UNWEIGH = range(5)


def own_part(own, which):
    per = own.shape[0] // 5
    return own[which * per : (which + 1) * per, :]


def own_arrays(right, damping, precond, keep, own):
    params, width = right.shape
    tiles = width // LANES
    weights = precond * keep
    parts = (right, damping, weights, weights * damping * weights * right, keep / precond)
    for t in range(tiles):
        lanes = slice(t * LANES, (t + 1) * LANES)
        for which, value in enumerate(parts):
            place = pl.ds(which * params * tiles + t, params, stride=tiles)
            own[place, :] = value[:, lanes]


def lane_ids(rows=1):
    return lax.broadcasted_iota(jnp.int32, (rows, LANES), 1)


def send_pairs(sums, scalars, send):
    ids = lane_ids()
    extra = jnp.zeros((1, LANES), F32)
    for index, row in enumerate(scalars):
        extra = jnp.where(ids == SCALARS + index, jnp.sum(row, axis=1, keepdims=True), extra)
    odd = lax.axis_index("core") == 1
    for chunk in range(16):
        q, i = chunk // 4, chunk % 4
        thirds = sums[(32 + q) * BLOCKS : (33 + q) * BLOCKS, :]
        low = pltpu.roll(thirds, (-QUARTER * i) % LANES, 1) if i else thirds
        high = pltpu.roll(thirds, (QUARTER - QUARTER * i) % LANES, 1) if i != 1 else thirds
        rows = sums[chunk * 2 * BLOCKS : (chunk + 1) * 2 * BLOCKS, :]

        def two(a, b):
            mixed = jnp.where(ids < SCALARS, high[b : b + 1], extra)
            mixed = jnp.where(ids < QUARTER, low[a : a + 1], mixed)
            pieces = [rows[at : at + 1] for at in (a, BLOCKS + a, b, BLOCKS + b)]
            return jnp.concatenate(pieces + [mixed], axis=0)

        same, other = two(0, 3), two(1, 2)
        base = 2 * chunk * PAIR
        send[base : base + PAIR, :] = jnp.where(odd, other, same)
        send[base + PAIR : base + 2 * PAIR, :] = jnp.where(odd, same, other)


def scalar(row, lane):
    return jnp.sum(jnp.where(lane_ids() == lane, row, 0.0), axis=1, keepdims=True)


def first_kernel(share, mine, after, before, across, keep, own, jac_cam, folded, lane, slot,
                 masks, inverse, send, start, sums, hot, error):
    params, tiles, _ = mine.shape
    for block, ref in enumerate((mine, after, before, across)):
        for t in range(tiles):
            place = pl.ds(t * BLOCKS + block, params, stride=tiles * BLOCKS)
            kept = keep[block : block + 1, t * LANES : (t + 1) * LANES]
            start[place, :] = ref[:, t, :] * kept
    energy = schur(start[...], sums, jac_cam, folded, lane, slot, masks, inverse, hot, error)
    vector = start[pl.ds(0, params * tiles, stride=BLOCKS), :]
    energy = energy + share * lane_sums(own_part(own, DAMPING) * vector * vector)
    gamma = share * lane_sums(own_part(own, RIGHT) * vector)
    send_pairs(sums, (energy, gamma), send)


def unpack(received, change):
    odd = lax.axis_index("core") == 1
    ids = lane_ids()
    for q in range(4):
        thirds = [jnp.zeros((1, LANES), F32)] * BLOCKS
        for i in range(4):
            chunk = 4 * q + i
            even = received[2 * chunk * PAIR : (2 * chunk + 1) * PAIR, :]
            odds = received[(2 * chunk + 1) * PAIR : (2 * chunk + 2) * PAIR, :]
            same, other = jnp.where(odd, odds, even), jnp.where(odd, even, odds)
            near = jnp.where(odd, other[2:4], other[0:2])
            far = jnp.where(odd, other[0:2], other[2:4])
            rows = []
            for r in range(2):
                rows += [same[r : r + 1], near[r : r + 1], far[r : r + 1], same[2 + r : 3 + r]]
            change[chunk * 8 : (chunk + 1) * 8, :] = jnp.concatenate(rows, axis=0)

            def moved(row, quarter):
                by = (QUARTER * (i - quarter)) % LANES
                return pltpu.roll(row, by, 1) if by else row

            first, second = moved(other[4:5], 0), moved(other[4:5], 1)
            pieces = (
                moved(same[4:5], 0),
                jnp.where(odd, second, first),
                jnp.where(odd, first, second),
                moved(same[4:5], 1),
            )
            thirds = [jnp.where(ids >= QUARTER * i, p, t) for p, t in zip(pieces, thirds)]
        at = (32 + q) * BLOCKS
        change[at : at + BLOCKS, :] = jnp.concatenate(thirds, axis=0)


def second_kernel(share, received, start, own, jac_cam, folded, lane, slot, masks, inverse,
                  send, step, change_ref, sums, hot, error):
    per = start.shape[0] // BLOCKS
    unpack(received, change_ref)
    scalars = received[PAIR - 1 : PAIR, :]
    alpha = scalar(scalars, SCALARS + 1) / scalar(scalars, SCALARS)
    step[...] = start[...] - alpha * change_ref[...]
    energy = schur(step[...], sums, jac_cam, folded, lane, slot, masks, inverse, hot, error)
    vector = step[pl.ds(0, per, stride=BLOCKS), :]
    change = change_ref[pl.ds(0, per, stride=BLOCKS), :]
    residual = own_part(own, UNWEIGH) * vector
    energy = energy + share * lane_sums(own_part(own, DAMPING) * vector * vector)
    fresh = share * lane_sums(residual * vector)
    cross = share * lane_sums(residual * change)
    send_pairs(sums, (energy, fresh, cross), send)


def own_block_kernel(received, send):
    same, other = core_sums(received)
    own, beside, across = three_blocks(same, other)
    scalars = same[PAIR - 1 : PAIR] + other[PAIR - 1 : PAIR]
    is_third = lax.broadcasted_iota(jnp.int32, (OWN, LANES), 0) == OWN - 1
    is_rest = jnp.logical_and(is_third, lane_ids(OWN) >= SCALARS)

    def with_scalars(value):
        return jnp.where(is_rest, scalars, value)

    size = lax.axis_size("z")
    columns = send.shape[0] // (size * OWN)
    nothing = with_scalars(jnp.zeros((OWN, LANES), F32))
    for spot in range(columns * size):
        send[spot * OWN : (spot + 1) * OWN, :] = nothing
    step = 1 - 2 * lax.axis_index("core")
    for shift, value in ((0, own), (step, beside), (size // 2, across)):
        place = lax.rem(lax.axis_index("z") + shift + size, size)
        value = with_scalars(value)
        for x in range(columns):
            send[pl.ds((x * size + place) * OWN, OWN), :] = value


def own_sum_kernel(received, send):
    total = received[0:OWN, :]
    for source in range(1, received.shape[0] // OWN):
        total = total + received[source * OWN : (source + 1) * OWN, :]
    for spot in range(send.shape[0] // OWN):
        send[spot * OWN : (spot + 1) * OWN, :] = total


def last_kernel(first, second, start, step, change_ref, own, solution, residual, sums):
    params, width = solution.shape
    tiles = width // LANES
    per = params * tiles
    ids = lane_ids()
    for chunk in range(16):
        sums[2 * chunk : 2 * chunk + 2, :] = second[chunk * OWN : chunk * OWN + 2, :]
    for q in range(4):
        third = jnp.zeros((1, LANES), F32)
        for i in range(4):
            at = (4 * q + i) * OWN + 2
            row = second[at : at + 1, :]
            row = pltpu.roll(row, QUARTER * i, 1) if i else row
            third = jnp.where(ids >= QUARTER * i, row, third)
        sums[32 + q : 33 + q, :] = third

    row = first[PAIR - 1 : PAIR, :]
    curve, gamma = scalar(row, SCALARS), scalar(row, SCALARS + 1)
    row = second[OWN - 1 : OWN, :]
    energy, fresh, cross = (scalar(row, SCALARS + i) for i in range(3))
    alpha = gamma / curve
    beta = fresh / gamma
    alpha_next = fresh / (energy + 2.0 * beta * cross + beta * beta * curve)
    for t in range(tiles):
        spread = pl.ds(t * BLOCKS, params, stride=tiles * BLOCKS)
        begin, vector, change = start[spread, :], step[spread, :], change_ref[spread, :]
        terms = sums[pl.ds(t, params, stride=tiles), :]
        damping, unweigh = (
            own[pl.ds(which * per + t, params, stride=tiles), :] for which in (DAMPING, UNWEIGH)
        )
        direction = vector + beta * begin
        image = jnp.where(unweigh > 0.0, damping * vector + terms, 0.0)
        image = image + beta * (unweigh * change)
        lanes = slice(t * LANES, (t + 1) * LANES)
        solution[:, lanes] = alpha * begin + alpha_next * direction
        residual[:, lanes] = unweigh * vector - alpha_next * image


def core_sums(received):
    evens = received[0:PAIR, :]
    odds = received[PAIR : 2 * PAIR, :]
    for source in range(2, received.shape[0] // PAIR, 2):
        evens = evens + received[source * PAIR : (source + 1) * PAIR, :]
        odds = odds + received[(source + 1) * PAIR : (source + 2) * PAIR, :]
    odd = lax.axis_index("core") == 1
    return jnp.where(odd, odds, evens), jnp.where(odd, evens, odds)


def three_blocks(same, other):
    odd = lax.axis_index("core") == 1

    def block(value, which):
        third = value[PAIR - 1 : PAIR]
        if which:
            third = pltpu.roll(third, LANES - QUARTER, 1)
        return jnp.concatenate([value[2 * which : 2 * which + 2], third], axis=0)

    first, second = block(other, 0), block(other, 1)
    own = block(same, 0) + jnp.where(odd, first, second)
    return own, jnp.where(odd, second, first), block(same, 1)


def own_rows(own):
    per = own.shape[0] // 5
    chunk = lax.axis_index("xb") * lax.axis_size("y") + lax.axis_index("y")
    found = []
    for which in (WEIGHTS, PULL):
        two = own[pl.ds(which * per + 2 * chunk, 2), :]
        third = own[pl.ds(which * per + 32 + lax.div(chunk, 4), 1), :]
        turned = third
        for i in range(1, 4):
            moved = pltpu.roll(third, LANES - QUARTER * i, 1)
            turned = jnp.where(lax.rem(chunk, 4) == i, moved, turned)
        found.append(jnp.concatenate([two, turned], axis=0))
    return found


def spread_kernel(received, own, send):
    same, other = core_sums(received)
    mine, beside, across = three_blocks(same, other)
    weights, pull = own_rows(own)
    scalars = same[PAIR - 1 : PAIR] + other[PAIR - 1 : PAIR]
    scalars = pltpu.roll(scalars, FIRST_SCALARS - SCALARS, 1)
    zero = jnp.zeros((OWN, LANES), F32)
    ids = lane_ids()
    size = lax.axis_size("z")
    columns = send.shape[0] // (size * TRIPLE)
    joint = pull * (1.0 / columns) + weights * mine

    def joined(*units):
        units = units + (zero,) * (3 - len(units))
        mixed = units[0][2:3]
        for u in (1, 2):
            mixed = jnp.where(ids >= QUARTER * u, pltpu.roll(units[u][2:3], QUARTER * u, 1), mixed)
        mixed = jnp.where(ids >= FIRST_SCALARS, scalars, mixed)
        return jnp.concatenate([unit[0:2] for unit in units] + [mixed], axis=0)

    nothing = joined()
    for spot in range(columns * size):
        send[spot * TRIPLE : (spot + 1) * TRIPLE, :] = nothing
    step = 1 - 2 * lax.axis_index("core")
    half = size // 2
    parts = (
        (0, joined(mine, beside, across)),
        (step, joined(beside)),
        (half, joined(across, joint, weights)),
        (-step, joined(zero, joint, weights)),
        (half - step, joined(across)),
        (half + step, joined(beside)),
    )
    for shift, value in parts:
        place = lax.rem(lax.axis_index("z") + shift + size, size)
        for x in range(columns):
            send[pl.ds((x * size + place) * TRIPLE, TRIPLE), :] = value


def combine_kernel(received, own, send):
    size = lax.axis_size("z")
    columns = received.shape[0] // (size * TRIPLE)
    step = 1 - 2 * lax.axis_index("core")
    half = size // 2
    ids = lane_ids()

    def message(shift, x):
        place = lax.rem(lax.axis_index("z") - shift + 2 * size, size)
        return received[pl.ds((x * size + place) * TRIPLE, TRIPLE), :]

    def summed(shift):
        total = message(shift, 0)
        for x in range(1, columns):
            total = total + message(shift, x)
        return total

    def unit(value, which):
        third = value[6:7]
        if which:
            third = pltpu.roll(third, LANES - QUARTER * which, 1)
        return jnp.concatenate([value[2 * which : 2 * which + 2], third], axis=0)

    here, over, back = summed(0), summed(half), summed(-step)
    weights, pull = own_rows(own)
    near_weights = unit(message(-step, 0), 2)
    far_weights = unit(message(half, 0), 2)
    changes = (
        pull + weights * (unit(here, 0) + (unit(summed(step), 0) + unit(over, 0))),
        unit(back, 1) + near_weights * (unit(here, 1) + unit(summed(half - step), 0)),
        unit(over, 1) + far_weights * (unit(summed(half + step), 0) + unit(here, 2)),
    )
    mixed = received[TRIPLE - 1 : TRIPLE, :]
    for source in range(1, received.shape[0] // TRIPLE):
        mixed = mixed + received[(source + 1) * TRIPLE - 1 : (source + 1) * TRIPLE, :]
    mixed = pltpu.roll(mixed, LANES + SCALARS - FIRST_SCALARS, 1)

    def two(first, second):
        row = jnp.where(ids < SCALARS, pltpu.roll(second[2:3], QUARTER, 1), mixed)
        row = jnp.where(ids < QUARTER, first[2:3], row)
        return jnp.concatenate([first[0:2], second[0:2], row], axis=0)

    same, other = two(changes[0], changes[2]), two(changes[0], changes[1])
    odd = lax.axis_index("core") == 1
    to_even, to_odd = jnp.where(odd, other, same), jnp.where(odd, same, other)
    for spot in range(0, send.shape[0] // PAIR, 2):
        send[spot * PAIR : (spot + 1) * PAIR, :] = to_even
        send[(spot + 1) * PAIR : (spot + 2) * PAIR, :] = to_odd


def call(kernel, outs, *args, scratch=(), name=None):
    single = not isinstance(outs, list)
    return pl.pallas_call(
        kernel,
        out_shape=outs,
        in_specs=[VMEM] * len(args),
        out_specs=VMEM if single else [VMEM] * len(outs),
        scratch_shapes=list(scratch),
        compiler_params=PARAMS,
        name=name,
    )(*args)


def swap(value, axes, tile=BLOCKS):
    size = lax.axis_size(axes)
    rows = value.shape[0] // size
    chunks = value.reshape(size, rows // tile, tile, LANES)
    return lax.all_to_all(chunks, axes, 0, 0).reshape(value.shape)


def on_device(right_side, camera_damping, preconditioner, jac_cam, jac_pt, camera_index,
              point_index, point_damping, anchors):
    params, width = right_side.shape
    pts, cam = ("xa", "xb", "y"), ("z", "core")
    near, wide, last = ("xb", "y", "core"), ("xa", "z"), ("xb", "y")
    owners, rows = lax.axis_size(cam), lax.axis_size(pts)
    per = params * width // LANES
    count = camera_index.shape[1]
    jac_cam, jac_pt = jac_cam[0], jac_pt[0]
    share = 1.0 / rows

    tiles = width // LANES
    mine = preconditioner.reshape(params, tiles, LANES) * right_side.reshape(params, tiles, LANES)
    shifts = (0, 1, -1, owners // 2)
    after, before, across = (
        lax.ppermute(mine, cam, [(i, (i - d) % owners) for i in range(owners)])
        for d in shifts[1:]
    )
    firsts = (cam_index() + jnp.array(shifts) + owners) % owners * width
    ids = firsts[:, None] + jnp.arange(width, dtype=jnp.int32)[None]
    keep = 1.0 - jnp.any(anchors[:, None, None] == ids[None], axis=0).astype(F32)
    folds = [
        jax.ShapeDtypeStruct((count_of * FOLDS, CHUNK), kind)
        for count_of, kind in ((6, F32), (2 * len(STEPS), F32), (6, F32), (1, jnp.int32), (1, jnp.int32))
    ]
    inverse, masks, folded, lane, slot, own = call(
        functools.partial(setup_kernel, owners),
        folds + [jax.ShapeDtypeStruct((5 * per, LANES), F32)],
        jac_pt, point_index, point_damping[0], camera_index, right_side, camera_damping,
        preconditioner, keep[:1], name="invert",
    )
    fixed = (jac_cam, folded, lane, slot, masks, inverse)
    half = width // (2 * LANES)
    scratch = (pltpu.VMEM((half * LANES, count), BF16), pltpu.VMEM((2 * FOLDS, CHUNK), F32))
    vector = jax.ShapeDtypeStruct((per * BLOCKS, LANES), F32)
    chunked = jax.ShapeDtypeStruct((lax.axis_size(near) * PAIR, LANES), F32)
    scratch = (pltpu.VMEM(vector.shape, F32), *scratch)

    send, start = call(
        functools.partial(first_kernel, share), [chunked, vector],
        mine, after, before, across, keep, own, *fixed, scratch=scratch, name="apply_first",
    )
    chunks = swap(send, near, 1)
    shape = jax.ShapeDtypeStruct((lax.axis_size(wide) * TRIPLE, LANES), F32)
    chunks = call(spread_kernel, shape, chunks, own, name="spread")
    chunks = swap(chunks, wide, 1)
    chunks = call(combine_kernel, chunked, chunks, own, name="combine")
    first = swap(chunks, near, 1)

    send, step, change = call(
        functools.partial(second_kernel, share), [chunked, vector, vector], first, start, own,
        *fixed, scratch=scratch, name="apply_second",
    )
    chunks = swap(send, near, 1)
    shape = jax.ShapeDtypeStruct((lax.axis_size(wide) * OWN, LANES), F32)
    chunks = call(own_block_kernel, shape, chunks, name="own_block")
    chunks = swap(chunks, wide, 1)
    shape = jax.ShapeDtypeStruct((lax.axis_size(last) * OWN, LANES), F32)
    chunks = call(own_sum_kernel, shape, chunks, name="own_sum")
    second = swap(chunks, last, 1)
    shape = jax.ShapeDtypeStruct((params, width), F32)
    return tuple(
        call(
            last_kernel, [shape, shape], first, second, start, step, change, own,
            scratch=[pltpu.VMEM((per, LANES), F32)], name="finish",
        )
    )


def solution(mesh):
    cores = 2
    high = mesh.shape["cam"] // cores
    side = int(mesh.shape["pts"] ** 0.5)
    grid = mesh.devices.reshape(side // 2, 2, mesh.shape["pts"] // side, high, cores)
    cam, whole = ("z", "core"), ("xa", "xb", "y", "z", "core")
    mesh = Mesh(grid, whole)
    return jax.shard_map(
        on_device,
        mesh=mesh,
        in_specs=(
            P(None, cam),
            P(None, cam),
            P(None, cam),
            P(whole, None, None),
            P(whole, None, None),
            P(whole, None),
            P(whole, None),
            P(whole, None, None),
            P(),
        ),
        out_specs=(P(None, cam), P(None, cam)),
        check_vma=False,
    )
```

```python
import functools

import jax
import jax.numpy as jnp
from jax import lax
from jax.experimental import pallas as pl
from jax.experimental.pallas import tpu as pltpu
from jax.sharding import Mesh, PartitionSpec as P

LANES = 128
BLOCKS = 4
STAGES = ((1, 2, 3), (4, 8, 12))
STEPS = STAGES[0] + STAGES[1]
CHUNK = 512
FOLDS = 8
QUARTER = 32
PAIR = 5
OWN = 3
TRIPLE = 7
FIRST_SCALARS = 96
SCALARS = 64
F32, BF16 = jnp.float32, jnp.bfloat16
VMEM = pl.BlockSpec(memory_space=pltpu.VMEM)
PARAMS = pltpu.CompilerParams(vmem_limit_bytes=40 * 1024 * 1024)


def one_hot(row, count):
    ids = lax.broadcasted_iota(jnp.int32, (count, row.shape[1]), 0)
    return jnp.where(ids == row, 1.0, 0.0)


def cam_index():
    return lax.axis_index("z") * 2 + lax.axis_index("core")


def short_one_hot(row, count):
    ids = lax.broadcasted_iota(jnp.int16, (count, row.shape[1]), 0)
    return jnp.where(ids == row.astype(jnp.int16), BF16(1), BF16(0))


def fold(ref, row):
    parts = [ref[row : row + 1, i * CHUNK : (i + 1) * CHUNK] for i in range(FOLDS)]
    return jnp.concatenate(parts, axis=0)


def shifted(value, step):
    ids = lax.broadcasted_iota(jnp.int32, value.shape, 1)
    rolled = pltpu.roll(value, step % CHUNK, 1)
    if step > 0:
        return jnp.where(ids < step, pltpu.roll(rolled, 1, 0), rolled)
    return jnp.where(ids >= CHUNK + step, pltpu.roll(rolled, FOLDS - 1, 0), rolled)


def part(ref, index):
    return ref[index * FOLDS : (index + 1) * FOLDS, :]


def point_totals(value, masks):
    before = value
    after = value
    index = 0
    for stage in STAGES:
        earlier, later = before, after
        for step in stage:
            before = before + part(masks, index) * shifted(earlier, step)
            after = after + part(masks, len(STEPS) + index) * shifted(later, -step)
            index += 1
    return before + (after - value)


def setup_kernel(owners, jac_pt, point_ref, damping, camera_ref, right_side, camera_damping,
                 preconditioner, keep, inverse, masks, folded, lane, slot, own):
    width = right_side.shape[1]
    own_arrays(right_side[...], camera_damping[...], preconditioner[...], keep[...], own)
    camera = fold(camera_ref, 0)
    shift = lax.rem(lax.div(camera, width) - cam_index() + owners, owners)
    block = jnp.where(shift == 1, 1, jnp.where(shift == owners - 1, 2, 3))
    block = jnp.where(shift == 0, 0, block)
    inner = lax.rem(camera, width)
    tile = lax.div(inner, LANES)
    lane[...] = lax.div(tile, 2) * LANES + lax.rem(inner, LANES)
    slot[...] = lax.rem(tile, 2) * BLOCKS + block

    point = fold(point_ref, 0)
    for i, step in enumerate(STEPS + tuple(-step for step in STEPS)):
        same = jnp.where(shifted(point, step) == point, 1.0, 0.0)
        masks[i * FOLDS : (i + 1) * FOLDS, :] = same
    rows = [fold(jac_pt, r) for r in range(6)]
    for r in range(6):
        folded[r * FOLDS : (r + 1) * FOLDS, :] = rows[r]
    pairs = [(0, 0), (0, 1), (0, 2), (1, 1), (1, 2), (2, 2)]
    xx, xy, xz, yy, yz, zz = (
        point_totals(rows[a] * rows[b] + rows[3 + a] * rows[3 + b], masks) for a, b in pairs
    )

    tiles = damping.shape[1] // LANES
    table = jnp.concatenate(
        [damping[k : k + 1, t * LANES : (t + 1) * LANES] for k in range(3) for t in range(tiles)],
        axis=0,
    )
    high = table.astype(BF16)
    rest = table - high.astype(F32)
    mid = rest.astype(BF16)
    low = (rest - mid.astype(F32)).astype(BF16)
    damp = [[], [], []]
    for i in range(FOLDS):
        spot = point[i : i + 1]
        hot = short_one_hot(lax.rem(spot, LANES), LANES)
        mask = one_hot(lax.div(spot, LANES), tiles)
        picked = sum(jnp.dot(piece, hot, preferred_element_type=F32) for piece in (high, mid, low))
        for k in range(3):
            damp[k].append(lane_sums(picked[k * tiles : (k + 1) * tiles] * mask))
    damp = [jnp.concatenate(rows_of, axis=0) for rows_of in damp]
    xx, yy, zz = xx + damp[0], yy + damp[1], zz + damp[2]
    cof_xx = yy * zz - yz * yz
    cof_xy = xz * yz - xy * zz
    cof_xz = xy * yz - xz * yy
    cof_yy = xx * zz - xz * xz
    cof_yz = xy * xz - xx * yz
    cof_zz = xx * yy - xy * xy
    det = xx * cof_xx + xy * cof_xy + xz * cof_xz
    for r, cof in enumerate((cof_xx, cof_xy, cof_xz, cof_yy, cof_yz, cof_zz)):
        inverse[r * FOLDS : (r + 1) * FOLDS, :] = cof / det


def lane_sums(value):
    return jnp.sum(value, axis=0, keepdims=True)


def schur(vector, send, jac_cam, folded, lane, slot, masks, inverse, hot, error):
    params = jac_cam.shape[0] // 2
    slots = 2 * BLOCKS
    half = hot.shape[0] // LANES
    rows = params * slots
    table = vector.reshape(params, half, slots, LANES)
    table = jnp.concatenate([table[:, h].reshape(rows, LANES) for h in range(half)], axis=1)
    high = table.astype(BF16)
    low = (table - high.astype(F32)).astype(BF16)
    table = jnp.concatenate([high, low], axis=0)

    for i in range(FOLDS):
        span = slice(i * CHUNK, (i + 1) * CHUNK)
        spot = short_one_hot(lane[i : i + 1, :], half * LANES)
        hot[:, span] = spot
        got = jnp.dot(table, spot, preferred_element_type=F32)
        got = got[:rows] + got[rows:]
        mask = one_hot(slot[i : i + 1, :], slots)
        for r in range(2):
            total = jnp.zeros((slots, CHUNK), F32)
            for a in range(params):
                jac = jac_cam[r * params + a : r * params + a + 1, span]
                total = total + jac * got[a * slots : (a + 1) * slots]
            error[r * FOLDS + i : r * FOLDS + i + 1, :] = lane_sums(total * mask)

    e0, e1 = part(error, 0), part(error, 1)
    jp = [part(folded, r) for r in range(6)]
    inv = [part(inverse, r) for r in range(6)]
    y0, y1, y2 = (point_totals(jp[k] * e0 + jp[3 + k] * e1, masks) for k in range(3))
    z = (
        inv[0] * y0 + inv[1] * y1 + inv[2] * y2,
        inv[1] * y0 + inv[3] * y1 + inv[4] * y2,
        inv[2] * y0 + inv[4] * y1 + inv[5] * y2,
    )
    left0 = e0 - (jp[0] * z[0] + jp[1] * z[1] + jp[2] * z[2])
    left1 = e1 - (jp[3] * z[0] + jp[4] * z[1] + jp[5] * z[2])
    energy = e0 * left0 + e1 * left1

    total = jnp.zeros((2 * rows, half * LANES), F32)
    for i in range(FOLDS):
        span = slice(i * CHUNK, (i + 1) * CHUNK)
        mask = one_hot(slot[i : i + 1, :], slots)
        first, second = mask * left0[i : i + 1], mask * left1[i : i + 1]
        highs, lows = [], []
        for a in range(params):
            value = jac_cam[a : a + 1, span] * first
            value = value + jac_cam[params + a : params + a + 1, span] * second
            near = value.astype(BF16)
            highs.append(near)
            lows.append((value - near.astype(F32)).astype(BF16))
        both = jnp.concatenate(highs + lows, axis=0)
        total = total + lax.dot_general(
            both, hot[:, span], (((1,), (1,)), ((), ())), preferred_element_type=F32
        )
    total = total[:rows] + total[rows:]
    for a in range(params):
        for h in range(half):
            start = (a * half + h) * slots
            send[start : start + slots, :] = total[
                a * slots : (a + 1) * slots, h * LANES : (h + 1) * LANES
            ]
    return lane_sums(sum(energy[:, t * LANES : (t + 1) * LANES] for t in range(CHUNK // LANES)))


RIGHT, DAMPING, WEIGHTS, PULL, UNWEIGH = range(5)


def own_part(own, which):
    per = own.shape[0] // 5
    return own[which * per : (which + 1) * per, :]


def own_arrays(right, damping, precond, keep, own):
    params, width = right.shape
    tiles = width // LANES
    weights = precond * keep
    parts = (right, damping, weights, weights * damping * weights * right, keep / precond)
    for t in range(tiles):
        lanes = slice(t * LANES, (t + 1) * LANES)
        for which, value in enumerate(parts):
            place = pl.ds(which * params * tiles + t, params, stride=tiles)
            own[place, :] = value[:, lanes]


def lane_ids(rows=1):
    return lax.broadcasted_iota(jnp.int32, (rows, LANES), 1)


def send_pairs(sums, scalars, send):
    ids = lane_ids()
    extra = jnp.zeros((1, LANES), F32)
    for index, row in enumerate(scalars):
        extra = jnp.where(ids == SCALARS + index, jnp.sum(row, axis=1, keepdims=True), extra)
    odd = lax.axis_index("core") == 1
    for chunk in range(16):
        q, i = chunk // 4, chunk % 4
        thirds = sums[(32 + q) * BLOCKS : (33 + q) * BLOCKS, :]
        low = pltpu.roll(thirds, (-QUARTER * i) % LANES, 1) if i else thirds
        high = pltpu.roll(thirds, (QUARTER - QUARTER * i) % LANES, 1) if i != 1 else thirds
        rows = sums[chunk * 2 * BLOCKS : (chunk + 1) * 2 * BLOCKS, :]

        def two(a, b):
            mixed = jnp.where(ids < SCALARS, high[b : b + 1], extra)
            mixed = jnp.where(ids < QUARTER, low[a : a + 1], mixed)
            pieces = [rows[at : at + 1] for at in (a, BLOCKS + a, b, BLOCKS + b)]
            return jnp.concatenate(pieces + [mixed], axis=0)

        same, other = two(0, 3), two(1, 2)
        base = 2 * chunk * PAIR
        send[base : base + PAIR, :] = jnp.where(odd, other, same)
        send[base + PAIR : base + 2 * PAIR, :] = jnp.where(odd, same, other)


def scalar(row, lane):
    return jnp.sum(jnp.where(lane_ids() == lane, row, 0.0), axis=1, keepdims=True)


def first_kernel(share, mine, after, before, across, keep, own, jac_cam, folded, lane, slot,
                 masks, inverse, send, start, sums, hot, error):
    params, tiles, _ = mine.shape
    for block, ref in enumerate((mine, after, before, across)):
        for t in range(tiles):
            place = pl.ds(t * BLOCKS + block, params, stride=tiles * BLOCKS)
            kept = keep[block : block + 1, t * LANES : (t + 1) * LANES]
            start[place, :] = ref[:, t, :] * kept
    energy = schur(start[...], sums, jac_cam, folded, lane, slot, masks, inverse, hot, error)
    vector = start[pl.ds(0, params * tiles, stride=BLOCKS), :]
    energy = energy + share * lane_sums(own_part(own, DAMPING) * vector * vector)
    gamma = share * lane_sums(own_part(own, RIGHT) * vector)
    send_pairs(sums, (energy, gamma), send)


def unpack(received, change):
    odd = lax.axis_index("core") == 1
    ids = lane_ids()
    for q in range(4):
        thirds = [jnp.zeros((1, LANES), F32)] * BLOCKS
        for i in range(4):
            chunk = 4 * q + i
            even = received[2 * chunk * PAIR : (2 * chunk + 1) * PAIR, :]
            odds = received[(2 * chunk + 1) * PAIR : (2 * chunk + 2) * PAIR, :]
            same, other = jnp.where(odd, odds, even), jnp.where(odd, even, odds)
            near = jnp.where(odd, other[2:4], other[0:2])
            far = jnp.where(odd, other[0:2], other[2:4])
            rows = []
            for r in range(2):
                rows += [same[r : r + 1], near[r : r + 1], far[r : r + 1], same[2 + r : 3 + r]]
            change[chunk * 8 : (chunk + 1) * 8, :] = jnp.concatenate(rows, axis=0)

            def moved(row, quarter):
                by = (QUARTER * (i - quarter)) % LANES
                return pltpu.roll(row, by, 1) if by else row

            first, second = moved(other[4:5], 0), moved(other[4:5], 1)
            pieces = (
                moved(same[4:5], 0),
                jnp.where(odd, second, first),
                jnp.where(odd, first, second),
                moved(same[4:5], 1),
            )
            thirds = [jnp.where(ids >= QUARTER * i, p, t) for p, t in zip(pieces, thirds)]
        at = (32 + q) * BLOCKS
        change[at : at + BLOCKS, :] = jnp.concatenate(thirds, axis=0)


def second_kernel(share, received, start, own, jac_cam, folded, lane, slot, masks, inverse,
                  send, step, change_ref, sums, hot, error):
    per = start.shape[0] // BLOCKS
    unpack(received, change_ref)
    scalars = received[PAIR - 1 : PAIR, :]
    alpha = scalar(scalars, SCALARS + 1) / scalar(scalars, SCALARS)
    step[...] = start[...] - alpha * change_ref[...]
    energy = schur(step[...], sums, jac_cam, folded, lane, slot, masks, inverse, hot, error)
    vector = step[pl.ds(0, per, stride=BLOCKS), :]
    change = change_ref[pl.ds(0, per, stride=BLOCKS), :]
    residual = own_part(own, UNWEIGH) * vector
    energy = energy + share * lane_sums(own_part(own, DAMPING) * vector * vector)
    fresh = share * lane_sums(residual * vector)
    cross = share * lane_sums(residual * change)
    send_pairs(sums, (energy, fresh, cross), send)


def own_block_kernel(received, send):
    same, other = core_sums(received)
    own, beside, across = three_blocks(same, other)
    scalars = same[PAIR - 1 : PAIR] + other[PAIR - 1 : PAIR]
    is_third = lax.broadcasted_iota(jnp.int32, (OWN, LANES), 0) == OWN - 1
    is_rest = jnp.logical_and(is_third, lane_ids(OWN) >= SCALARS)

    def with_scalars(value):
        return jnp.where(is_rest, scalars, value)

    size = lax.axis_size("z")
    columns = send.shape[0] // (size * OWN)
    nothing = with_scalars(jnp.zeros((OWN, LANES), F32))
    for spot in range(columns * size):
        send[spot * OWN : (spot + 1) * OWN, :] = nothing
    step = 1 - 2 * lax.axis_index("core")
    for shift, value in ((0, own), (step, beside), (size // 2, across)):
        place = lax.rem(lax.axis_index("z") + shift + size, size)
        value = with_scalars(value)
        for x in range(columns):
            send[pl.ds((x * size + place) * OWN, OWN), :] = value


def own_sum_kernel(received, send):
    total = received[0:OWN, :]
    for source in range(1, received.shape[0] // OWN):
        total = total + received[source * OWN : (source + 1) * OWN, :]
    for spot in range(send.shape[0] // OWN):
        send[spot * OWN : (spot + 1) * OWN, :] = total


def last_kernel(first, second, start, step, change_ref, own, solution, residual, sums):
    params, width = solution.shape
    tiles = width // LANES
    per = params * tiles
    ids = lane_ids()
    for chunk in range(16):
        sums[2 * chunk : 2 * chunk + 2, :] = second[chunk * OWN : chunk * OWN + 2, :]
    for q in range(4):
        third = jnp.zeros((1, LANES), F32)
        for i in range(4):
            at = (4 * q + i) * OWN + 2
            row = second[at : at + 1, :]
            row = pltpu.roll(row, QUARTER * i, 1) if i else row
            third = jnp.where(ids >= QUARTER * i, row, third)
        sums[32 + q : 33 + q, :] = third

    row = first[PAIR - 1 : PAIR, :]
    curve, gamma = scalar(row, SCALARS), scalar(row, SCALARS + 1)
    row = second[OWN - 1 : OWN, :]
    energy, fresh, cross = (scalar(row, SCALARS + i) for i in range(3))
    alpha = gamma / curve
    beta = fresh / gamma
    alpha_next = fresh / (energy + 2.0 * beta * cross + beta * beta * curve)
    for t in range(tiles):
        spread = pl.ds(t * BLOCKS, params, stride=tiles * BLOCKS)
        begin, vector, change = start[spread, :], step[spread, :], change_ref[spread, :]
        terms = sums[pl.ds(t, params, stride=tiles), :]
        damping, unweigh = (
            own[pl.ds(which * per + t, params, stride=tiles), :] for which in (DAMPING, UNWEIGH)
        )
        direction = vector + beta * begin
        image = jnp.where(unweigh > 0.0, damping * vector + terms, 0.0)
        image = image + beta * (unweigh * change)
        lanes = slice(t * LANES, (t + 1) * LANES)
        solution[:, lanes] = alpha * begin + alpha_next * direction
        residual[:, lanes] = unweigh * vector - alpha_next * image


def core_sums(received):
    evens = received[0:PAIR, :]
    odds = received[PAIR : 2 * PAIR, :]
    for source in range(2, received.shape[0] // PAIR, 2):
        evens = evens + received[source * PAIR : (source + 1) * PAIR, :]
        odds = odds + received[(source + 1) * PAIR : (source + 2) * PAIR, :]
    odd = lax.axis_index("core") == 1
    return jnp.where(odd, odds, evens), jnp.where(odd, evens, odds)


def three_blocks(same, other):
    odd = lax.axis_index("core") == 1

    def block(value, which):
        third = value[PAIR - 1 : PAIR]
        if which:
            third = pltpu.roll(third, LANES - QUARTER, 1)
        return jnp.concatenate([value[2 * which : 2 * which + 2], third], axis=0)

    first, second = block(other, 0), block(other, 1)
    own = block(same, 0) + jnp.where(odd, first, second)
    return own, jnp.where(odd, second, first), block(same, 1)


def own_rows(own):
    per = own.shape[0] // 5
    chunk = lax.axis_index("x") * lax.axis_size("yb") + lax.axis_index("yb")
    found = []
    for which in (WEIGHTS, PULL):
        two = own[pl.ds(which * per + 2 * chunk, 2), :]
        third = own[pl.ds(which * per + 32 + lax.div(chunk, 4), 1), :]
        turned = third
        for i in range(1, 4):
            moved = pltpu.roll(third, LANES - QUARTER * i, 1)
            turned = jnp.where(lax.rem(chunk, 4) == i, moved, turned)
        found.append(jnp.concatenate([two, turned], axis=0))
    return found


def spread_kernel(received, own, send):
    same, other = core_sums(received)
    mine, beside, across = three_blocks(same, other)
    weights, pull = own_rows(own)
    scalars = same[PAIR - 1 : PAIR] + other[PAIR - 1 : PAIR]
    scalars = pltpu.roll(scalars, FIRST_SCALARS - SCALARS, 1)
    zero = jnp.zeros((OWN, LANES), F32)
    ids = lane_ids()
    size = lax.axis_size("z")
    columns = send.shape[0] // (size * TRIPLE)
    joint = pull * (1.0 / columns) + weights * mine

    def joined(*units):
        units = units + (zero,) * (3 - len(units))
        mixed = units[0][2:3]
        for u in (1, 2):
            mixed = jnp.where(ids >= QUARTER * u, pltpu.roll(units[u][2:3], QUARTER * u, 1), mixed)
        mixed = jnp.where(ids >= FIRST_SCALARS, scalars, mixed)
        return jnp.concatenate([unit[0:2] for unit in units] + [mixed], axis=0)

    nothing = joined()
    for spot in range(columns * size):
        send[spot * TRIPLE : (spot + 1) * TRIPLE, :] = nothing
    step = 1 - 2 * lax.axis_index("core")
    half = size // 2
    parts = (
        (0, joined(mine, beside, across)),
        (step, joined(beside)),
        (half, joined(across, joint, weights)),
        (-step, joined(zero, joint, weights)),
        (half - step, joined(across)),
        (half + step, joined(beside)),
    )
    for shift, value in parts:
        place = lax.rem(lax.axis_index("z") + shift + size, size)
        for x in range(columns):
            send[pl.ds((x * size + place) * TRIPLE, TRIPLE), :] = value


def combine_kernel(received, own, send):
    size = lax.axis_size("z")
    columns = received.shape[0] // (size * TRIPLE)
    step = 1 - 2 * lax.axis_index("core")
    half = size // 2
    ids = lane_ids()

    def message(shift, x):
        place = lax.rem(lax.axis_index("z") - shift + 2 * size, size)
        return received[pl.ds((x * size + place) * TRIPLE, TRIPLE), :]

    def summed(shift):
        total = message(shift, 0)
        for x in range(1, columns):
            total = total + message(shift, x)
        return total

    def unit(value, which):
        third = value[6:7]
        if which:
            third = pltpu.roll(third, LANES - QUARTER * which, 1)
        return jnp.concatenate([value[2 * which : 2 * which + 2], third], axis=0)

    here, over, back = summed(0), summed(half), summed(-step)
    weights, pull = own_rows(own)
    near_weights = unit(message(-step, 0), 2)
    far_weights = unit(message(half, 0), 2)
    changes = (
        pull + weights * (unit(here, 0) + (unit(summed(step), 0) + unit(over, 0))),
        unit(back, 1) + near_weights * (unit(here, 1) + unit(summed(half - step), 0)),
        unit(over, 1) + far_weights * (unit(summed(half + step), 0) + unit(here, 2)),
    )
    mixed = received[TRIPLE - 1 : TRIPLE, :]
    for source in range(1, received.shape[0] // TRIPLE):
        mixed = mixed + received[(source + 1) * TRIPLE - 1 : (source + 1) * TRIPLE, :]
    mixed = pltpu.roll(mixed, LANES + SCALARS - FIRST_SCALARS, 1)

    def two(first, second):
        row = jnp.where(ids < SCALARS, pltpu.roll(second[2:3], QUARTER, 1), mixed)
        row = jnp.where(ids < QUARTER, first[2:3], row)
        return jnp.concatenate([first[0:2], second[0:2], row], axis=0)

    same, other = two(changes[0], changes[2]), two(changes[0], changes[1])
    odd = lax.axis_index("core") == 1
    to_even, to_odd = jnp.where(odd, other, same), jnp.where(odd, same, other)
    for spot in range(0, send.shape[0] // PAIR, 2):
        send[spot * PAIR : (spot + 1) * PAIR, :] = to_even
        send[(spot + 1) * PAIR : (spot + 2) * PAIR, :] = to_odd


def call(kernel, outs, *args, scratch=(), name=None):
    single = not isinstance(outs, list)
    return pl.pallas_call(
        kernel,
        out_shape=outs,
        in_specs=[VMEM] * len(args),
        out_specs=VMEM if single else [VMEM] * len(outs),
        scratch_shapes=list(scratch),
        compiler_params=PARAMS,
        name=name,
    )(*args)


def swap(value, axes, tile=BLOCKS):
    size = lax.axis_size(axes)
    rows = value.shape[0] // size
    chunks = value.reshape(size, rows // tile, tile, LANES)
    return lax.all_to_all(chunks, axes, 0, 0).reshape(value.shape)


def on_device(right_side, camera_damping, preconditioner, jac_cam, jac_pt, camera_index,
              point_index, point_damping, anchors):
    params, width = right_side.shape
    pts, cam = ("x", "ya", "yb"), ("z", "core")
    near, wide, last = ("x", "yb", "core"), ("ya", "z"), ("x", "yb")
    owners, rows = lax.axis_size(cam), lax.axis_size(pts)
    per = params * width // LANES
    count = camera_index.shape[1]
    jac_cam, jac_pt = jac_cam[0], jac_pt[0]
    share = 1.0 / rows

    tiles = width // LANES
    mine = preconditioner.reshape(params, tiles, LANES) * right_side.reshape(params, tiles, LANES)
    shifts = (0, 1, -1, owners // 2)
    after, before, across = (
        lax.ppermute(mine, cam, [(i, (i - d) % owners) for i in range(owners)])
        for d in shifts[1:]
    )
    firsts = (cam_index() + jnp.array(shifts) + owners) % owners * width
    ids = firsts[:, None] + jnp.arange(width, dtype=jnp.int32)[None]
    keep = 1.0 - jnp.any(anchors[:, None, None] == ids[None], axis=0).astype(F32)
    folds = [
        jax.ShapeDtypeStruct((count_of * FOLDS, CHUNK), kind)
        for count_of, kind in ((6, F32), (2 * len(STEPS), F32), (6, F32), (1, jnp.int32), (1, jnp.int32))
    ]
    inverse, masks, folded, lane, slot, own = call(
        functools.partial(setup_kernel, owners),
        folds + [jax.ShapeDtypeStruct((5 * per, LANES), F32)],
        jac_pt, point_index, point_damping[0], camera_index, right_side, camera_damping,
        preconditioner, keep[:1], name="invert",
    )
    fixed = (jac_cam, folded, lane, slot, masks, inverse)
    half = width // (2 * LANES)
    scratch = (pltpu.VMEM((half * LANES, count), BF16), pltpu.VMEM((2 * FOLDS, CHUNK), F32))
    vector = jax.ShapeDtypeStruct((per * BLOCKS, LANES), F32)
    chunked = jax.ShapeDtypeStruct((lax.axis_size(near) * PAIR, LANES), F32)
    scratch = (pltpu.VMEM(vector.shape, F32), *scratch)

    send, start = call(
        functools.partial(first_kernel, share), [chunked, vector],
        mine, after, before, across, keep, own, *fixed, scratch=scratch, name="apply_first",
    )
    chunks = swap(send, near, 1)
    shape = jax.ShapeDtypeStruct((lax.axis_size(wide) * TRIPLE, LANES), F32)
    chunks = call(spread_kernel, shape, chunks, own, name="spread")
    chunks = swap(chunks, wide, 1)
    chunks = call(combine_kernel, chunked, chunks, own, name="combine")
    first = swap(chunks, near, 1)

    send, step, change = call(
        functools.partial(second_kernel, share), [chunked, vector, vector], first, start, own,
        *fixed, scratch=scratch, name="apply_second",
    )
    chunks = swap(send, near, 1)
    shape = jax.ShapeDtypeStruct((lax.axis_size(wide) * OWN, LANES), F32)
    chunks = call(own_block_kernel, shape, chunks, name="own_block")
    chunks = swap(chunks, wide, 1)
    shape = jax.ShapeDtypeStruct((lax.axis_size(last) * OWN, LANES), F32)
    chunks = call(own_sum_kernel, shape, chunks, name="own_sum")
    second = swap(chunks, last, 1)
    shape = jax.ShapeDtypeStruct((params, width), F32)
    return tuple(
        call(
            last_kernel, [shape, shape], first, second, start, step, change, own,
            scratch=[pltpu.VMEM((per, LANES), F32)], name="finish",
        )
    )


def solution(mesh):
    cores = 2
    high = mesh.shape["cam"] // cores
    side = int(mesh.shape["pts"] ** 0.5)
    grid = mesh.devices.reshape(side, mesh.shape["pts"] // side // 2, 2, high, cores)
    cam, whole = ("z", "core"), ("x", "ya", "yb", "z", "core")
    mesh = Mesh(grid, whole)
    return jax.shard_map(
        on_device,
        mesh=mesh,
        in_specs=(
            P(None, cam),
            P(None, cam),
            P(None, cam),
            P(whole, None, None),
            P(whole, None, None),
            P(whole, None),
            P(whole, None),
            P(whole, None, None),
            P(),
        ),
        out_specs=(P(None, cam), P(None, cam)),
        check_vma=False,
    )
```
